32 devices in a mesh: fsdp: 4 (over z), heads: 4 (over y, x), tensor: 2 (over core).
Axes of the slice: x: 2, y: 2, z: 4, core: 2. Of those that a mesh axis runs over, the one named last changes fastest.
Arguments:
- tokens: bfloat16 [4096, 2048], P('fsdp'), may hold values from -6 to 6
- segments: int32 [4, 1024], P('fsdp'), may hold values from 0 to 7, never falling along the last dimension, each value on 1 to 512 neighbouring positions
- ln1_gain: bfloat16 [2048], P('fsdp'), may hold values from 0.25 to 1.75
- w_query: bfloat16 [2048, 2048], P('fsdp', ('heads', 'tensor')), may hold values from -0.125 to 0.125
- w_key: bfloat16 [2048, 1024], P('fsdp', ('heads', 'tensor')), may hold values from -0.125 to 0.125
- w_value: bfloat16 [2048, 1024], P('fsdp', ('heads', 'tensor')), may hold values from -0.125 to 0.125
- query_gain: bfloat16 [128], P('fsdp'), may hold values from 0.25 to 1.75
- key_gain: bfloat16 [128], P('fsdp'), may hold values from 0.25 to 1.75
- w_out: bfloat16 [2048, 2048], P('fsdp', ('heads', 'tensor')), may hold values from -1 to 1
- ln2_gain: bfloat16 [2048], P('fsdp'), may hold values from 0.25 to 1.75
- w_gate: bfloat16 [2048, 6144], P('fsdp', ('heads', 'tensor')), may hold values from -0.125 to 0.125
- w_up: bfloat16 [2048, 6144], P('fsdp', ('heads', 'tensor')), may hold values from -0.125 to 0.125
- w_down: bfloat16 [2048, 6144], P('fsdp', ('heads', 'tensor')), may hold values from -0.078125 to 0.078125
- cotangent: bfloat16 [4096, 2048], P('fsdp'), may hold values from -6 to 6
Outputs:
- block_out: bfloat16 [4096, 2048], P(('fsdp', 'heads', 'tensor'))
- tokens_grad: bfloat16 [4096, 2048], P(('fsdp', 'heads', 'tensor'))
- ln1_grad: float32 [2048], P('fsdp')
- query_w_grad: float32 [2048, 2048], P('fsdp', ('heads', 'tensor'))
- key_w_grad: float32 [2048, 1024], P('fsdp', ('heads', 'tensor'))
- value_w_grad: float32 [2048, 1024], P('fsdp', ('heads', 'tensor'))
- query_gain_grad: float32 [128], P('fsdp')
- key_gain_grad: float32 [128], P('fsdp')
- out_w_grad: float32 [2048, 2048], P('fsdp', ('heads', 'tensor'))
- ln2_grad: float32 [2048], P('fsdp')
- gate_w_grad: float32 [2048, 6144], P('fsdp', ('heads', 'tensor'))
- up_w_grad: float32 [2048, 6144], P('fsdp', ('heads', 'tensor'))
- down_w_grad: float32 [2048, 6144], P('fsdp', ('heads', 'tensor'))
The draws below stay inside these ranges and needn't reach their ends.
Inputs may be any that keep to these rules, and one draw needn't show every extreme that they name: `segments`: in each sequence the segment numbers never fall, and some segment holds exactly 512 tokens.
All inputs are finite; a program needn't handle non-finite values.
Results may differ from the reference program's by a relative error of at most 0.02.
Values may be sent and summed in bfloat16 or wider, within the bound.
No kernel may reach another device: no remote copies, remote signals or barrier semaphores. Data moves between devices by JAX's collectives and lax.ppermute only.
A program may use at most 256 MiB of HBM per device.

```python
import math
import jax
import jax.numpy as jnp
import numpy as np
from jax import lax

D = 2048
HEADS = 16
KV = 8
HD = 128
FF = 6144
LEN = 1024
SEQS = 4
TOKENS = 4096


def level_of(stream_key, dims, cuts, least, largest):
    loudness, own = 1.0, jax.random.fold_in(stream_key, 6)
    for dim, shards_of in cuts:
        draws = jnp.exp(jax.random.uniform(jax.random.fold_in(own, dim), (shards_of,), jnp.float32, least / len(cuts), largest / len(cuts)))
        loudness = loudness * jnp.repeat(draws, dims[dim] // shards_of).reshape([-1 if axis == dim else 1 for axis in range(len(dims))])
    return loudness


def length_profile(amount, total, limit, skew):
    portions = [(1 << 20) // math.isqrt(grade ** skew) + 1 for grade in range(2, amount + 1)]
    surplus, given = total - limit - (amount - 1), [1] * (amount - 1)
    while surplus > 0:
        free = [i for i in range(amount - 1) if given[i] < limit]
        mass, remaining = sum([portions[i] for i in free]), surplus
        for i in free:
            more = min(limit - given[i], max(1, remaining * portions[i] // mass), surplus)
            given[i] = given[i] + more
            surplus = surplus - more
    return np.array([limit] + given)


def uneven(own_key, amount, total, most, lean):
    if amount == 2:
        one = jax.random.randint(own_key, (), max(1, total - most), min(most, total - 1) + 1)
        return jnp.stack([one, total - one])
    sizes = jnp.asarray(length_profile(amount, total, most, lean), jnp.int32)
    couples = (amount - 1) // 2
    donor, sink = sizes[1:1 + 2 * couples:2], sizes[2:2 + 2 * couples:2]
    room = jnp.minimum(donor - 1, most - sink)
    passed = jax.random.randint(jax.random.fold_in(own_key, 1), (couples,), 0, 1 << 20) % (room + 1)
    sizes = sizes.at[1:1 + 2 * couples:2].set(donor - passed).at[2:2 + 2 * couples:2].set(sink + passed)
    return sizes[jax.random.permutation(jax.random.fold_in(own_key, 2), amount)]


def noise(key, extent, spread, reach, pieces=(), kind=jnp.bfloat16):
    result = spread * jax.random.normal(key, extent, jnp.float32)
    if pieces:
        result = result * level_of(key, extent, pieces, -0.22, 0.18)
    return jnp.clip(result, -reach, reach).astype(kind)


def setup_inputs(seed: int = 0) -> dict:
    seeds = jax.random.split(jax.random.key(seed), 15)
    tokens = noise(seeds[0], (TOKENS, D), 1.0, 6.0, ((0, 4),))
    segments = jax.vmap(lambda own: jnp.searchsorted(jnp.cumsum(uneven(own, 8, LEN, LEN // 2, 0)), jnp.arange(LEN), side="right"))(jax.random.split(seeds[1], SEQS)).reshape((SEQS, LEN)).astype(jnp.int32)
    ln1_gain = jnp.clip(1.0 + 0.15 * jax.random.normal(seeds[2], (D,), jnp.float32), 0.25, 1.75).astype(jnp.bfloat16)
    w_query = noise(seeds[3], (D, HEADS * HD), D ** -0.5, 0.125, ((0, 4), (1, 8)))
    w_key = noise(seeds[4], (D, KV * HD), D ** -0.5, 0.125, ((0, 4), (1, 8)))
    w_value = noise(seeds[5], (D, KV * HD), D ** -0.5, 0.125, ((0, 4), (1, 8)))
    query_gain = jnp.clip(1.0 + 0.15 * jax.random.normal(seeds[6], (HD,), jnp.float32), 0.25, 1.75).astype(jnp.bfloat16)
    key_gain = jnp.clip(1.0 + 0.15 * jax.random.normal(seeds[7], (HD,), jnp.float32), 0.25, 1.75).astype(jnp.bfloat16)
    w_out = noise(seeds[8], (D, HEADS * HD), (HEADS * HD // 64) ** -0.5, 1.0, ((0, 4), (1, 8)))
    ln2_gain = jnp.clip(1.0 + 0.15 * jax.random.normal(seeds[9], (D,), jnp.float32), 0.25, 1.75).astype(jnp.bfloat16)
    w_gate = noise(seeds[10], (D, FF), D ** -0.5, 0.125, ((0, 4), (1, 8)))
    w_up = noise(seeds[11], (D, FF), D ** -0.5, 0.125, ((0, 4), (1, 8)))
    w_down = noise(seeds[12], (D, FF), FF ** -0.5, 0.078125, ((0, 4), (1, 8)))
    cotangent = noise(seeds[13], (TOKENS, D), 1.0, 6.0, ((0, 4),))
    return dict(tokens=tokens, segments=segments, ln1_gain=ln1_gain, w_query=w_query, w_key=w_key, w_value=w_value, query_gain=query_gain, key_gain=key_gain, w_out=w_out, ln2_gain=ln2_gain, w_gate=w_gate, w_up=w_up, w_down=w_down, cotangent=cotangent)


EPSILON = 1e-06
THETA = 1000000.0

@jax.custom_vjp
def low(v):
    return lax.optimization_barrier(v.astype(jnp.bfloat16)).astype(jnp.float32)

@jax.custom_vjp
def low_back(v):
    return v

def low_keep(v):
    return (low(v), None)

def low_pass(kept, grad):
    return (grad,)

def back_keep(v):
    return (v, None)

def back_low(kept, grad):
    return (low(grad),)
low.defvjp(low_keep, low_pass)
low_back.defvjp(back_keep, back_low)

def rms_scale(values, gain):
    return values * lax.rsqrt(lax.optimization_barrier(jnp.mean(values * values, axis=-1, keepdims=True)) + EPSILON) * gain

def highest(left, right):
    return jnp.dot(left, right, precision=lax.Precision.HIGHEST)

def doc_positions(segment_row):
    places = jnp.arange(segment_row.shape[0], dtype=jnp.int32)
    previous = jnp.concatenate([segment_row[:1], segment_row[:-1]])
    starts = lax.cummax(jnp.where(segment_row != previous, places, 0), axis=0)
    return places - starts

def rope_tables(positions):
    frequency = THETA ** (-(jnp.arange(HD // 2, dtype=jnp.float32) * 2.0 / HD))
    angles = positions.astype(jnp.float32)[:, None] * frequency[None, :]
    return (jnp.cos(angles), jnp.sin(angles))

def rotate(values, cosine, sine):
    middle = values.shape[-1] // 2
    front_half = values[..., :middle]
    back_half = values[..., middle:]
    cosine = cosine[:, None, :]
    sine = sine[:, None, :]
    return jnp.concatenate([front_half * cosine - back_half * sine, back_half * cosine + front_half * sine], axis=-1)

def attend_one(packed):
    query, keys, values, segment_row = packed
    group = HEADS // KV
    keys = jnp.repeat(keys, group, axis=1)
    values = jnp.repeat(values, group, axis=1)
    scores = low_back(jnp.einsum('qhd,khd->hqk', query, keys, precision=lax.Precision.HIGHEST)) * HD ** (-0.5)
    places = jnp.arange(LEN, dtype=jnp.int32)
    allowed = (places[:, None] >= places[None, :]) & (segment_row[:, None] == segment_row[None, :])
    scores = jnp.where(allowed[None], scores, -1e+30)
    weights = low(jax.nn.softmax(scores, axis=-1))
    return jnp.einsum('hqk,khd->qhd', weights, values, precision=lax.Precision.HIGHEST)

def reference(tokens, segments, ln1_gain, w_query, w_key, w_value, query_gain, key_gain, w_out, ln2_gain, w_gate, w_up, w_down, cotangent):
    positions = jax.vmap(doc_positions)(segments).reshape(-1)
    cosine, sine = rope_tables(positions)

    def layer(block_in, params):
        gain_attn, query_proj, key_proj, value_proj, query_norm, key_norm, output_proj, gain_ffn, gate_proj, up_proj, down_proj = params
        normed = low(rms_scale(block_in, gain_attn))
        query = low_back(highest(normed, query_proj)).reshape(TOKENS, HEADS, HD)
        keys = low_back(highest(normed, key_proj)).reshape(TOKENS, KV, HD)
        values = low_back(low(highest(normed, value_proj))).reshape(TOKENS, KV, HD)
        query = low(rotate(rms_scale(query, query_norm), cosine, sine))
        keys = low(rotate(rms_scale(keys, key_norm), cosine, sine))
        mixed = lax.map(jax.checkpoint(attend_one), (query.reshape(SEQS, LEN, HEADS, HD), keys.reshape(SEQS, LEN, KV, HD), values.reshape(SEQS, LEN, KV, HD), segments))
        mixed = low_back(low(mixed.reshape(TOKENS, HEADS * HD)))
        hidden_one = block_in + low_back(highest(mixed, output_proj.T))
        normed_two = low(rms_scale(hidden_one, gain_ffn))
        gate_value = low_back(highest(normed_two, gate_proj))
        up_value = low_back(highest(normed_two, up_proj))
        activated = low(jax.nn.silu(gate_value) * up_value)
        return hidden_one + low_back(highest(activated, down_proj.T))
    params = tuple((weight.astype(jnp.float32) for weight in (ln1_gain, w_query, w_key, w_value, query_gain, key_gain, w_out, ln2_gain, w_gate, w_up, w_down)))
    block_out, pullback = jax.vjp(layer, tokens.astype(jnp.float32), params)
    tokens_grad, grads = pullback(cotangent.astype(jnp.float32))
    return (block_out.astype(jnp.bfloat16), tokens_grad.astype(jnp.bfloat16), grads[0], grads[1], grads[2], grads[3], grads[4], grads[5], grads[6], grads[7], grads[8], grads[9], grads[10])
```

```python
import functools

import jax
import jax.numpy as jnp
from jax import lax
from jax.experimental import pallas as pl
from jax.experimental.pallas import tpu as pltpu
from jax.sharding import PartitionSpec as P

HD = 128


EPSILON = 1e-06
THETA = 1000000.0
ROWS = 256
BAND = 512
PLANE = ("heads", "tensor")
SWAP = ((0, 1), (1, 0))
NEAR = ((0, 1), (1, 0), (2, 3), (3, 2))
FAR = ((0, 2), (2, 0), (1, 3), (3, 1))


def rms_parts(values):
    return lax.rsqrt(jnp.mean(values * values, axis=-1, keepdims=True) + EPSILON)


def norm_back(values, scale, upstream):
    return scale * upstream - values * scale**3 * jnp.mean(
        values * upstream, axis=-1, keepdims=True
    )


def contract(left, right, left_dim, right_dim):
    return lax.dot_general(
        left, right, (((left_dim,), (right_dim,)), ((), ())), preferred_element_type=jnp.float32
    )


def doc_positions(segment_row):
    places = jnp.arange(segment_row.shape[0], dtype=jnp.int32)
    previous = jnp.concatenate([segment_row[:1], segment_row[:-1]])
    starts = lax.cummax(jnp.where(segment_row != previous, places, 0), axis=0)
    return places - starts


def rope_tables(positions):
    frequency = THETA ** (-(jnp.arange(HD // 2, dtype=jnp.float32) * 2.0 / HD))
    angles = positions.astype(jnp.float32)[:, None] * frequency[None, :]
    cosine, sine = jnp.cos(angles), jnp.sin(angles)
    return (
        jnp.concatenate([cosine, cosine], axis=1),
        jnp.concatenate([-sine, sine], axis=1),
    )


def low(values):
    return values.astype(jnp.bfloat16)


def wide(values):
    return values.astype(jnp.float32)


def flip(axis, stride):
    return [(k, k ^ stride) for k in range(lax.axis_size(axis))]


class Job:
    def __init__(self, steps):
        self.steps, self.moves, self.value = steps, (), None
        self.resume(None)

    def resume(self, got):
        try:
            self.moves = self.steps.send(got)
        except StopIteration as end:
            self.moves, self.value = (), end.value


def beside(*jobs, kernels=()):
    jobs = [job for job in jobs if job.moves]
    given = [[move[0] for move in job.moves] for job in jobs], [args for _, args in kernels]
    arrays, args = lax.optimization_barrier(given)
    got = [
        [lax.ppermute(array, *move[1:]) for array, move in zip(held, job.moves)]
        for held, job in zip(arrays, jobs)
    ]
    results = [kernel[0](*own) for own, kernel in zip(args, kernels)]
    got, results = lax.optimization_barrier((got, results))
    for job, arrived in zip(jobs, got):
        job.resume(arrived)
    return results


def finish(*jobs):
    while any(job.moves for job in jobs):
        beside(*jobs)


def bits(axis):
    size = lax.axis_size(axis)
    return [1 << k for k in range(size.bit_length() - 1)]


def swap(array, axis, stride):
    return lax.ppermute(array, axis, flip(axis, stride))


def bit(axis, stride):
    return (lax.axis_index(axis) // stride) % 2


def line_gather(block, strides):
    block = block[None]
    for stride in strides:
        block = both(block, swap(block, "fsdp", stride), bit("fsdp", stride), 0)
        block = block.reshape(-1, *block.shape[2:])
    return block


def sum_small(values, axis):
    for stride in bits(axis):
        values = values + swap(values, axis, stride)
    return values


def pick(array, index, axis):
    return lax.dynamic_index_in_dim(array, index, axis, keepdims=False)


def both(mine, got, index, axis):
    lower = jnp.where(index == 0, mine, got)
    upper = jnp.where(index == 0, got, mine)
    return jnp.stack([lower, upper], axis=axis)


def plane_scatter(part):
    rows, width = part.shape
    heads = lax.axis_index("heads")
    x, y, core = heads % 2, heads // 2, lax.axis_index("tensor")
    cut = part.reshape(2, 2, 2, rows // 8, width)
    (got,) = yield [(pick(cut, 1 - core, 2), "tensor", SWAP)]
    chip = low(wide(pick(cut, core, 2)) + wide(got))
    first, second = chip[..., : width // 2], chip[..., width // 2 :]
    got = yield [(pick(first, 1 - x, 1), "heads", NEAR), (pick(second, 1 - y, 0), "heads", FAR)]
    first = low(wide(pick(first, x, 1)) + wide(got[0]))
    second = low(wide(pick(second, y, 0)) + wide(got[1]))
    got = yield [(pick(first, 1 - y, 0), "heads", FAR), (pick(second, 1 - x, 0), "heads", NEAR)]
    first = wide(pick(first, y, 0)) + wide(got[0])
    second = wide(pick(second, x, 0)) + wide(got[1])
    return jnp.concatenate([first, second], axis=-1)


def plane_gather(share):
    lead, rows, width = share.shape
    heads = lax.axis_index("heads")
    x, y, core = heads % 2, heads // 2, lax.axis_index("tensor")
    first, second = share[..., : width // 2], share[..., width // 2 :]
    got = yield [(first, "heads", FAR), (second, "heads", NEAR)]
    first = both(first, got[0], y, 1)
    second = both(second, got[1], x, 1)
    got = yield [(first, "heads", NEAR), (second, "heads", FAR)]
    first = both(first, got[0], x, 2)
    second = both(second, got[1], y, 1)
    chip = jnp.concatenate([first, second], axis=-1)
    (got,) = yield [(chip, "tensor", SWAP)]
    return both(chip, got, core, 3).reshape(lead, rows * 8, width)


def pair_swap(array):
    (got,) = yield [(array, "fsdp", flip("fsdp", 1))]
    return got


def pair_cot(cotangent):
    core = lax.axis_index("tensor")
    rows, width = cotangent.shape
    half = lax.dynamic_slice_in_dim(cotangent, core * (rows // 2), rows // 2, 0)
    got = []
    for cut in range(0, rows // 2, rows // 8):
        (arrived,) = yield [(half[cut : cut + rows // 8], "fsdp", flip("fsdp", 1))]
        got.append(arrived)
    got = jnp.concatenate(got, axis=0)
    (other,) = yield [(got, "tensor", SWAP)]
    return both(got, other, core, 0).reshape(rows, width)


def weights_gather(mine, given):
    size, rows = lax.axis_size("fsdp"), mine.shape[0]
    pair = flip("fsdp", 1)
    slots = [[] for _ in range(size)]
    slots[0] = [mine]
    if size == 4:
        far = flip("fsdp", 2)
        plan = [(0, 96, 0, 256), (96, 64), (160, 144, 256, 256), (304, 96), (400, 112)]
        unit = rows // 32
        for start, count, *near in plan:
            start, count = start * unit // 16, count * unit // 16
            moves = [(mine[start : start + count], "fsdp", far)]
            if near:
                at, span = near[0] * unit // 16, near[1] * unit // 16
                moves.append((given[at : at + span], "fsdp", pair))
            got = yield moves
            slots[2].append(got[0])
            slots[1] += got[1:]
        for steps in ([(0, 144)], [(144, 112), (256, 128)], [(384, 128)]):
            moves = []
            for start, count in steps:
                held = slots[1][start // 256]
                start, count = (start % 256) * unit // 16, count * unit // 16
                moves.append((held[start : start + count], "fsdp", far))
            slots[3] += yield moves
        return slots
    slots[1] = yield [(given, "fsdp", pair)]
    stride = 2
    while stride < size:
        for slot in range(stride):
            slots[stride + slot] = yield [(slots[slot][0], "fsdp", flip("fsdp", stride))]
        stride *= 2
    return slots


def weights_scatter(near, far):
    size, rows = lax.axis_size("fsdp"), near.shape[1]
    pair = flip("fsdp", 1)
    if size == 4:
        cross = flip("fsdp", 2)
        own, other = [], []
        unit = rows // 32
        first = []
        waiting = []
        plan = [(3, 0, 160), (3, 160, 128), (3, 288, 96), (3, 384, 128), (2, 0, 96), (2, 96, 176), (2, 272, 128), (2, 400, 112)]
        for slot, start, count in plan:
            here = slice(start * unit // 16, (start + count) * unit // 16)
            moves = [(far[slot - 2, here], "fsdp", cross)]
            if slot == 2 and waiting:
                moves.append((waiting.pop(0), "fsdp", pair))
            got = yield moves
            summed = wide(near[slot - 2, here]) + wide(got[0])
            if slot == 3:
                waiting.append(low(summed))
            else:
                own.append(summed)
            other += got[1:]
        return own, other
    sums = [near[k] for k in range(size // 2)] + [far[k] for k in range(size // 2)]
    stride = size // 2
    while stride > 1:
        for slot in range(stride):
            (got,) = yield [(low(sums[stride + slot]), "fsdp", flip("fsdp", stride))]
            sums[slot] = wide(sums[slot]) + wide(got)
        stride //= 2
    (got,) = yield [(low(sums[1]), "fsdp", pair)]
    return [wide(sums[0])], [got]


def rotate(values, cosine, sine):
    return values * cosine + pltpu.roll(values, HD // 2, 1) * sine


def call_params(megabytes):
    return pltpu.CompilerParams(vmem_limit_bytes=megabytes << 20)


def cheap():
    return pl.CostEstimate(flops=1000, bytes_accessed=1000, transcendentals=0)


def key_blocks(at, count):
    return max(0, at - BAND // ROWS), at + 1


def masked_probs(query, keys, seg_rows, seg_keys, first_row, first_key):
    scores = contract(query, keys, 1, 1) * HD**-0.5
    rows = first_row + lax.broadcasted_iota(jnp.int32, scores.shape, 0)
    cols = first_key + lax.broadcasted_iota(jnp.int32, scores.shape, 1)
    scores = jnp.where((rows >= cols) & (seg_rows == seg_keys), scores, -1e30)
    expo = jnp.exp(scores - jnp.max(scores, axis=-1, keepdims=True))
    return expo / jnp.sum(expo, axis=-1, keepdims=True)


def attend_kernel(
    group,
    normed_ref,
    proj_ref,
    cosine_ref,
    sine_ref,
    query_gain_ref,
    key_gain_ref,
    seg_rows_ref,
    seg_keys_ref,
    raw_ref,
    query_ref,
    key_ref,
    value_ref,
    mixed_ref,
    part_ref,
    keys,
    values,
):
    length, kv_cols = keys.shape
    kv_local = kv_cols // HD
    query_cols = kv_cols * group
    count = length // ROWS
    step = pl.program_id(0)
    split = query_cols + 2 * kv_cols
    raw = jnp.dot(normed_ref[...], proj_ref[:, :split], preferred_element_type=jnp.float32)
    raw_ref[...] = raw[:, : query_cols + kv_cols]
    cosine, sine = cosine_ref[...], sine_ref[...]
    here = pl.ds(pl.multiple_of(step * ROWS, ROWS), ROWS)

    def turned(head, gain_ref):
        one = raw[:, head * HD : (head + 1) * HD]
        return low(rotate(one * rms_parts(one) * gain_ref[...], cosine, sine))

    for kv in range(kv_local):
        at = slice(kv * HD, (kv + 1) * HD)
        new_keys = turned(query_cols // HD + kv, key_gain_ref)
        new_values = low(raw[:, query_cols + kv_cols + kv * HD : query_cols + kv_cols + (kv + 1) * HD])
        key_ref[:, at] = new_keys
        value_ref[:, at] = new_values
        keys[here, at] = new_keys
        values[here, at] = new_values
    for head in range(query_cols // HD):
        query_ref[:, head * HD : (head + 1) * HD] = turned(head, query_gain_ref)

    for at in range(count):

        @pl.when(step == at)
        def _():
            lower, upper = key_blocks(at, count)
            span = slice(lower * ROWS, upper * ROWS)
            for head in range(query_cols // HD):
                cols = slice(head * HD, (head + 1) * HD)
                kv = slice((head // group) * HD, (head // group + 1) * HD)
                probs = masked_probs(
                    query_ref[:, cols],
                    keys[span, kv],
                    seg_rows_ref[...],
                    seg_keys_ref[:, span],
                    at * ROWS,
                    lower * ROWS,
                )
                mixed_ref[:, cols] = low(
                    jnp.dot(low(probs), values[span, kv], preferred_element_type=jnp.float32)
                )

    part_ref[...] = low(contract(mixed_ref[...], proj_ref[:, split:], 1, 1))


def attend(group, normed, proj, cosine, sine, query_gain, key_gain, segment_row):
    length, model = normed.shape
    kv_cols = proj.shape[1] // (2 * group + 2)
    query_cols = kv_cols * group

    def rows(width):
        return pl.BlockSpec((ROWS, width), lambda i: (i, 0))

    def whole(array):
        return pl.BlockSpec(array.shape, lambda i: (0, 0))

    seg_rows, seg_keys = segment_row[:, None], segment_row[None, :]
    args = (normed, proj, cosine, sine, query_gain[None], key_gain[None], seg_rows, seg_keys)
    outs = [
        (query_cols + kv_cols, jnp.float32),
        (query_cols, jnp.bfloat16),
        (kv_cols, jnp.bfloat16),
        (kv_cols, jnp.bfloat16),
        (query_cols, jnp.bfloat16),
        (model, jnp.bfloat16),
    ]
    return pl.pallas_call(
        functools.partial(attend_kernel, group),
        grid=(length // ROWS,),
        in_specs=[
            rows(model),
            whole(proj),
            rows(HD),
            rows(HD),
            whole(args[4]),
            whole(args[5]),
            rows(1),
            whole(seg_keys),
        ],
        out_specs=[rows(width) for width, _ in outs],
        out_shape=[jax.ShapeDtypeStruct((length, width), kind) for width, kind in outs],
        scratch_shapes=[
            pltpu.VMEM((length, kv_cols), jnp.bfloat16),
            pltpu.VMEM((length, kv_cols), jnp.bfloat16),
        ],
        compiler_params=call_params(40),
        cost_estimate=cheap(),
        name="attend",
    )(*args)


def attend_back_kernel(
    group,
    grad_ref,
    proj_ref,
    cosine_ref,
    sine_ref,
    query_gain_ref,
    key_gain_ref,
    seg_rows_ref,
    seg_keys_ref,
    raw_ref,
    query_ref,
    key_ref,
    value_ref,
    tokens_ref,
    scale_ref,
    low_ref,
    part_ref,
    gain_ref,
    head_gain_ref,
    mixed_grad,
    query_sum,
    key_sum,
    value_sum,
):
    length, kv_cols = key_sum.shape
    query_cols = kv_cols * group
    count = length // ROWS
    split = query_cols + 2 * kv_cols
    for at in range(count):
        here = slice(at * ROWS, (at + 1) * ROWS)
        mixed_grad[here, :] = low(
            jnp.dot(grad_ref[here, :], proj_ref[:, split:], preferred_element_type=jnp.float32)
        )
    key_sum[...] = jnp.zeros_like(key_sum)
    value_sum[...] = jnp.zeros_like(value_sum)
    for at in range(count):
        here = slice(at * ROWS, (at + 1) * ROWS)
        lower, upper = key_blocks(at, count)
        span = slice(lower * ROWS, upper * ROWS)
        for head in range(query_cols // HD):
            cols = slice(head * HD, (head + 1) * HD)
            kv = slice((head // group) * HD, (head // group + 1) * HD)
            query = query_ref[here, cols]
            grad = mixed_grad[here, cols]
            probs = masked_probs(
                query,
                key_ref[span, kv],
                seg_rows_ref[here, :],
                seg_keys_ref[:, span],
                at * ROWS,
                lower * ROWS,
            )
            prob_grad = contract(grad, value_ref[span, kv], 1, 1)
            row_inner = jnp.sum(probs * prob_grad, axis=-1, keepdims=True)
            score_grad = low(HD**-0.5 * probs * (prob_grad - row_inner))
            query_sum[here, cols] = jnp.dot(
                score_grad, key_ref[span, kv], preferred_element_type=jnp.float32
            )
            key_sum[span, kv] += contract(score_grad, query, 0, 0)
            value_sum[span, kv] += contract(low(probs), grad, 0, 0)

    gain_ref[...] = jnp.zeros_like(gain_ref)
    head_gain_ref[...] = jnp.zeros_like(head_gain_ref)
    for at in range(count):
        here = slice(at * ROWS, (at + 1) * ROWS)
        cosine, sine = cosine_ref[here, :], -sine_ref[here, :]
        for head in range((query_cols + kv_cols) // HD):
            cols = slice(head * HD, (head + 1) * HD)
            own = slice(head * HD - query_cols, (head + 1) * HD - query_cols)
            is_query = head * HD < query_cols
            turned = rotate(query_sum[here, cols] if is_query else key_sum[here, own], cosine, sine)
            raw = raw_ref[here, cols]
            scale = rms_parts(raw)
            row = 0 if is_query else 1
            head_gain_ref[row : row + 1, :] += jnp.sum(turned * raw * scale, axis=0, keepdims=True)
            gain = query_gain_ref[...] if is_query else key_gain_ref[...]
            low_ref[here, cols] = low(norm_back(raw, scale, turned * gain))
        low_ref[here, query_cols + kv_cols :] = low(value_sum[here, :])
        part = contract(low_ref[here, :], proj_ref[:, :split], 1, 1)
        part_ref[here, :] = low(part)
        gain_ref[...] += jnp.sum(part * wide(tokens_ref[here, :]) * scale_ref[here, :], axis=0, keepdims=True)


def attend_back(
    group, grad, proj, cosine, sine, query_gain, key_gain, segment_row, raw, query, key, value, tokens, scale
):
    length, model = grad.shape
    query_cols, kv_cols = query.shape[1], key.shape[1]
    args = (
        grad, proj, cosine, sine, query_gain[None], key_gain[None],
        segment_row[:, None], segment_row[None, :], raw, query, key, value, tokens, scale,
    )
    return pl.pallas_call(
        functools.partial(attend_back_kernel, group),
        in_specs=[pl.BlockSpec(memory_space=pltpu.VMEM)] * len(args),
        out_specs=[pl.BlockSpec(memory_space=pltpu.VMEM)] * 4,
        out_shape=[
            jax.ShapeDtypeStruct((length, query_cols + 2 * kv_cols), jnp.bfloat16),
            jax.ShapeDtypeStruct((length, model), jnp.bfloat16),
            jax.ShapeDtypeStruct((1, model), jnp.float32),
            jax.ShapeDtypeStruct((2, HD), jnp.float32),
        ],
        scratch_shapes=[
            pltpu.VMEM((length, query_cols), jnp.bfloat16),
            pltpu.VMEM((length, query_cols), jnp.float32),
            pltpu.VMEM((length, kv_cols), jnp.float32),
            pltpu.VMEM((length, kv_cols), jnp.float32),
        ],
        compiler_params=call_params(48),
        cost_estimate=cheap(),
        name="attend_back",
    )(*args)


def feed_kernel(layout, shard, place_ref, normed_ref, cotangent_ref, *refs):
    parts, (act_ref, gate_up_grad_ref, normed_grad_ref, proj_ref) = refs[:-4], refs[-4:]
    half = act_ref.shape[1]
    if layout:

        @pl.when(pl.program_id(0) == 0)
        def _():
            for part, (slot, first) in zip(parts, layout):
                owner = lax.bitwise_xor(place_ref[0], slot)
                start = pl.multiple_of(owner * shard + first, 16)
                proj_ref[pl.ds(start, part.shape[0]), :] = part[...]

        proj = proj_ref
    else:
        proj = parts[0]
    gate_up = jnp.dot(normed_ref[...], proj[:, : 2 * half], preferred_element_type=jnp.float32)
    gate, up = gate_up[:, :half], gate_up[:, half:]
    act_grad = jnp.dot(cotangent_ref[...], proj[:, 2 * half :], preferred_element_type=jnp.float32)
    sigmoid = jax.nn.sigmoid(gate)
    silu = gate * sigmoid
    act_ref[...] = low(silu * up)
    gate_up_grad_ref[:, :half] = low(act_grad * up * sigmoid * (1.0 + gate * (1.0 - sigmoid)))
    gate_up_grad_ref[:, half:] = low(act_grad * silu)
    normed_grad_ref[...] = low(contract(gate_up_grad_ref[...], proj[:, : 2 * half], 1, 1))


def feed(place, normed, cotangent, *slots):
    tokens, model = normed.shape
    layout, parts = [], []
    if len(slots) == 1:
        parts = slots
    else:
        for slot, held in enumerate(slots):
            first = 0
            for part in held:
                layout.append((slot, first))
                parts.append(part)
                first += part.shape[0]
    width = parts[0].shape[1]
    half = width // 3
    shard = model // len(slots)

    def rows(width):
        return pl.BlockSpec((ROWS, width), lambda i, place: (i, 0))

    def whole(shape):
        return pl.BlockSpec(shape, lambda i, place: (0, 0), pipeline_mode=pl.Buffered(1))

    widths = [half, 2 * half, model]
    out_shape = [jax.ShapeDtypeStruct((tokens, w), jnp.bfloat16) for w in widths]
    proj_shape = (model, width) if layout else (16, 128)
    return pl.pallas_call(
        functools.partial(feed_kernel, layout, shard),
        grid_spec=pltpu.PrefetchScalarGridSpec(
            num_scalar_prefetch=1,
            grid=(tokens // ROWS,),
            in_specs=[rows(model), rows(model)] + [whole(p.shape) for p in parts],
            out_specs=[rows(w) for w in widths] + [whole(proj_shape)],
        ),
        out_shape=out_shape + [jax.ShapeDtypeStruct(proj_shape, jnp.bfloat16)],
        compiler_params=call_params(40),
        cost_estimate=cheap(),
        name="feed",
    )(place, normed, cotangent, *parts)


def feed_weights_kernel(
    slots, place_ref, normed_own, normed_pair, cot_own, cot_pair, grad_own, grad_pair, act_own, act_pair, out_ref
):
    wide_cols = grad_own.shape[1]
    out_ref[0, :, :wide_cols] = low(
        contract(normed_own[...], grad_own[...], 0, 0) + contract(normed_pair[...], grad_pair[...], 0, 0)
    )
    out_ref[0, :, wide_cols:] = low(
        contract(cot_own[...], act_own[...], 0, 0) + contract(cot_pair[...], act_pair[...], 0, 0)
    )


def feed_weights(size, slots, place, normed, cotangent, grad, act):
    length, model = normed[0].shape
    shard = model // size
    width = grad[0].shape[1] + act[0].shape[1]
    first, count = slots

    def columns():
        return pl.BlockSpec((length, shard), lambda i, place: (0, lax.bitwise_xor(place[0], first + i)))

    def whole(array):
        return pl.BlockSpec(array.shape, lambda i, place: (0, 0), pipeline_mode=pl.Buffered(1))

    return pl.pallas_call(
        functools.partial(feed_weights_kernel, slots),
        grid_spec=pltpu.PrefetchScalarGridSpec(
            num_scalar_prefetch=1,
            grid=(count,),
            in_specs=[columns()] * 4 + [whole(a) for a in (*grad, *act)],
            out_specs=pl.BlockSpec((1, shard, width), lambda i, place: (i, 0, 0)),
        ),
        out_shape=jax.ShapeDtypeStruct((count, shard, width), jnp.bfloat16),
        compiler_params=call_params(48),
        cost_estimate=cheap(),
        name="feed_weights",
    )(place, *normed, *cotangent, *grad, *act)


def feed_sums_kernel(count, side_ref, *refs):
    own, other, outs = refs[:count], refs[count:-3], refs[-3:]
    half = outs[0].shape[1]
    mine = pl.program_id(0) == side_ref[0]
    for held, keep in ((own, mine), (other, jnp.logical_not(mine))):

        @pl.when(keep)
        def _():
            first = 0
            for part in held:
                for k, out in enumerate(outs):
                    out[first : first + part.shape[0], :] = wide(part[:, k * half : (k + 1) * half])
                first += part.shape[0]


def feed_sums(side, own, other):
    rows, width = sum(part.shape[0] for part in own), own[0].shape[1]
    half = width // 3
    parts = (*own, *other)
    return pl.pallas_call(
        functools.partial(feed_sums_kernel, len(own)),
        grid_spec=pltpu.PrefetchScalarGridSpec(
            num_scalar_prefetch=1,
            grid=(2,),
            in_specs=[
                pl.BlockSpec(p.shape, lambda i, side: (0, 0), pipeline_mode=pl.Buffered(1)) for p in parts
            ],
            out_specs=[pl.BlockSpec((rows, half), lambda i, side: (0, i))] * 3,
        ),
        out_shape=[jax.ShapeDtypeStruct((rows, 2 * half), jnp.float32)] * 3,
        compiler_params=call_params(32),
        cost_estimate=cheap(),
        name="feed_sums",
    )(side, *parts)


def per_device(
    tokens,
    segments,
    ln1_gain,
    w_query,
    w_key,
    w_value,
    query_gain,
    key_gain,
    w_out,
    ln2_gain,
    w_gate,
    w_up,
    w_down,
    cotangent,
):
    length, model = tokens.shape
    query_cols, key_cols = w_query.shape[1], w_key.shape[1]
    query_heads = query_cols // HD
    kv_local = key_cols // HD
    group = query_heads // kv_local
    size = lax.axis_size("fsdp")
    shard = model // size
    hidden = w_gate.shape[1]
    half = hidden // 2
    strides = bits("fsdp")
    group_size = lax.axis_size(PLANE)
    share_rows = length // group_size
    share_start = lax.axis_index(PLANE) * share_rows
    segment_row = segments[0]

    def share_of(array):
        return lax.dynamic_slice_in_dim(array, share_start, share_rows, 0)

    proj = lax.all_gather(
        jnp.concatenate([w_query, w_key, w_value, w_out], axis=1), "fsdp", axis=0, tiled=True
    )
    side = bit("fsdp", 1)
    place = lax.axis_index("fsdp")[None]

    def half_of(which):
        return jnp.concatenate(
            [lax.dynamic_slice_in_dim(w, which * half, half, 1) for w in (w_gate, w_up, w_down)], axis=1
        )

    mine, given = half_of(side), half_of(1 - side)

    gains = line_gather(jnp.concatenate([ln1_gain, ln2_gain, query_gain, key_gain]), strides)
    gain_attn = gains[:, :shard].reshape(model)
    gain_ffn = gains[:, shard : 2 * shard].reshape(model)
    head_part = HD // size
    query_norm = gains[:, 2 * shard : 2 * shard + head_part].reshape(HD)
    key_norm = gains[:, 2 * shard + head_part :].reshape(HD)

    cosine, sine = rope_tables(doc_positions(segment_row))
    block_in = tokens.astype(jnp.float32)
    scale_one = rms_parts(block_in)
    normed = (block_in * scale_one * gain_attn.astype(jnp.float32)).astype(jnp.bfloat16)
    query_gain_wide, key_gain_wide = wide(query_norm), wide(key_norm)
    weights = Job(weights_gather(mine, given))
    cot = Job(pair_cot(cotangent))
    attend_args = (normed, proj, cosine, sine, query_gain_wide, key_gain_wide, segment_row)
    ((raw, query_rot, key_rot, values, mixed_low, out_part),) = beside(
        weights, kernels=[(functools.partial(attend, group), attend_args)]
    )
    out_sum = Job(plane_scatter(out_part))
    beside(out_sum, weights)
    beside(out_sum, weights)
    beside(out_sum, weights, cot)
    hidden_share = wide(share_of(tokens)) + out_sum.value
    scale_share = rms_parts(hidden_share)
    normed_share = low(hidden_share * scale_share * wide(gain_ffn))
    pair_share = Job(pair_swap(normed_share))
    beside(pair_share, weights)
    gather = Job(plane_gather(jnp.stack([normed_share, pair_share.value])))
    beside(gather, weights, cot)
    beside(gather, weights, cot)
    beside(gather, weights, cot)
    finish(gather, weights, cot)
    normed_two, pair_normed_two = gather.value
    pair_cotangent = cot.value

    pair_act, pair_grad, pair_normed_grad, feed_proj = feed(
        place, pair_normed_two, pair_cotangent, *weights.value
    )
    pair_sum = Job(plane_scatter(pair_normed_grad))
    ((act, grad, normed_grad, _),) = beside(
        pair_sum, kernels=[(feed, (place, normed_two, cotangent, feed_proj))]
    )
    own_sum = Job(plane_scatter(normed_grad))
    weight_args = (
        place, (normed_two, pair_normed_two), (cotangent, pair_cotangent), (grad, pair_grad), (act, pair_act)
    )
    (far,) = beside(
        pair_sum,
        own_sum,
        kernels=[(functools.partial(feed_weights, size, (size // 2, size // 2)), weight_args)],
    )
    near = feed_weights(size, (0, size // 2), *weight_args)
    weight_sums = Job(weights_scatter(near, far))
    beside(pair_sum, own_sum, weight_sums)
    pair_share = Job(pair_swap(low(pair_sum.value)))
    beside(pair_share, own_sum, weight_sums)
    grad_share = own_sum.value + wide(pair_share.value)
    hidden_grad_share = wide(share_of(cotangent)) + norm_back(
        hidden_share, scale_share, grad_share * wide(gain_ffn)
    )
    ffn_gain_part = jnp.sum(grad_share * hidden_share * scale_share, axis=0)
    gather = Job(plane_gather(low(hidden_grad_share)[None]))
    beside(gather, weight_sums)
    beside(gather, weight_sums)
    beside(gather, weight_sums)
    attn_out_grad = gather.value[0]
    down_proj = feed_proj[:, 2 * half :]
    out_sum = Job(plane_scatter(low(contract(act, down_proj, 1, 1))))
    pair_out_sum = Job(plane_scatter(low(contract(pair_act, down_proj, 1, 1))))

    out_w_part = low(contract(attn_out_grad, mixed_low, 0, 0))
    out_w_grad = wide(lax.psum_scatter(out_w_part, "fsdp", scatter_dimension=0, tiled=True))

    back_args = (
        attn_out_grad, proj, cosine, sine, query_gain_wide, key_gain_wide, segment_row,
        raw, query_rot, key_rot, values, tokens, scale_one,
    )
    ((low_grad, normed_part, attn_gain_part, head_gain_part),) = beside(
        weight_sums, pair_out_sum, kernels=[(functools.partial(attend_back, group), back_args)]
    )
    query_gain_part, key_gain_part = head_gain_part[0], head_gain_part[1]
    attn_w_part = low(contract(normed, low_grad, 0, 0))
    attn_w_grad = wide(lax.psum_scatter(attn_w_part, "fsdp", scatter_dimension=0, tiled=True))
    normed_sum = Job(plane_scatter(normed_part))
    beside(normed_sum, weight_sums, pair_out_sum, out_sum)
    beside(normed_sum, weight_sums, pair_out_sum, out_sum)
    pair_out = Job(pair_swap(low(pair_out_sum.value)))
    beside(normed_sum, weight_sums, pair_out, out_sum)
    finish(weight_sums, pair_out, out_sum)
    normed_share = normed_sum.value
    block_out = low(hidden_share + out_sum.value + wide(pair_out.value))
    gate_w_grad, up_w_grad, down_w_grad = feed_sums(side[None], *weight_sums.value)

    token_share = wide(share_of(tokens))
    scale_one_share = share_of(scale_one)
    tokens_grad = (
        hidden_grad_share + norm_back(token_share, scale_one_share, normed_share * wide(gain_attn))
    ).astype(jnp.bfloat16)

    gain_sums = jnp.concatenate(
        [
            attn_gain_part.reshape(size, shard),
            ffn_gain_part.reshape(size, shard),
            query_gain_part.reshape(size, head_part),
            key_gain_part.reshape(size, head_part),
        ],
        axis=1,
    )
    gain_sums = sum_small(sum_small(sum_small(gain_sums, "tensor"), "heads"), "fsdp")
    gain_sums = pick(gain_sums, lax.axis_index("fsdp"), 0)
    ln1_grad = gain_sums[:shard]
    ln2_grad = gain_sums[shard : 2 * shard]
    query_gain_grad = gain_sums[2 * shard : 2 * shard + head_part]
    key_gain_grad = gain_sums[2 * shard + head_part :]

    return (
        block_out,
        tokens_grad,
        ln1_grad,
        attn_w_grad[:, :query_cols],
        attn_w_grad[:, query_cols : query_cols + key_cols],
        attn_w_grad[:, query_cols + key_cols :],
        query_gain_grad,
        key_gain_grad,
        out_w_grad,
        ln2_grad,
        gate_w_grad,
        up_w_grad,
        down_w_grad,
    )


def solution(mesh):
    in_specs = (
        P("fsdp", None),
        P("fsdp", None),
        P("fsdp"),
        P("fsdp", ("heads", "tensor")),
        P("fsdp", ("heads", "tensor")),
        P("fsdp", ("heads", "tensor")),
        P("fsdp"),
        P("fsdp"),
        P("fsdp", ("heads", "tensor")),
        P("fsdp"),
        P("fsdp", ("heads", "tensor")),
        P("fsdp", ("heads", "tensor")),
        P("fsdp", ("heads", "tensor")),
        P("fsdp", None),
    )
    out_specs = (
        P(("fsdp", "heads", "tensor"), None),
        P(("fsdp", "heads", "tensor"), None),
        P("fsdp"),
        P("fsdp", ("heads", "tensor")),
        P("fsdp", ("heads", "tensor")),
        P("fsdp", ("heads", "tensor")),
        P("fsdp"),
        P("fsdp"),
        P("fsdp", ("heads", "tensor")),
        P("fsdp"),
        P("fsdp", ("heads", "tensor")),
        P("fsdp", ("heads", "tensor")),
        P("fsdp", ("heads", "tensor")),
    )
    return jax.shard_map(
        per_device, mesh=mesh, in_specs=in_specs, out_specs=out_specs, check_vma=False
    )
```

```python
import functools

import jax
import jax.numpy as jnp
from jax import lax
from jax.experimental import pallas as pl
from jax.experimental.pallas import tpu as pltpu
from jax.sharding import PartitionSpec as P

HD = 128


EPSILON = 1e-06
THETA = 1000000.0
ROWS = 256
BAND = 512
PLANE = ("heads", "tensor")
SWAP = ((0, 1), (1, 0))
NEAR = ((0, 1), (1, 0), (2, 3), (3, 2))
FAR = ((0, 2), (2, 0), (1, 3), (3, 1))


def rms_parts(values):
    return lax.rsqrt(jnp.mean(values * values, axis=-1, keepdims=True) + EPSILON)


def norm_back(values, scale, upstream):
    return scale * upstream - values * scale**3 * jnp.mean(
        values * upstream, axis=-1, keepdims=True
    )


def contract(left, right, left_dim, right_dim):
    return lax.dot_general(
        left, right, (((left_dim,), (right_dim,)), ((), ())), preferred_element_type=jnp.float32
    )


def doc_positions(segment_row):
    places = jnp.arange(segment_row.shape[0], dtype=jnp.int32)
    previous = jnp.concatenate([segment_row[:1], segment_row[:-1]])
    starts = lax.cummax(jnp.where(segment_row != previous, places, 0), axis=0)
    return places - starts


def rope_tables(positions):
    frequency = THETA ** (-(jnp.arange(HD // 2, dtype=jnp.float32) * 2.0 / HD))
    angles = positions.astype(jnp.float32)[:, None] * frequency[None, :]
    cosine, sine = jnp.cos(angles), jnp.sin(angles)
    return (
        jnp.concatenate([cosine, cosine], axis=1),
        jnp.concatenate([-sine, sine], axis=1),
    )


def low(values):
    return values.astype(jnp.bfloat16)


def wide(values):
    return values.astype(jnp.float32)


def flip(axis, stride):
    return [(k, k ^ stride) for k in range(lax.axis_size(axis))]


def after(value, *others):
    return lax.optimization_barrier((value, *others))[0]


def apart(work, *args):
    zeros = [jnp.zeros(out.shape, out.dtype) for out in jax.eval_shape(work, *args)]
    return lax.cond(
        lax.axis_index("fsdp") < lax.axis_size("fsdp"), work, lambda *_: tuple(zeros), *args
    )


class Job:
    def __init__(self, steps):
        self.steps, self.moves, self.keep, self.value = steps, (), (), None
        self.resume(None)

    def resume(self, got):
        try:
            given = self.steps.send(got)
            self.moves, self.keep = given if isinstance(given, tuple) else (given, ())
        except StopIteration as end:
            self.moves, self.keep, self.value = (), (), end.value


def beside(*jobs, kernels=()):
    jobs = [job for job in jobs if job.moves]
    given = [[move[0] for move in job.moves] for job in jobs], [args for _, args in kernels]
    arrays, args = lax.optimization_barrier(given)
    got = [
        [lax.ppermute(array, *move[1:]) for array, move in zip(held, job.moves)]
        for held, job in zip(arrays, jobs)
    ]
    results = [kernel[0](*own) for own, kernel in zip(args, kernels)]
    got, results = lax.optimization_barrier((got, results))
    for job, arrived in zip(jobs, got):
        job.resume(arrived)
    return results


def finish(*jobs):
    while any(job.moves for job in jobs):
        beside(*jobs)


def bits(axis):
    size = lax.axis_size(axis)
    return [1 << k for k in range(size.bit_length() - 1)]


def swap(array, axis, stride):
    return lax.ppermute(array, axis, flip(axis, stride))


def bit(axis, stride):
    return (lax.axis_index(axis) // stride) % 2


def line_gather(block, strides):
    block = block[None]
    for stride in strides:
        block = both(block, swap(block, "fsdp", stride), bit("fsdp", stride), 0)
        block = block.reshape(-1, *block.shape[2:])
    return block


def pick(array, index, axis):
    return lax.dynamic_index_in_dim(array, index, axis, keepdims=False)


def both(mine, got, index, axis):
    lower = jnp.where(index == 0, mine, got)
    upper = jnp.where(index == 0, got, mine)
    return jnp.stack([lower, upper], axis=axis)


def position():
    heads = lax.axis_index("heads")
    return jnp.stack([lax.axis_index("tensor"), heads % 2, heads // 2]).astype(jnp.int32)


def vmem_call(kernel, name, megabytes, out_shape, *args):
    return pl.pallas_call(
        kernel,
        in_specs=[pl.BlockSpec(memory_space=pltpu.SMEM)]
        + [pl.BlockSpec(memory_space=pltpu.VMEM)] * len(args),
        out_specs=[pl.BlockSpec(memory_space=pltpu.VMEM)] * len(out_shape),
        out_shape=[jax.ShapeDtypeStruct(shape, jnp.bfloat16) for shape in out_shape],
        compiler_params=call_params(megabytes),
        cost_estimate=cheap(),
        name=name,
    )(position(), *args)


def fold_chip_kernel(position_ref, keep_ref, got_ref, give_first, keep_first, give_second, keep_second):
    x, y = position_ref[1], position_ref[2]
    middle = keep_ref.shape[-1] // 2
    first, second = slice(0, middle), slice(middle, 2 * middle)

    def summed(row, column, cols):
        return low(wide(keep_ref[row, column, :, cols]) + wide(got_ref[row, column, :, cols]))

    for k in range(2):
        give_first[k] = summed(k, 1 - x, first)
        keep_first[k] = summed(k, x, first)
        give_second[k] = summed(1 - y, k, second)
        keep_second[k] = summed(y, k, second)


def fold_chip(keep, got):
    rows, width = keep.shape
    shape = (2, 2, rows // 4, width)
    return vmem_call(
        fold_chip_kernel, "fold_chip", 24, [(2, rows // 4, width // 2)] * 4, keep.reshape(shape), got.reshape(shape)
    )


def fold_line_kernel(
    position_ref, keep_first_ref, got_first_ref, keep_second_ref, got_second_ref, give_first, keep_first, give_second, keep_second
):
    x, y = position_ref[1], position_ref[2]
    for at, keep_ref, got_ref, give, keep in (
        (y, keep_first_ref, got_first_ref, give_first, keep_first),
        (x, keep_second_ref, got_second_ref, give_second, keep_second),
    ):
        give[...] = low(wide(keep_ref[1 - at]) + wide(got_ref[1 - at]))
        keep[...] = low(wide(keep_ref[at]) + wide(got_ref[at]))


def fold_line(keep_first, got_first, keep_second, got_second):
    shape = keep_first.shape[1:]
    return vmem_call(
        fold_line_kernel, "fold_line", 16, [shape] * 4, keep_first, got_first, keep_second, got_second
    )


def plane_scatter(keep, give):
    (got,) = yield [(give, "tensor", SWAP)]
    folded = fold_chip(keep, got)
    return (yield from chip_scatter(*folded))


def chip_scatter(give_first, keep_first, give_second, keep_second):
    held = (give_first, keep_first, give_second, keep_second)
    got = yield [(give_first, "heads", NEAR), (give_second, "heads", FAR)], held
    return (yield from line_scatter(*fold_line(keep_first, got[0], keep_second, got[1])))


def line_scatter(give_first, keep_first, give_second, keep_second):
    held = (give_first, keep_first, give_second, keep_second)
    got = yield [(give_first, "heads", FAR), (give_second, "heads", NEAR)], held
    first = wide(keep_first) + wide(got[0])
    second = wide(keep_second) + wide(got[1])
    return jnp.concatenate([first, second], axis=-1)


def open_line_kernel(position_ref, first_ref, got_first_ref, second_ref, got_second_ref, first, second):
    x, y = position_ref[1], position_ref[2]
    first[y] = first_ref[...]
    first[1 - y] = got_first_ref[...]
    second[x] = second_ref[...]
    second[1 - x] = got_second_ref[...]


def open_chip_kernel(position_ref, first_ref, got_first_ref, second_ref, got_second_ref, out_ref):
    x, y = position_ref[1], position_ref[2]
    lead, middle = first_ref.shape[1], first_ref.shape[-1]
    for k in range(lead):
        for j in range(2):
            out_ref[k, j, x, :, :middle] = first_ref[j, k]
            out_ref[k, j, 1 - x, :, :middle] = got_first_ref[j, k]
            out_ref[k, y, j, :, middle:] = second_ref[j, k]
            out_ref[k, 1 - y, j, :, middle:] = got_second_ref[j, k]


def plane_gather(share):
    lead, rows, width = share.shape
    first, second = share[..., : width // 2], share[..., width // 2 :]
    got = yield [(first, "heads", FAR), (second, "heads", NEAR)]
    first, second = vmem_call(
        open_line_kernel, "open_line", 16, [(2, lead, rows, width // 2)] * 2, first, got[0], second, got[1]
    )
    got = yield [(first, "heads", NEAR), (second, "heads", FAR)]
    (mine,) = vmem_call(
        open_chip_kernel, "open_chip", 24, [(lead, 2, 2, rows, width)], first, got[0], second, got[1]
    )
    mine = mine.reshape(lead, 4 * rows, width)
    (other,) = yield [(mine, "tensor", SWAP)]
    return mine, other


def pair_swap(array, pieces=1):
    rows = array.shape[0] // pieces
    got = []
    for k in range(pieces):
        got += yield [(array[k * rows : (k + 1) * rows], "fsdp", flip("fsdp", 1))]
    return jnp.concatenate(got, axis=0) if pieces > 1 else got[0]


def pair_gather(share, pieces):
    got = yield from pair_swap(share, pieces)
    return (yield from plane_gather(got[None]))


def sum_all(values):
    for axis in ("tensor", "heads", "fsdp"):
        for stride in bits(axis):
            (got,) = yield [(values, axis, flip(axis, stride))]
            values = values + got
    return values


def alike():
    return [list(range(k, lax.axis_size("fsdp"), 2)) for k in range(2)]


def rotate(values, cosine, sine):
    return values * cosine + pltpu.roll(values, HD // 2, 1) * sine


def call_params(megabytes):
    return pltpu.CompilerParams(vmem_limit_bytes=megabytes << 20)


def cheap():
    return pl.CostEstimate(flops=1000, bytes_accessed=1000, transcendentals=0)


def key_blocks(at, count):
    return max(0, at - BAND // ROWS), at + 1


def masked_probs(query, keys, seg_rows, seg_keys, first_row, first_key):
    scores = contract(query, keys, 1, 1) * HD**-0.5
    rows = first_row + lax.broadcasted_iota(jnp.int32, scores.shape, 0)
    cols = first_key + lax.broadcasted_iota(jnp.int32, scores.shape, 1)
    scores = jnp.where((rows >= cols) & (seg_rows == seg_keys), scores, -1e30)
    expo = jnp.exp(scores - jnp.max(scores, axis=-1, keepdims=True))
    return expo / jnp.sum(expo, axis=-1, keepdims=True)


def by_core(core, block):
    middle = block.shape[0] // 2
    lower, upper = block[:middle], block[middle:]
    first = core == 0
    return jnp.where(first, lower, upper), jnp.where(first, upper, lower)


def joined(core, mine, other):
    first = core == 0
    return jnp.concatenate([jnp.where(first, mine, other), jnp.where(first, other, mine)], axis=0)


def attend_kernel(
    group,
    normed_ref,
    proj_ref,
    cosine_ref,
    sine_ref,
    query_gain_ref,
    key_gain_ref,
    seg_rows_ref,
    seg_keys_ref,
    position_ref,
    raw_ref,
    query_ref,
    key_ref,
    value_ref,
    mixed_ref,
    keep_ref,
    give_ref,
    keys,
    values,
):
    length, kv_cols = keys.shape
    kv_local = kv_cols // HD
    query_cols = kv_cols * group
    count = length // ROWS
    step = pl.program_id(0)
    split = query_cols + 2 * kv_cols
    raw = jnp.dot(normed_ref[...], proj_ref[:, :split], preferred_element_type=jnp.float32)
    raw_ref[...] = raw[:, : query_cols + kv_cols]
    cosine, sine = cosine_ref[...], sine_ref[...]
    here = pl.ds(pl.multiple_of(step * ROWS, ROWS), ROWS)

    def turned(head, gain_ref):
        one = raw[:, head * HD : (head + 1) * HD]
        return low(rotate(one * rms_parts(one) * gain_ref[...], cosine, sine))

    for kv in range(kv_local):
        at = slice(kv * HD, (kv + 1) * HD)
        new_keys = turned(query_cols // HD + kv, key_gain_ref)
        new_values = low(raw[:, query_cols + kv_cols + kv * HD : query_cols + kv_cols + (kv + 1) * HD])
        key_ref[:, at] = new_keys
        value_ref[:, at] = new_values
        keys[here, at] = new_keys
        values[here, at] = new_values
    for head in range(query_cols // HD):
        query_ref[:, head * HD : (head + 1) * HD] = turned(head, query_gain_ref)

    for at in range(count):

        @pl.when(step == at)
        def _():
            lower, upper = key_blocks(at, count)
            span = slice(lower * ROWS, upper * ROWS)
            for head in range(query_cols // HD):
                cols = slice(head * HD, (head + 1) * HD)
                kv = slice((head // group) * HD, (head // group + 1) * HD)
                probs = masked_probs(
                    query_ref[:, cols],
                    keys[span, kv],
                    seg_rows_ref[...],
                    seg_keys_ref[:, span],
                    at * ROWS,
                    lower * ROWS,
                )
                mixed_ref[:, cols] = low(
                    jnp.dot(low(probs), values[span, kv], preferred_element_type=jnp.float32)
                )

    keep_ref[...], give_ref[...] = by_core(
        position_ref[0], low(contract(mixed_ref[...], proj_ref[:, split:], 1, 1))
    )


def attend(group, normed, proj, cosine, sine, query_gain, key_gain, segment_row):
    length, model = normed.shape
    kv_cols = proj.shape[1] // (2 * group + 2)
    query_cols = kv_cols * group

    def rows(width):
        return pl.BlockSpec((ROWS, width), lambda i: (i, 0))

    def whole(array):
        return pl.BlockSpec(array.shape, lambda i: (0, 0))

    seg_rows, seg_keys = segment_row[:, None], segment_row[None, :]
    args = (normed, proj, cosine, sine, query_gain[None], key_gain[None], seg_rows, seg_keys, position())
    outs = [
        (query_cols + kv_cols, jnp.float32),
        (query_cols, jnp.bfloat16),
        (kv_cols, jnp.bfloat16),
        (kv_cols, jnp.bfloat16),
        (query_cols, jnp.bfloat16),
    ]
    halves = (length // 2, model)
    return pl.pallas_call(
        functools.partial(attend_kernel, group),
        grid=(length // ROWS,),
        in_specs=[
            rows(model),
            whole(proj),
            rows(HD),
            rows(HD),
            whole(args[4]),
            whole(args[5]),
            rows(1),
            whole(seg_keys),
            pl.BlockSpec(memory_space=pltpu.SMEM),
        ],
        out_specs=[rows(width) for width, _ in outs]
        + [pl.BlockSpec((ROWS // 2, model), lambda i: (i, 0))] * 2,
        out_shape=[jax.ShapeDtypeStruct((length, width), kind) for width, kind in outs]
        + [jax.ShapeDtypeStruct(halves, jnp.bfloat16)] * 2,
        scratch_shapes=[
            pltpu.VMEM((length, kv_cols), jnp.bfloat16),
            pltpu.VMEM((length, kv_cols), jnp.bfloat16),
        ],
        compiler_params=call_params(40),
        cost_estimate=cheap(),
        name="attend",
    )(*args)


def attend_back_kernel(
    group,
    grad_mine_ref,
    grad_other_ref,
    proj_ref,
    cosine_ref,
    sine_ref,
    query_gain_ref,
    key_gain_ref,
    seg_rows_ref,
    seg_keys_ref,
    raw_ref,
    query_ref,
    key_ref,
    value_ref,
    tokens_ref,
    scale_ref,
    normed_ref,
    mixed_ref,
    position_ref,
    weight_ref,
    keep_ref,
    give_ref,
    gain_ref,
    head_gain_ref,
    grad_ref,
    low_ref,
    mixed_grad,
    query_sum,
    key_sum,
    value_sum,
):
    length, kv_cols = key_sum.shape
    query_cols = kv_cols * group
    count = length // ROWS
    split = query_cols + 2 * kv_cols
    for at in range(count):
        here = slice(at * ROWS, (at + 1) * ROWS)
        rows = slice(at * ROWS // 2, (at + 1) * ROWS // 2)
        grad_ref[here, :] = joined(position_ref[0], grad_mine_ref[rows, :], grad_other_ref[rows, :])
        mixed_grad[here, :] = low(
            jnp.dot(grad_ref[here, :], proj_ref[:, split:], preferred_element_type=jnp.float32)
        )
    key_sum[...] = jnp.zeros_like(key_sum)
    value_sum[...] = jnp.zeros_like(value_sum)
    for at in range(count):
        here = slice(at * ROWS, (at + 1) * ROWS)
        lower, upper = key_blocks(at, count)
        span = slice(lower * ROWS, upper * ROWS)
        for head in range(query_cols // HD):
            cols = slice(head * HD, (head + 1) * HD)
            kv = slice((head // group) * HD, (head // group + 1) * HD)
            query = query_ref[here, cols]
            grad = mixed_grad[here, cols]
            probs = masked_probs(
                query,
                key_ref[span, kv],
                seg_rows_ref[here, :],
                seg_keys_ref[:, span],
                at * ROWS,
                lower * ROWS,
            )
            prob_grad = contract(grad, value_ref[span, kv], 1, 1)
            row_inner = jnp.sum(probs * prob_grad, axis=-1, keepdims=True)
            score_grad = low(HD**-0.5 * probs * (prob_grad - row_inner))
            query_sum[here, cols] = jnp.dot(
                score_grad, key_ref[span, kv], preferred_element_type=jnp.float32
            )
            key_sum[span, kv] += contract(score_grad, query, 0, 0)
            value_sum[span, kv] += contract(low(probs), grad, 0, 0)

    gain_ref[...] = jnp.zeros_like(gain_ref)
    head_gain_ref[...] = jnp.zeros_like(head_gain_ref)
    for at in range(count):
        here = slice(at * ROWS, (at + 1) * ROWS)
        cosine, sine = cosine_ref[here, :], -sine_ref[here, :]
        for head in range((query_cols + kv_cols) // HD):
            cols = slice(head * HD, (head + 1) * HD)
            own = slice(head * HD - query_cols, (head + 1) * HD - query_cols)
            is_query = head * HD < query_cols
            turned = rotate(query_sum[here, cols] if is_query else key_sum[here, own], cosine, sine)
            raw = raw_ref[here, cols]
            scale = rms_parts(raw)
            row = 0 if is_query else 1
            head_gain_ref[row : row + 1, :] += jnp.sum(turned * raw * scale, axis=0, keepdims=True)
            gain = query_gain_ref[...] if is_query else key_gain_ref[...]
            low_ref[here, cols] = low(norm_back(raw, scale, turned * gain))
        low_ref[here, query_cols + kv_cols :] = low(value_sum[here, :])
        part = contract(low_ref[here, :], proj_ref[:, :split], 1, 1)
        rows = slice(at * ROWS // 2, (at + 1) * ROWS // 2)
        keep_ref[rows, :], give_ref[rows, :] = by_core(position_ref[0], low(part))
        gain_ref[...] += jnp.sum(part * wide(tokens_ref[here, :]) * scale_ref[here, :], axis=0, keepdims=True)
    cols = 512
    for at in range(0, normed_ref.shape[1], cols):
        here = slice(at, at + cols)
        weight_ref[here, :split] = low(contract(normed_ref[:, here], low_ref[...], 0, 0))
        weight_ref[here, split:] = low(contract(grad_ref[:, here], mixed_ref[...], 0, 0))


def attend_back(
    group, grad_mine, grad_other, proj, cosine, sine, query_gain, key_gain, segment_row, raw, query, key, value, tokens, scale,
    normed, mixed,
):
    length, model = tokens.shape
    query_cols, kv_cols = query.shape[1], key.shape[1]
    args = (
        grad_mine, grad_other, proj, cosine, sine, query_gain[None], key_gain[None],
        segment_row[:, None], segment_row[None, :], raw, query, key, value, tokens, scale, normed, mixed, position(),
    )
    return pl.pallas_call(
        functools.partial(attend_back_kernel, group),
        in_specs=[pl.BlockSpec(memory_space=pltpu.VMEM)] * (len(args) - 1)
        + [pl.BlockSpec(memory_space=pltpu.SMEM)],
        out_specs=[pl.BlockSpec(memory_space=pltpu.VMEM)] * 5,
        out_shape=[
            jax.ShapeDtypeStruct(proj.shape, jnp.bfloat16),
            jax.ShapeDtypeStruct((length // 2, model), jnp.bfloat16),
            jax.ShapeDtypeStruct((length // 2, model), jnp.bfloat16),
            jax.ShapeDtypeStruct((1, model), jnp.float32),
            jax.ShapeDtypeStruct((2, HD), jnp.float32),
        ],
        scratch_shapes=[
            pltpu.VMEM((length, model), jnp.bfloat16),
            pltpu.VMEM((length, query_cols + 2 * kv_cols), jnp.bfloat16),
            pltpu.VMEM((length, query_cols), jnp.bfloat16),
            pltpu.VMEM((length, query_cols), jnp.float32),
            pltpu.VMEM((length, kv_cols), jnp.float32),
            pltpu.VMEM((length, kv_cols), jnp.float32),
        ],
        compiler_params=call_params(56),
        cost_estimate=cheap(),
        name="attend_back",
    )(*args)


def feed_kernel(own, position_ref, *refs):
    count = 3 if own else 4
    proj_ref = refs[count]
    act_ref, gate_up_grad_ref, keep_ref, give_ref, normed, cotangent = refs[count + 1 :]
    core = position_ref[0]
    half = act_ref.shape[-1]
    middle = normed.shape[0] // 2
    normed[:middle, :], normed[middle:, :] = refs[0][...], refs[1][...]
    if own:
        cotangent[:middle, :], cotangent[middle:, :] = by_core(core, refs[2][...])
    else:
        cotangent[:middle, :], cotangent[middle:, :] = refs[2][...], refs[3][...]
    gate_up = jnp.dot(normed[...], proj_ref[:, : 2 * half], preferred_element_type=jnp.float32)
    gate, up = gate_up[:, :half], gate_up[:, half:]
    act_grad = jnp.dot(cotangent[...], proj_ref[:, 2 * half :], preferred_element_type=jnp.float32)
    sigmoid = jax.nn.sigmoid(gate)
    silu = gate * sigmoid
    activated = low(silu * up)
    gate_grad = low(act_grad * up * sigmoid * (1.0 + gate * (1.0 - sigmoid)))
    up_grad = low(act_grad * silu)
    for k in range(2):
        here = slice(k * middle, (k + 1) * middle)
        act_ref[k] = activated[here]
        gate_up_grad_ref[k, :, :half] = gate_grad[here]
        gate_up_grad_ref[k, :, half:] = up_grad[here]
    normed_grad = contract(gate_grad, proj_ref[:, :half], 1, 1) + contract(
        up_grad, proj_ref[:, half : 2 * half], 1, 1
    )
    keep_ref[...], give_ref[...] = low(normed_grad[:middle]), low(normed_grad[middle:])


def feed(which, mine, other, cotangent, proj):
    _, rows, model = mine.shape
    half = proj.shape[1] // 3
    own = len(cotangent) == 1
    tile = ROWS // 2

    def halves(index):
        return pl.BlockSpec((None, tile, model), lambda i: (index, i, 0))

    return pl.pallas_call(
        functools.partial(feed_kernel, own),
        grid=(rows // tile,),
        in_specs=[pl.BlockSpec(memory_space=pltpu.SMEM), halves(which), halves(which)]
        + ([pl.BlockSpec((ROWS, model), lambda i: (i, 0))] if own else [halves(0), halves(0)])
        + [pl.BlockSpec(proj.shape, lambda i: (0, 0), pipeline_mode=pl.Buffered(1))],
        out_specs=[pl.BlockSpec((2, tile, w), lambda i: (0, i, 0)) for w in (half, 2 * half)]
        + [pl.BlockSpec((tile, model), lambda i: (i, 0))] * 2,
        out_shape=[jax.ShapeDtypeStruct((2, rows, w), jnp.bfloat16) for w in (half, 2 * half)]
        + [jax.ShapeDtypeStruct((rows, model), jnp.bfloat16)] * 2,
        scratch_shapes=[pltpu.VMEM((ROWS, model), jnp.bfloat16)] * 2,
        compiler_params=call_params(48),
        cost_estimate=cheap(),
        name="feed",
    )(position(), mine, other, *cotangent, proj)


def feed_out_kernel(act_ref, proj_ref, keep_ref, give_ref):
    half = act_ref.shape[-1]
    for k, out_ref in enumerate((keep_ref, give_ref)):
        out_ref[...] = low(contract(act_ref[k], proj_ref[:, 2 * half :], 1, 1))


def feed_out(act, proj):
    _, rows, half = act.shape
    model = proj.shape[0]
    tile = ROWS
    return pl.pallas_call(
        feed_out_kernel,
        grid=(rows // tile,),
        in_specs=[
            pl.BlockSpec((2, tile, half), lambda i: (0, i, 0)),
            pl.BlockSpec(proj.shape, lambda i: (0, 0), pipeline_mode=pl.Buffered(1)),
        ],
        out_specs=[pl.BlockSpec((tile, model), lambda i: (i, 0))] * 2,
        out_shape=[jax.ShapeDtypeStruct((rows, model), jnp.bfloat16)] * 2,
        compiler_params=call_params(32),
        cost_estimate=cheap(),
        name="feed_out",
    )(act, proj)


def feed_weights_kernel(
    position_ref, mine_own, mine_pair, other_own, other_pair, cot_own, cot_mine, cot_other, grad_own, grad_pair, act_own, act_pair,
    out_ref,
):
    wide_cols = grad_own.shape[-1]
    core = position_ref[0]
    rows, cols = mine_own.shape
    out_ref[:, :wide_cols] = low(
        contract(mine_own[...], grad_own[0], 0, 0)
        + contract(other_own[...], grad_own[1], 0, 0)
        + contract(mine_pair[...], grad_pair[0], 0, 0)
        + contract(other_pair[...], grad_pair[1], 0, 0)
    )
    out_ref[:, wide_cols:] = low(
        contract(cot_own[:, core].reshape(rows, cols), act_own[0], 0, 0)
        + contract(cot_own[:, 1 - core].reshape(rows, cols), act_own[1], 0, 0)
        + contract(cot_mine[...], act_pair[0], 0, 0)
        + contract(cot_other[...], act_pair[1], 0, 0)
    )


def feed_weights(mine, other, cotangent, cot_mine, cot_other, grad, act):
    _, rows, model = mine.shape
    width = grad[0].shape[-1] + act[0].shape[-1]
    cols = min(512, model)
    cotangent = cotangent.reshape(-1, 2, ROWS // 2, model)

    def whole(array):
        return pl.BlockSpec(array.shape, lambda i: (0, 0, 0), pipeline_mode=pl.Buffered(1))

    def part(index):
        return pl.BlockSpec((None, rows, cols), lambda i: (index, 0, i))

    return pl.pallas_call(
        feed_weights_kernel,
        grid=(model // cols,),
        in_specs=[
            pl.BlockSpec(memory_space=pltpu.SMEM),
            part(0),
            part(1),
            part(0),
            part(1),
            pl.BlockSpec((*cotangent.shape[:3], cols), lambda i: (0, 0, 0, i)),
            part(0),
            part(0),
        ]
        + [whole(a) for a in (*grad, *act)],
        out_specs=pl.BlockSpec((cols, width), lambda i: (i, 0)),
        out_shape=jax.ShapeDtypeStruct((model, width), jnp.bfloat16),
        compiler_params=call_params(48),
        cost_estimate=cheap(),
        name="feed_weights",
    )(position(), mine, mine, other, other, cotangent, cot_mine, cot_other, *grad, *act)


def feed_sums_kernel(count, side_ref, *refs):
    own, other, outs = refs[:count], refs[count:-3], refs[-3:]
    half = outs[0].shape[1]
    mine = pl.program_id(0) == side_ref[0]
    for held, keep in ((own, mine), (other, jnp.logical_not(mine))):

        @pl.when(keep)
        def _():
            first = 0
            for part in held:
                for k, out in enumerate(outs):
                    out[first : first + part.shape[0], :] = wide(part[:, k * half : (k + 1) * half])
                first += part.shape[0]


def feed_sums(side, own, other):
    rows, width = sum(part.shape[0] for part in own), own[0].shape[1]
    half = width // 3
    parts = (*own, *other)
    return pl.pallas_call(
        functools.partial(feed_sums_kernel, len(own)),
        grid_spec=pltpu.PrefetchScalarGridSpec(
            num_scalar_prefetch=1,
            grid=(2,),
            in_specs=[
                pl.BlockSpec(p.shape, lambda i, side: (0, 0), pipeline_mode=pl.Buffered(1)) for p in parts
            ],
            out_specs=[pl.BlockSpec((rows, half), lambda i, side: (0, i))] * 3,
        ),
        out_shape=[jax.ShapeDtypeStruct((rows, 2 * half), jnp.float32)] * 3,
        compiler_params=call_params(32),
        cost_estimate=cheap(),
        name="feed_sums",
    )(side, *parts)


def per_device(
    tokens,
    segments,
    ln1_gain,
    w_query,
    w_key,
    w_value,
    query_gain,
    key_gain,
    w_out,
    ln2_gain,
    w_gate,
    w_up,
    w_down,
    cotangent,
):
    length, model = tokens.shape
    query_cols, key_cols = w_query.shape[1], w_key.shape[1]
    query_heads = query_cols // HD
    kv_local = key_cols // HD
    group = query_heads // kv_local
    size = lax.axis_size("fsdp")
    shard = model // size
    hidden = w_gate.shape[1]
    half = hidden // 2
    strides = bits("fsdp")
    group_size = lax.axis_size(PLANE)
    share_rows = length // group_size
    share_start = lax.axis_index(PLANE) * share_rows
    segment_row = segments[0]

    def share_of(array):
        return lax.dynamic_slice_in_dim(array, share_start, share_rows, 0)

    proj = lax.all_gather(
        jnp.concatenate([w_query, w_key, w_value, w_out], axis=1), "fsdp", axis=0, tiled=True
    )
    side = bit("fsdp", 1)

    def half_of(which):
        return jnp.concatenate(
            [lax.dynamic_slice_in_dim(w, which * half, half, 1) for w in (w_gate, w_up, w_down)], axis=1
        )

    got = swap(after(half_of(1 - side), proj), "fsdp", 1)
    feed_block = both(half_of(side), got, side, 0)

    gains = line_gather(jnp.concatenate([ln1_gain, ln2_gain, query_gain, key_gain]), strides)
    gain_attn = gains[:, :shard].reshape(model)
    gain_ffn = gains[:, shard : 2 * shard].reshape(model)
    head_part = HD // size
    query_norm = gains[:, 2 * shard : 2 * shard + head_part].reshape(HD)
    key_norm = gains[:, 2 * shard + head_part :].reshape(HD)

    cosine, sine = rope_tables(doc_positions(segment_row))
    block_in = tokens.astype(jnp.float32)
    scale_one = rms_parts(block_in)
    normed = (block_in * scale_one * gain_attn.astype(jnp.float32)).astype(jnp.bfloat16)
    query_gain_wide, key_gain_wide = wide(query_norm), wide(key_norm)
    raw, query_rot, key_rot, values, mixed_low, out_keep, out_give = attend(
        group, normed, proj, cosine, sine, query_gain_wide, key_gain_wide, segment_row
    )
    out_give, feed_block = lax.optimization_barrier((out_give, feed_block))
    feed_proj = lax.all_gather(
        feed_block, "fsdp", axis=0, tiled=True, axis_index_groups=alike()
    ).reshape(model, -1)

    def middle(out_keep, out_give, tokens, cotangent):
        cot = Job(pair_gather(share_of(cotangent), 2))
        out_sum = Job(plane_scatter(out_keep, out_give))
        beside(out_sum)
        beside(out_sum, cot)
        beside(out_sum, cot)
        hidden_share = wide(share_of(tokens)) + out_sum.value
        scale_share = rms_parts(hidden_share)
        normed_share = low(hidden_share * scale_share * wide(gain_ffn))
        pair_share = Job(pair_swap(normed_share))
        beside(pair_share, cot)
        gather = Job(plane_gather(jnp.stack([normed_share, pair_share.value])))
        beside(gather, cot)
        beside(gather, cot)
        finish(gather)
        return hidden_share, scale_share, *gather.value, *cot.value

    hidden_share, scale_share, mine, other, cot_mine, cot_other = apart(
        middle, out_keep, out_give, tokens, cotangent
    )

    pair_act, pair_grad, *pair_parts = feed(1, mine, other, (cot_mine, cot_other), feed_proj)
    pair_sum = Job(plane_scatter(*pair_parts))
    ((act, grad, *own_parts),) = beside(
        pair_sum, kernels=[(functools.partial(feed, 0), (mine, other, (cotangent,), feed_proj))]
    )
    own_sum = Job(plane_scatter(*own_parts))
    weight_args = (mine, other, cotangent, cot_mine, cot_other, (grad, pair_grad), (act, pair_act))
    (feed_w_part,) = beside(pair_sum, own_sum, kernels=[(feed_weights, weight_args)])
    feed_w_sum = lax.psum_scatter(
        feed_w_part, "fsdp", scatter_dimension=0, tiled=True, axis_index_groups=alike()
    ).reshape(2, shard, -1)
    pair_held, own_held = (tuple(job.keep) for job in (pair_sum, own_sum))

    def back(hidden_share, scale_share, cotangent, act, pair_act, feed_proj, *kept):
        pair_sum = Job(line_scatter(*pair_held))
        own_sum = Job(chip_scatter(*own_held))
        out_parts, pair_out_parts = beside(
            pair_sum, own_sum, kernels=[(feed_out, (act, feed_proj)), (feed_out, (pair_act, feed_proj))]
        )
        out_sum = Job(plane_scatter(*out_parts))
        pair_out_sum = Job(plane_scatter(*pair_out_parts))
        pair_share = Job(pair_swap(low(pair_sum.value), 2))
        beside(pair_share, own_sum, pair_out_sum, out_sum)
        beside(pair_share, pair_out_sum)
        grad_share = own_sum.value + wide(pair_share.value)
        hidden_grad_share = wide(share_of(cotangent)) + norm_back(
            hidden_share, scale_share, grad_share * wide(gain_ffn)
        )
        ffn_gain_part = jnp.sum(grad_share * hidden_share * scale_share, axis=0)
        gather = Job(plane_gather(low(hidden_grad_share)[None]))
        beside(gather)
        beside(gather)
        beside(gather, pair_out_sum)
        pair_out = Job(pair_swap(low(pair_out_sum.value)))
        grad_mine, grad_other = gather.value
        ((attn_w_part, keep, give, attn_gain_part, head_gain_part),) = beside(
            pair_out,
            out_sum,
            kernels=[(functools.partial(attend_back, group), (grad_mine[0], grad_other[0], *kept))],
        )
        out_share = hidden_share + wide(pair_out.value)
        return (
            hidden_grad_share, attn_w_part, keep, give, attn_gain_part, head_gain_part, ffn_gain_part, out_share,
            *out_sum.keep,
        )

    hidden_grad_share, attn_w_part, keep, give, attn_gain_part, head_gain_part, ffn_gain_part, out_share, *held = apart(
        back, hidden_share, scale_share, cotangent, act, pair_act, feed_proj,
        proj, cosine, sine, query_gain_wide, key_gain_wide, segment_row, raw, query_rot, key_rot, values, tokens,
        scale_one, normed, mixed_low,
    )
    attn_w_part, feed_w_sum, give = lax.optimization_barrier((attn_w_part, feed_w_sum, give))
    attn_w_sum = lax.psum_scatter(attn_w_part, "fsdp", scatter_dimension=0, tiled=True)

    def last(feed_w_sum, keep, give, out_share, hidden_grad_share, tokens, scale_one, *rest):
        gain_parts, held = rest[:4], rest[4:]
        out_sum = Job(line_scatter(*held))
        feed_pair = Job(pair_swap(pick(feed_w_sum, 1 - side, 0), 4))
        normed_sum = Job(plane_scatter(keep, give))
        gains = Job(sum_all(jnp.concatenate([part.reshape(size, -1) for part in gain_parts], axis=1)))
        beside(normed_sum, out_sum, gains)
        beside(normed_sum, feed_pair, gains)
        beside(normed_sum, feed_pair, gains)
        finish(feed_pair, gains)
        gate_w_grad, up_w_grad, down_w_grad = feed_sums(side[None], [pick(feed_w_sum, side, 0)], [feed_pair.value])
        block_out = low(out_share + out_sum.value)
        token_share = wide(share_of(tokens))
        scale_one_share = share_of(scale_one)
        tokens_grad = low(
            hidden_grad_share + norm_back(token_share, scale_one_share, normed_sum.value * wide(gain_attn))
        )
        gain_sums = pick(gains.value, lax.axis_index("fsdp"), 0)
        return block_out, tokens_grad, gate_w_grad, up_w_grad, down_w_grad, gain_sums

    block_out, tokens_grad, gate_w_grad, up_w_grad, down_w_grad, gain_sums = apart(
        last, feed_w_sum, keep, give, out_share, hidden_grad_share, tokens, scale_one,
        attn_gain_part, ffn_gain_part, head_gain_part[0], head_gain_part[1], *held,
    )
    attn_w_grad, gain_sums = lax.optimization_barrier((attn_w_sum, gain_sums))
    attn_w_grad = wide(attn_w_grad)
    out_w_grad = attn_w_grad[:, query_cols + 2 * key_cols :]
    ln1_grad = gain_sums[:shard]
    ln2_grad = gain_sums[shard : 2 * shard]
    query_gain_grad = gain_sums[2 * shard : 2 * shard + head_part]
    key_gain_grad = gain_sums[2 * shard + head_part :]

    return (
        block_out,
        tokens_grad,
        ln1_grad,
        attn_w_grad[:, :query_cols],
        attn_w_grad[:, query_cols : query_cols + key_cols],
        attn_w_grad[:, query_cols + key_cols : query_cols + 2 * key_cols],
        query_gain_grad,
        key_gain_grad,
        out_w_grad,
        ln2_grad,
        gate_w_grad,
        up_w_grad,
        down_w_grad,
    )


def solution(mesh):
    in_specs = (
        P("fsdp", None),
        P("fsdp", None),
        P("fsdp"),
        P("fsdp", ("heads", "tensor")),
        P("fsdp", ("heads", "tensor")),
        P("fsdp", ("heads", "tensor")),
        P("fsdp"),
        P("fsdp"),
        P("fsdp", ("heads", "tensor")),
        P("fsdp"),
        P("fsdp", ("heads", "tensor")),
        P("fsdp", ("heads", "tensor")),
        P("fsdp", ("heads", "tensor")),
        P("fsdp", None),
    )
    out_specs = (
        P(("fsdp", "heads", "tensor"), None),
        P(("fsdp", "heads", "tensor"), None),
        P("fsdp"),
        P("fsdp", ("heads", "tensor")),
        P("fsdp", ("heads", "tensor")),
        P("fsdp", ("heads", "tensor")),
        P("fsdp"),
        P("fsdp"),
        P("fsdp", ("heads", "tensor")),
        P("fsdp"),
        P("fsdp", ("heads", "tensor")),
        P("fsdp", ("heads", "tensor")),
        P("fsdp", ("heads", "tensor")),
    )
    return jax.shard_map(
        per_device, mesh=mesh, in_specs=in_specs, out_specs=out_specs, check_vma=False
    )
```

```python
import functools

import jax
import jax.numpy as jnp
from jax import lax
from jax.experimental import pallas as pl
from jax.experimental.pallas import tpu as pltpu
from jax.sharding import PartitionSpec as P

HD = 128


EPSILON = 1e-06
THETA = 1000000.0
ROWS = 256
BAND = 512
PLANE = ("heads", "tensor")
SWAP = ((0, 1), (1, 0))
NEAR = ((0, 1), (1, 0), (2, 3), (3, 2))
FAR = ((0, 2), (2, 0), (1, 3), (3, 1))


def rms_parts(values):
    return lax.rsqrt(jnp.mean(values * values, axis=-1, keepdims=True) + EPSILON)


def norm_back(values, scale, upstream):
    return scale * upstream - values * scale**3 * jnp.mean(
        values * upstream, axis=-1, keepdims=True
    )


def contract(left, right, left_dim, right_dim):
    return lax.dot_general(
        left, right, (((left_dim,), (right_dim,)), ((), ())), preferred_element_type=jnp.float32
    )


def doc_positions(segment_row):
    places = jnp.arange(segment_row.shape[0], dtype=jnp.int32)
    previous = jnp.concatenate([segment_row[:1], segment_row[:-1]])
    starts = lax.cummax(jnp.where(segment_row != previous, places, 0), axis=0)
    return places - starts


def rope_tables(positions):
    frequency = THETA ** (-(jnp.arange(HD // 2, dtype=jnp.float32) * 2.0 / HD))
    angles = positions.astype(jnp.float32)[:, None] * frequency[None, :]
    cosine, sine = jnp.cos(angles), jnp.sin(angles)
    return (
        jnp.concatenate([cosine, cosine], axis=1),
        jnp.concatenate([-sine, sine], axis=1),
    )


def low(values):
    return values.astype(jnp.bfloat16)


def wide(values):
    return values.astype(jnp.float32)


def flip(axis, stride):
    return [(k, k ^ stride) for k in range(lax.axis_size(axis))]


def after(value, *others):
    return lax.optimization_barrier((value, *others))[0]


def apart(work, *args):
    zeros = [jnp.zeros(out.shape, out.dtype) for out in jax.eval_shape(work, *args)]
    return lax.cond(
        lax.axis_index("fsdp") < lax.axis_size("fsdp"), work, lambda *_: tuple(zeros), *args
    )


class Job:
    def __init__(self, steps):
        self.steps, self.moves, self.keep, self.held, self.value = steps, (), (), (), None
        self.resume(None)

    def resume(self, got):
        self.held, self.arrived = self.keep, got
        try:
            given = self.steps.send(got)
            self.moves, self.keep = given if isinstance(given, tuple) else (given, ())
        except StopIteration as end:
            self.moves, self.keep, self.value = (), (), end.value


def beside(*jobs, kernels=(), ready=()):
    jobs = [job for job in jobs if job.moves]
    ready = [job for job in ready if job.moves]
    given = [[move[0] for move in job.moves] for job in jobs], [args for _, args in kernels]
    arrays, args = lax.optimization_barrier(given)
    got = [
        [lax.ppermute(array, *move[1:]) for array, move in zip(held, job.moves)]
        for held, job in zip(arrays, jobs)
    ]
    results = [kernel[0](*own) for own, kernel in zip(args, kernels)]
    later = [[move[0] for move in job.moves] for job in ready]
    got, results, later = lax.optimization_barrier((got, results, later))
    for job, arrays in zip(ready, later):
        job.moves = [(array, *move[1:]) for array, move in zip(arrays, job.moves)]
    for job, arrived in zip(jobs, got):
        job.resume(arrived)
    return results


def finish(*jobs):
    while any(job.moves for job in jobs):
        beside(*jobs)


def bits(axis):
    size = lax.axis_size(axis)
    return [1 << k for k in range(size.bit_length() - 1)]


def swap(array, axis, stride):
    return lax.ppermute(array, axis, flip(axis, stride))


def bit(axis, stride):
    return (lax.axis_index(axis) // stride) % 2


def line_gather(block, strides):
    block = block[None]
    for stride in strides:
        block = both(block, swap(block, "fsdp", stride), bit("fsdp", stride), 0)
        block = block.reshape(-1, *block.shape[2:])
    return block


def pick(array, index, axis):
    return lax.dynamic_index_in_dim(array, index, axis, keepdims=False)


def both(mine, got, index, axis):
    lower = jnp.where(index == 0, mine, got)
    upper = jnp.where(index == 0, got, mine)
    return jnp.stack([lower, upper], axis=axis)


def position():
    heads = lax.axis_index("heads")
    return jnp.stack([lax.axis_index("tensor"), heads % 2, heads // 2]).astype(jnp.int32)


def vmem_call(kernel, name, megabytes, out_shape, *args):
    return pl.pallas_call(
        kernel,
        in_specs=[pl.BlockSpec(memory_space=pltpu.SMEM)]
        + [pl.BlockSpec(memory_space=pltpu.VMEM)] * len(args),
        out_specs=[pl.BlockSpec(memory_space=pltpu.VMEM)] * len(out_shape),
        out_shape=[jax.ShapeDtypeStruct(shape, jnp.bfloat16) for shape in out_shape],
        compiler_params=call_params(megabytes),
        cost_estimate=cheap(),
        name=name,
    )(position(), *args)


def fold_chip_kernel(position_ref, keep_ref, got_ref, give_first, keep_first, give_second, keep_second):
    x, y = position_ref[1], position_ref[2]
    middle = keep_ref.shape[-1] // 2
    first, second = slice(0, middle), slice(middle, 2 * middle)

    def summed(row, column, cols):
        return low(wide(keep_ref[row, column, :, cols]) + wide(got_ref[row, column, :, cols]))

    for k in range(2):
        give_first[k] = summed(k, 1 - x, first)
        keep_first[k] = summed(k, x, first)
        give_second[k] = summed(1 - y, k, second)
        keep_second[k] = summed(y, k, second)


def fold_chip(keep, got):
    rows, width = keep.shape
    shape = (2, 2, rows // 4, width)
    return vmem_call(
        fold_chip_kernel, "fold_chip", 24, [(2, rows // 4, width // 2)] * 4, keep.reshape(shape), got.reshape(shape)
    )


def fold_line_kernel(
    position_ref, keep_first_ref, got_first_ref, keep_second_ref, got_second_ref, give_first, keep_first, give_second, keep_second
):
    x, y = position_ref[1], position_ref[2]
    for at, keep_ref, got_ref, give, keep in (
        (y, keep_first_ref, got_first_ref, give_first, keep_first),
        (x, keep_second_ref, got_second_ref, give_second, keep_second),
    ):
        give[...] = low(wide(keep_ref[1 - at]) + wide(got_ref[1 - at]))
        keep[...] = low(wide(keep_ref[at]) + wide(got_ref[at]))


def fold_line(keep_first, got_first, keep_second, got_second):
    shape = keep_first.shape[1:]
    return vmem_call(
        fold_line_kernel, "fold_line", 16, [shape] * 4, keep_first, got_first, keep_second, got_second
    )


def fold_end_kernel(position_ref, keep_first_ref, got_first_ref, keep_second_ref, got_second_ref, out_ref):
    middle = keep_first_ref.shape[-1]
    out_ref[:, :middle] = low(wide(keep_first_ref[...]) + wide(got_first_ref[...]))
    out_ref[:, middle:] = low(wide(keep_second_ref[...]) + wide(got_second_ref[...]))


def fold_end(keep_first, got_first, keep_second, got_second):
    rows, width = keep_first.shape
    (out,) = vmem_call(
        fold_end_kernel, "fold_end", 16, [(rows, 2 * width)], keep_first, got_first, keep_second, got_second
    )
    return out


def plane_scatter(keep, give, rounded=False):
    (got,) = yield [(give, "tensor", SWAP)]
    folded = fold_chip(keep, got)
    return (yield from chip_scatter(*folded, rounded))


def chip_scatter(give_first, keep_first, give_second, keep_second, rounded=False):
    held = (give_first, keep_first, give_second, keep_second)
    got = yield [(give_first, "heads", NEAR), (give_second, "heads", FAR)], held
    return (yield from line_scatter(*fold_line(keep_first, got[0], keep_second, got[1]), rounded))


def line_scatter(give_first, keep_first, give_second, keep_second, rounded=False):
    held = (give_first, keep_first, give_second, keep_second)
    got = yield [(give_first, "heads", FAR), (give_second, "heads", NEAR)], held
    if rounded:
        return fold_end(keep_first, got[0], keep_second, got[1])
    first = wide(keep_first) + wide(got[0])
    second = wide(keep_second) + wide(got[1])
    return jnp.concatenate([first, second], axis=-1)


def open_line_kernel(position_ref, first_ref, got_first_ref, second_ref, got_second_ref, first, second):
    x, y = position_ref[1], position_ref[2]
    first[y] = first_ref[...]
    first[1 - y] = got_first_ref[...]
    second[x] = second_ref[...]
    second[1 - x] = got_second_ref[...]


def open_chip_kernel(position_ref, first_ref, got_first_ref, second_ref, got_second_ref, out_ref):
    x, y = position_ref[1], position_ref[2]
    lead, middle = first_ref.shape[1], first_ref.shape[-1]
    for k in range(lead):
        for j in range(2):
            out_ref[k, j, x, :, :middle] = first_ref[j, k]
            out_ref[k, j, 1 - x, :, :middle] = got_first_ref[j, k]
            out_ref[k, y, j, :, middle:] = second_ref[j, k]
            out_ref[k, 1 - y, j, :, middle:] = got_second_ref[j, k]


def plane_gather(share):
    lead, rows, width = share.shape
    first, second = share[..., : width // 2], share[..., width // 2 :]
    got = yield [(first, "heads", FAR), (second, "heads", NEAR)]
    first, second = vmem_call(
        open_line_kernel, "open_line", 16, [(2, lead, rows, width // 2)] * 2, first, got[0], second, got[1]
    )
    got = yield [(first, "heads", NEAR), (second, "heads", FAR)]
    (mine,) = vmem_call(
        open_chip_kernel, "open_chip", 24, [(lead, 2, 2, rows, width)], first, got[0], second, got[1]
    )
    mine = mine.reshape(lead, 4 * rows, width)
    (other,) = yield [(mine, "tensor", SWAP)]
    return mine, other


def pair_swap(array, pieces=1):
    rows = array.shape[0] // pieces
    got = []
    for k in range(pieces):
        got += yield [(array[k * rows : (k + 1) * rows], "fsdp", flip("fsdp", 1))]
    return jnp.concatenate(got, axis=0) if pieces > 1 else got[0]


def pair_gather(share, pieces):
    got = yield from pair_swap(share, pieces)
    return (yield from plane_gather(got[None]))


def sum_all(values):
    for axis in ("fsdp", "tensor", "heads"):
        for stride in bits(axis):
            (got,) = yield [(values, axis, flip(axis, stride))]
            values = values + got
    return values


def alike():
    return [list(range(k, lax.axis_size("fsdp"), 2)) for k in range(2)]


def rotate(values, cosine, sine):
    return values * cosine + pltpu.roll(values, HD // 2, 1) * sine


def call_params(megabytes):
    return pltpu.CompilerParams(vmem_limit_bytes=megabytes << 20)


def cheap():
    return pl.CostEstimate(flops=1000, bytes_accessed=1000, transcendentals=0)


def key_blocks(at, count):
    return max(0, at - BAND // ROWS), at + 1


def masked_probs(query, keys, seg_rows, seg_keys, first_row, first_key):
    scores = contract(query, keys, 1, 1) * HD**-0.5
    rows = first_row + lax.broadcasted_iota(jnp.int32, scores.shape, 0)
    cols = first_key + lax.broadcasted_iota(jnp.int32, scores.shape, 1)
    scores = jnp.where((rows >= cols) & (seg_rows == seg_keys), scores, -1e30)
    expo = jnp.exp(scores - jnp.max(scores, axis=-1, keepdims=True))
    return expo / jnp.sum(expo, axis=-1, keepdims=True)


def by_core(core, block):
    middle = block.shape[0] // 2
    lower, upper = block[:middle], block[middle:]
    first = core == 0
    return jnp.where(first, lower, upper), jnp.where(first, upper, lower)


def joined(core, mine, other):
    first = core == 0
    return jnp.concatenate([jnp.where(first, mine, other), jnp.where(first, other, mine)], axis=0)


def attend_kernel(
    group,
    normed_ref,
    proj_ref,
    cosine_ref,
    sine_ref,
    query_gain_ref,
    key_gain_ref,
    seg_rows_ref,
    seg_keys_ref,
    raw_ref,
    query_ref,
    key_ref,
    value_ref,
    mixed_ref,
    keys,
    values,
):
    length, kv_cols = keys.shape
    kv_local = kv_cols // HD
    query_cols = kv_cols * group
    count = length // ROWS
    step = pl.program_id(0)
    raw = jnp.dot(normed_ref[...], proj_ref[...], preferred_element_type=jnp.float32)
    raw_ref[...] = raw[:, : query_cols + kv_cols]
    cosine, sine = cosine_ref[...], sine_ref[...]
    here = pl.ds(pl.multiple_of(step * ROWS, ROWS), ROWS)

    def turned(head, gain_ref):
        one = raw[:, head * HD : (head + 1) * HD]
        return low(rotate(one * rms_parts(one) * gain_ref[...], cosine, sine))

    for kv in range(kv_local):
        at = slice(kv * HD, (kv + 1) * HD)
        new_keys = turned(query_cols // HD + kv, key_gain_ref)
        new_values = low(raw[:, query_cols + kv_cols + kv * HD : query_cols + kv_cols + (kv + 1) * HD])
        key_ref[:, at] = new_keys
        value_ref[:, at] = new_values
        keys[here, at] = new_keys
        values[here, at] = new_values
    for head in range(query_cols // HD):
        query_ref[:, head * HD : (head + 1) * HD] = turned(head, query_gain_ref)

    for at in range(count):

        @pl.when(step == at)
        def _():
            lower, upper = key_blocks(at, count)
            span = slice(lower * ROWS, upper * ROWS)
            for head in range(query_cols // HD):
                cols = slice(head * HD, (head + 1) * HD)
                kv = slice((head // group) * HD, (head // group + 1) * HD)
                probs = masked_probs(
                    query_ref[:, cols],
                    keys[span, kv],
                    seg_rows_ref[...],
                    seg_keys_ref[:, span],
                    at * ROWS,
                    lower * ROWS,
                )
                mixed_ref[:, cols] = low(
                    jnp.dot(low(probs), values[span, kv], preferred_element_type=jnp.float32)
                )


def attend(group, normed, proj, cosine, sine, query_gain, key_gain, seg_rows, segment_row):
    length, model = normed.shape
    kv_cols = proj.shape[1] // (2 * group + 2)
    query_cols = kv_cols * group

    def rows(width):
        return pl.BlockSpec((ROWS, width), lambda i: (i, 0))

    def whole(array):
        return pl.BlockSpec(array.shape, lambda i: (0, 0))

    seg_keys = segment_row[None, :]
    args = (normed, proj, cosine, sine, query_gain[None], key_gain[None], seg_rows, seg_keys)
    outs = [
        (query_cols + kv_cols, jnp.float32),
        (query_cols, jnp.bfloat16),
        (kv_cols, jnp.bfloat16),
        (kv_cols, jnp.bfloat16),
        (query_cols, jnp.bfloat16),
    ]
    return pl.pallas_call(
        functools.partial(attend_kernel, group),
        grid=(length // ROWS,),
        in_specs=[
            rows(model),
            pl.BlockSpec((model, query_cols + 2 * kv_cols), lambda i: (0, 0)),
            rows(HD),
            rows(HD),
            whole(args[4]),
            whole(args[5]),
            rows(1),
            whole(seg_keys),
        ],
        out_specs=[rows(width) for width, _ in outs],
        out_shape=[jax.ShapeDtypeStruct((length, width), kind) for width, kind in outs],
        scratch_shapes=[
            pltpu.VMEM((length, kv_cols), jnp.bfloat16),
            pltpu.VMEM((length, kv_cols), jnp.bfloat16),
        ],
        compiler_params=call_params(40),
        cost_estimate=cheap(),
        name="attend",
    )(*args)


def attend_out_kernel(position_ref, mixed_ref, proj_ref, keep_ref, give_ref):
    keep_ref[...], give_ref[...] = by_core(
        position_ref[0], low(contract(mixed_ref[...], proj_ref[...], 1, 1))
    )


def attend_out(mixed, proj):
    length, cols = mixed.shape
    model = proj.shape[0]
    return pl.pallas_call(
        attend_out_kernel,
        grid=(length // ROWS,),
        in_specs=[
            pl.BlockSpec(memory_space=pltpu.SMEM),
            pl.BlockSpec((ROWS, cols), lambda i: (i, 0)),
            pl.BlockSpec((model, cols), lambda i: (0, proj.shape[1] // cols - 1)),
        ],
        out_specs=[pl.BlockSpec((ROWS // 2, model), lambda i: (i, 0))] * 2,
        out_shape=[jax.ShapeDtypeStruct((length // 2, model), jnp.bfloat16)] * 2,
        compiler_params=call_params(24),
        cost_estimate=cheap(),
        name="attend_out",
    )(position(), mixed, proj)


def attend_back_kernel(
    group,
    grad_mine_ref,
    grad_other_ref,
    out_proj_ref,
    cosine_ref,
    sine_ref,
    query_gain_ref,
    key_gain_ref,
    seg_rows_ref,
    seg_keys_ref,
    raw_ref,
    query_ref,
    key_ref,
    value_ref,
    mixed_ref,
    position_ref,
    low_ref,
    mixed_split_ref,
    head_gain_ref,
    mixed_grad,
    query_sum,
    key_sum,
    value_sum,
):
    length, kv_cols = key_sum.shape
    query_cols = kv_cols * group
    count = length // ROWS
    share = ROWS // 2
    core = position_ref[0]
    for k, ref in enumerate((grad_mine_ref, grad_other_ref)):
        part = low(jnp.dot(ref[...], out_proj_ref[...], preferred_element_type=jnp.float32))
        for at in range(count):
            start = pl.multiple_of(at * ROWS + (core + k - 2 * k * core) * share, share)
            mixed_grad[pl.ds(start, share), :] = part[at * share : (at + 1) * share]
            mixed_split_ref[k, at * share : (at + 1) * share, :] = mixed_ref[pl.ds(start, share), :]
    key_sum[...] = jnp.zeros_like(key_sum)
    value_sum[...] = jnp.zeros_like(value_sum)
    for at in range(count):
        here = slice(at * ROWS, (at + 1) * ROWS)
        lower, upper = key_blocks(at, count)
        span = slice(lower * ROWS, upper * ROWS)
        for head in range(query_cols // HD):
            cols = slice(head * HD, (head + 1) * HD)
            kv = slice((head // group) * HD, (head // group + 1) * HD)
            query = query_ref[here, cols]
            grad = mixed_grad[here, cols]
            probs = masked_probs(
                query,
                key_ref[span, kv],
                seg_rows_ref[here, :],
                seg_keys_ref[:, span],
                at * ROWS,
                lower * ROWS,
            )
            prob_grad = contract(grad, value_ref[span, kv], 1, 1)
            row_inner = jnp.sum(probs * prob_grad, axis=-1, keepdims=True)
            score_grad = low(HD**-0.5 * probs * (prob_grad - row_inner))
            query_sum[here, cols] = jnp.dot(
                score_grad, key_ref[span, kv], preferred_element_type=jnp.float32
            )
            key_sum[span, kv] += contract(score_grad, query, 0, 0)
            value_sum[span, kv] += contract(low(probs), grad, 0, 0)

    head_gain_ref[...] = jnp.zeros_like(head_gain_ref)
    for at in range(count):
        here = slice(at * ROWS, (at + 1) * ROWS)
        cosine, sine = cosine_ref[here, :], -sine_ref[here, :]
        for head in range((query_cols + kv_cols) // HD):
            cols = slice(head * HD, (head + 1) * HD)
            own = slice(head * HD - query_cols, (head + 1) * HD - query_cols)
            is_query = head * HD < query_cols
            turned = rotate(query_sum[here, cols] if is_query else key_sum[here, own], cosine, sine)
            raw = raw_ref[here, cols]
            scale = rms_parts(raw)
            row = 0 if is_query else 1
            head_gain_ref[row : row + 1, :] += jnp.sum(turned * raw * scale, axis=0, keepdims=True)
            gain = query_gain_ref[...] if is_query else key_gain_ref[...]
            low_ref[here, cols] = low(norm_back(raw, scale, turned * gain))
        low_ref[here, query_cols + kv_cols :] = low(value_sum[here, :])


def attend_back(
    group, grad_mine, grad_other, proj, cosine, sine, query_gain, key_gain, seg_rows, segment_row, raw, query, key, value, mixed
):
    length, query_cols, kv_cols = query.shape[0], query.shape[1], key.shape[1]
    args = (
        grad_mine, grad_other, proj, cosine, sine, query_gain[None], key_gain[None],
        seg_rows, segment_row[None, :], raw, query, key, value, mixed, position(),
    )
    out_shape = [
        jax.ShapeDtypeStruct((length, query_cols + 2 * kv_cols), jnp.bfloat16),
        jax.ShapeDtypeStruct((2, length // 2, query_cols), jnp.bfloat16),
        jax.ShapeDtypeStruct((2, HD), jnp.float32),
    ]

    def whole(array):
        return pl.BlockSpec(array.shape, lambda i: (0,) * len(array.shape), pipeline_mode=pl.Buffered(1))

    return pl.pallas_call(
        functools.partial(attend_back_kernel, group),
        grid=(1,),
        in_specs=[whole(grad_mine), whole(grad_other)]
        + [pl.BlockSpec((proj.shape[0], query_cols), lambda i: (0, proj.shape[1] // query_cols - 1))]
        + [whole(array) for array in args[3:-1]]
        + [pl.BlockSpec(memory_space=pltpu.SMEM)],
        out_specs=[whole(out) for out in out_shape],
        out_shape=out_shape,
        scratch_shapes=[
            pltpu.VMEM((length, query_cols), jnp.bfloat16),
            pltpu.VMEM((length, query_cols), jnp.float32),
            pltpu.VMEM((length, kv_cols), jnp.float32),
            pltpu.VMEM((length, kv_cols), jnp.float32),
        ],
        compiler_params=call_params(40),
        cost_estimate=cheap(),
        name="attend_back",
    )(*args)


def attend_weights_kernel(
    position_ref, low_ref, mixed_ref, scale_ref, grad_mine_ref, grad_other_ref, proj_ref, tokens_ref, normed_ref,
    weight_ref, keep_ref, give_ref, gain_ref,
):
    split = low_ref.shape[1]
    share = ROWS // 2
    gain = jnp.zeros_like(gain_ref)
    for at in range(low_ref.shape[0] // ROWS):
        here = slice(at * ROWS, (at + 1) * ROWS)
        rows = slice(at * share, (at + 1) * share)
        part = contract(low_ref[here, :], proj_ref[...], 1, 1)
        keep_ref[rows, :], give_ref[rows, :] = by_core(position_ref[0], low(part))
        gain += jnp.sum(part * wide(tokens_ref[here, :]) * scale_ref[here, :], axis=0, keepdims=True)
    gain_ref[...] = gain
    weight_ref[:, :split] = low(contract(normed_ref[...], low_ref[...], 0, 0))
    weight_ref[:, split:] = low(
        contract(grad_mine_ref[...], mixed_ref[0], 0, 0) + contract(grad_other_ref[...], mixed_ref[1], 0, 0)
    )


def attend_weights(low_grad, mixed, scale, grad_mine, grad_other, proj, tokens, normed):
    length, model = tokens.shape
    split = low_grad.shape[1]
    width = split + mixed.shape[-1]
    cols = min(512, model)

    def whole(array):
        return pl.BlockSpec(array.shape, lambda i: (0,) * array.ndim, pipeline_mode=pl.Buffered(1))

    def columns(rows):
        return pl.BlockSpec((rows, cols), lambda i: (0, i))

    return pl.pallas_call(
        attend_weights_kernel,
        grid=(model // cols,),
        in_specs=[
            pl.BlockSpec(memory_space=pltpu.SMEM),
            whole(low_grad),
            whole(mixed),
            whole(scale),
            columns(length // 2),
            columns(length // 2),
            pl.BlockSpec((cols, split), lambda i: (i, 0)),
            columns(length),
            columns(length),
        ],
        out_specs=[
            pl.BlockSpec((cols, width), lambda i: (i, 0)),
            columns(length // 2),
            columns(length // 2),
            columns(1),
        ],
        out_shape=[
            jax.ShapeDtypeStruct((model, width), jnp.bfloat16),
            jax.ShapeDtypeStruct((length // 2, model), jnp.bfloat16),
            jax.ShapeDtypeStruct((length // 2, model), jnp.bfloat16),
            jax.ShapeDtypeStruct((1, model), jnp.float32),
        ],
        compiler_params=call_params(40),
        cost_estimate=cheap(),
        name="attend_weights",
    )(position(), low_grad, mixed, scale, grad_mine, grad_other, proj, tokens, normed)


def prepare_kernel(tokens_ref, gain_ref, seg_ref, normed_ref, scale_ref, seg_rows_ref):
    block_in = wide(tokens_ref[...])
    scale = rms_parts(block_in)
    scale_ref[...] = scale
    normed_ref[...] = low(block_in * scale * gain_ref[...])
    seg_rows_ref[...] = seg_ref[...]


def prepare(tokens, gain, seg_rows):
    length, model = tokens.shape

    def rows(width):
        return pl.BlockSpec((ROWS, width), lambda i: (i, 0))

    return pl.pallas_call(
        prepare_kernel,
        grid=(length // ROWS,),
        in_specs=[rows(model), pl.BlockSpec((1, model), lambda i: (0, 0)), rows(1)],
        out_specs=[rows(model), rows(1), rows(1)],
        out_shape=[
            jax.ShapeDtypeStruct((length, model), jnp.bfloat16),
            jax.ShapeDtypeStruct((length, 1), jnp.float32),
            jax.ShapeDtypeStruct((length, 1), jnp.int32),
        ],
        compiler_params=call_params(24),
        cost_estimate=cheap(),
        name="prepare",
    )(tokens, gain[None], seg_rows)


def feed_kernel(*refs):
    normed, cotangent, proj_ref, (act_refs, grad_refs) = refs[:4], refs[4:8], refs[8], (refs[9:11], refs[11:])
    half = act_refs[0].shape[-1]
    for k in range(4):
        act_ref, grad_ref = act_refs[k // 2], grad_refs[k // 2]
        gate_up = jnp.dot(normed[k][...], proj_ref[:, : 2 * half], preferred_element_type=jnp.float32)
        gate, up = gate_up[:, :half], gate_up[:, half:]
        act_grad = jnp.dot(cotangent[k][...], proj_ref[:, 2 * half :], preferred_element_type=jnp.float32)
        sigmoid = jax.nn.sigmoid(gate)
        silu = gate * sigmoid
        act_ref[k % 2] = low(silu * up)
        grad_ref[k % 2, :, :half] = low(act_grad * up * sigmoid * (1.0 + gate * (1.0 - sigmoid)))
        grad_ref[k % 2, :, half:] = low(act_grad * silu)


def feed(normed, cotangent, proj):
    rows, model = normed[0].shape
    half = proj.shape[1] // 3
    tile = min(256, rows)
    block = pl.BlockSpec((tile, model), lambda i: (i, 0))
    widths = (half, half, 2 * half, 2 * half)
    return pl.pallas_call(
        feed_kernel,
        grid=(rows // tile,),
        in_specs=[block] * 8 + [pl.BlockSpec(proj.shape, lambda i: (0, 0), pipeline_mode=pl.Buffered(1))],
        out_specs=[pl.BlockSpec((2, tile, w), lambda i: (0, i, 0)) for w in widths],
        out_shape=[jax.ShapeDtypeStruct((2, rows, w), jnp.bfloat16) for w in widths],
        compiler_params=call_params(48),
        cost_estimate=cheap(),
        name="feed",
    )(*normed, *cotangent, proj)


def feed_model_kernel(act_ref, grad_ref, proj_ref, keep_ref, give_ref, keep_out_ref, give_out_ref):
    half = act_ref.shape[-1]
    for k, (out_ref, out_out_ref) in enumerate(((keep_ref, keep_out_ref), (give_ref, give_out_ref))):
        out_ref[...] = low(contract(grad_ref[k], proj_ref[:, : 2 * half], 1, 1))
        out_out_ref[...] = low(contract(act_ref[k], proj_ref[:, 2 * half :], 1, 1))


def feed_model(act, grad, proj):
    _, rows, half = act.shape
    model = proj.shape[0]
    tile = min(256, rows)
    return pl.pallas_call(
        feed_model_kernel,
        grid=(rows // tile,),
        in_specs=[
            pl.BlockSpec((2, tile, half), lambda i: (0, i, 0)),
            pl.BlockSpec((2, tile, 2 * half), lambda i: (0, i, 0)),
            pl.BlockSpec(proj.shape, lambda i: (0, 0), pipeline_mode=pl.Buffered(1)),
        ],
        out_specs=[pl.BlockSpec((tile, model), lambda i: (i, 0))] * 4,
        out_shape=[jax.ShapeDtypeStruct((rows, model), jnp.bfloat16)] * 4,
        compiler_params=call_params(40),
        cost_estimate=cheap(),
        name="feed_model",
    )(act, grad, proj)


def feed_weights_kernel(*refs):
    normed, cotangent, grad, act, out_ref = refs[:4], refs[4:8], refs[8:10], refs[10:12], refs[12]
    wide_cols = grad[0].shape[-1]
    out_ref[:, :wide_cols] = low(
        sum(contract(normed[k][...], grad[k // 2][k % 2], 0, 0) for k in range(4))
    )
    out_ref[:, wide_cols:] = low(
        sum(contract(cotangent[k][...], act[k // 2][k % 2], 0, 0) for k in range(4))
    )


def feed_weights(normed, cotangent, grad, act):
    rows, model = normed[0].shape
    width = grad[0].shape[-1] + act[0].shape[-1]
    cols = min(512, model)

    def whole(array):
        return pl.BlockSpec(array.shape, lambda i: (0, 0, 0), pipeline_mode=pl.Buffered(1))

    return pl.pallas_call(
        feed_weights_kernel,
        grid=(model // cols,),
        in_specs=[pl.BlockSpec((rows, cols), lambda i: (0, i))] * 8 + [whole(a) for a in (*grad, *act)],
        out_specs=pl.BlockSpec((cols, width), lambda i: (i, 0)),
        out_shape=jax.ShapeDtypeStruct((model, width), jnp.bfloat16),
        compiler_params=call_params(48),
        cost_estimate=cheap(),
        name="feed_weights",
    )(*normed, *cotangent, *grad, *act)


def feed_sums_kernel(count, side_ref, *refs):
    own, other, outs = refs[:count], refs[count:-3], refs[-3:]
    half = outs[0].shape[1]
    mine = pl.program_id(0) == side_ref[0]
    for held, keep in ((own, mine), (other, jnp.logical_not(mine))):

        @pl.when(keep)
        def _():
            first = 0
            for part in held:
                for k, out in enumerate(outs):
                    out[first : first + part.shape[0], :] = wide(part[:, k * half : (k + 1) * half])
                first += part.shape[0]


def feed_sums(side, own, other):
    rows, width = sum(part.shape[0] for part in own), own[0].shape[1]
    half = width // 3
    parts = (*own, *other)
    return pl.pallas_call(
        functools.partial(feed_sums_kernel, len(own)),
        grid_spec=pltpu.PrefetchScalarGridSpec(
            num_scalar_prefetch=1,
            grid=(2,),
            in_specs=[
                pl.BlockSpec(p.shape, lambda i, side: (0, 0), pipeline_mode=pl.Buffered(1)) for p in parts
            ],
            out_specs=[pl.BlockSpec((rows, half), lambda i, side: (0, i))] * 3,
        ),
        out_shape=[jax.ShapeDtypeStruct((rows, 2 * half), jnp.float32)] * 3,
        compiler_params=call_params(32),
        cost_estimate=cheap(),
        name="feed_sums",
    )(side, *parts)


def per_device(
    tokens,
    segments,
    ln1_gain,
    w_query,
    w_key,
    w_value,
    query_gain,
    key_gain,
    w_out,
    ln2_gain,
    w_gate,
    w_up,
    w_down,
    cotangent,
):
    length, model = tokens.shape
    query_cols, key_cols = w_query.shape[1], w_key.shape[1]
    query_heads = query_cols // HD
    kv_local = key_cols // HD
    group = query_heads // kv_local
    size = lax.axis_size("fsdp")
    shard = model // size
    hidden = w_gate.shape[1]
    half = hidden // 2
    strides = bits("fsdp")
    group_size = lax.axis_size(PLANE)
    share_rows = length // group_size
    share_start = lax.axis_index(PLANE) * share_rows
    segment_row = segments[0]

    def share_of(array):
        return lax.dynamic_slice_in_dim(array, share_start, share_rows, 0)

    proj = lax.all_gather(
        jnp.concatenate([w_query, w_key, w_value, w_out], axis=1), "fsdp", axis=0, tiled=True
    )
    side = bit("fsdp", 1)

    def half_of(which):
        return jnp.concatenate(
            [lax.dynamic_slice_in_dim(w, which * half, half, 1) for w in (w_gate, w_up, w_down)], axis=1
        )

    got = swap(after(half_of(1 - side), proj), "fsdp", 1)
    feed_block = both(half_of(side), got, side, 0)

    gains = line_gather(jnp.concatenate([ln1_gain, ln2_gain, query_gain, key_gain]), strides)
    gain_attn = gains[:, :shard].reshape(model)
    gain_ffn = gains[:, shard : 2 * shard].reshape(model)
    head_part = HD // size
    query_norm = gains[:, 2 * shard : 2 * shard + head_part].reshape(HD)
    key_norm = gains[:, 2 * shard + head_part :].reshape(HD)

    cosine, sine = rope_tables(doc_positions(segment_row))
    normed, scale_one, seg_rows = prepare(tokens, wide(gain_attn), segment_row[:, None])
    query_gain_wide, key_gain_wide = wide(query_norm), wide(key_norm)
    by_chip = cotangent.reshape(4, 2, share_rows, model)
    core = lax.axis_index("tensor")
    own_cot = [pick(by_chip, k, 1).reshape(length // 2, model) for k in (core, 1 - core)]
    own_cot, normed = lax.optimization_barrier((own_cot, normed))
    raw, query_rot, key_rot, values, mixed_low = attend(
        group, normed, proj, cosine, sine, query_gain_wide, key_gain_wide, seg_rows, segment_row
    )
    out_keep, out_give = attend_out(mixed_low, proj)
    out_got = swap(out_give, "tensor", 1)
    out_got, feed_block = lax.optimization_barrier((out_got, feed_block))
    feed_proj = lax.all_gather(
        feed_block, "fsdp", axis=0, tiled=True, axis_index_groups=alike()
    ).reshape(model, -1)

    def middle(tokens, cotangent, out_keep, out_got):
        cot = Job(pair_gather(share_of(cotangent), 2))
        out_sum = Job(chip_scatter(*fold_chip(out_keep, out_got)))
        beside(out_sum, cot)
        beside(out_sum, cot)
        hidden_share = wide(share_of(tokens)) + out_sum.value
        scale_share = rms_parts(hidden_share)
        normed_share = low(hidden_share * scale_share * wide(gain_ffn))
        gather = Job(plane_gather(normed_share[None]))
        pair_share = Job(pair_swap(normed_share, 2))
        beside(pair_share, gather, cot)
        beside(pair_share, gather)
        pair_gather_x = Job(plane_gather(pair_share.value[None]))
        beside(pair_gather_x, cot, gather)
        beside(pair_gather_x, cot)
        finish(pair_gather_x, cot, gather)
        arrays = (*gather.value, *pair_gather_x.value, *cot.value)
        return hidden_share, scale_share, *(array[0] for array in arrays)

    hidden_share, scale_share, *parts = apart(middle, tokens, cotangent, out_keep, out_got)
    own_normed, pair_normed, pair_cot = parts[:2], parts[2:4], parts[4:]

    act, pair_act, grad, pair_grad = feed((*own_normed, *pair_normed), (*own_cot, *pair_cot), feed_proj)
    pair_parts = feed_model(pair_act, pair_grad, feed_proj)
    pair_sum = Job(plane_scatter(*pair_parts[:2]))
    (own_parts,) = beside(pair_sum, kernels=[(feed_model, (act, grad, feed_proj))])
    weight_args = ((*own_normed, *pair_normed), (*own_cot, *pair_cot), (grad, pair_grad), (act, pair_act))
    (feed_w_part,) = beside(pair_sum, kernels=[(feed_weights, weight_args)])
    feed_w_sum = lax.psum_scatter(
        feed_w_part, "fsdp", scatter_dimension=0, tiled=True, axis_index_groups=alike()
    ).reshape(2, shard, -1)
    pair_held = pair_sum.keep

    def back(hidden_share, scale_share, cotangent, *kept):
        pair_sum = Job(line_scatter(*pair_held, True))
        own_sum = Job(plane_scatter(*own_parts[:2]))
        out_sum = Job(plane_scatter(*own_parts[2:]))
        pair_out_sum = Job(plane_scatter(*pair_parts[2:], True))
        beside(pair_sum, own_sum, pair_out_sum, out_sum)
        pair_share = Job(pair_swap(pair_sum.value, 2))
        beside(pair_share, own_sum, ready=[pair_out_sum])
        beside(pair_share, own_sum, pair_out_sum, ready=[out_sum])
        grad_share = own_sum.value + wide(pair_share.value)
        hidden_grad_share = wide(share_of(cotangent)) + norm_back(
            hidden_share, scale_share, grad_share * wide(gain_ffn)
        )
        ffn_gain_part = jnp.sum(grad_share * hidden_share * scale_share, axis=0)
        gather = Job(plane_gather(low(hidden_grad_share)[None]))
        beside(gather, ready=[pair_out_sum])
        beside(gather)
        beside(gather, pair_out_sum)
        grad_mine, grad_other = (array[0] for array in gather.value)
        pair_out = Job(pair_swap(pair_out_sum.value))

        def attended(*kept):
            low_grad, mixed_split, head_gain_part = attend_back(group, grad_mine, grad_other, *kept)
            return *attend_weights(low_grad, mixed_split, scale_one, grad_mine, grad_other, proj, tokens, normed), head_gain_part

        (results,) = beside(pair_out, out_sum, kernels=[(attended, kept)])
        return hidden_grad_share, ffn_gain_part, *results, pair_out.value, *out_sum.held, *out_sum.arrived

    (
        hidden_grad_share, ffn_gain_part, attn_w_part, keep, give, attn_gain_part, head_gain_part, pair_out, *held
    ) = apart(
        back, hidden_share, scale_share, cotangent, proj, cosine, sine, query_gain_wide, key_gain_wide, seg_rows, segment_row,
        raw, query_rot, key_rot, values, mixed_low,
    )
    feed_w_sum, attn_w_part = lax.optimization_barrier((feed_w_sum, attn_w_part))
    attn_w_part, give = lax.optimization_barrier((attn_w_part, give))
    attn_w_sum = lax.psum_scatter(attn_w_part, "fsdp", scatter_dimension=0, tiled=True)

    def last(keep, give, feed_w_sum, hidden_share, pair_out, hidden_grad_share, tokens, scale_one, *rest):
        gain_parts, (_, keep_first, _, keep_second, got_first, got_second) = rest[:4], rest[4:]
        out_sum = Job(line_scatter(*fold_line(keep_first, got_first, keep_second, got_second)))
        feed_pair = Job(pair_swap(pick(feed_w_sum, 1 - side, 0), 4))
        normed_sum = Job(plane_scatter(keep, give))
        gains = Job(sum_all(jnp.concatenate([part.reshape(size, -1) for part in gain_parts], axis=1)))
        beside(normed_sum, out_sum, gains)
        beside(normed_sum, feed_pair, gains)
        beside(normed_sum, feed_pair, gains)
        finish(feed_pair, gains)
        gate_w_grad, up_w_grad, down_w_grad = feed_sums(
            side[None], [pick(feed_w_sum, side, 0)], [feed_pair.value]
        )
        block_out = low(hidden_share + wide(pair_out) + out_sum.value)
        token_share = wide(share_of(tokens))
        scale_one_share = share_of(scale_one)
        tokens_grad = low(
            hidden_grad_share + norm_back(token_share, scale_one_share, normed_sum.value * wide(gain_attn))
        )
        gain_sums = pick(gains.value, lax.axis_index("fsdp"), 0)
        return block_out, tokens_grad, gate_w_grad, up_w_grad, down_w_grad, gain_sums

    block_out, tokens_grad, gate_w_grad, up_w_grad, down_w_grad, gain_sums = apart(
        last, keep, give, feed_w_sum, hidden_share, pair_out, hidden_grad_share, tokens, scale_one,
        attn_gain_part, ffn_gain_part, head_gain_part[0], head_gain_part[1], *held,
    )
    attn_w_grad, gain_sums = lax.optimization_barrier((attn_w_sum, gain_sums))
    attn_w_grad = wide(attn_w_grad)
    out_w_grad = attn_w_grad[:, query_cols + 2 * key_cols :]
    ln1_grad = gain_sums[:shard]
    ln2_grad = gain_sums[shard : 2 * shard]
    query_gain_grad = gain_sums[2 * shard : 2 * shard + head_part]
    key_gain_grad = gain_sums[2 * shard + head_part :]

    return (
        block_out,
        tokens_grad,
        ln1_grad,
        attn_w_grad[:, :query_cols],
        attn_w_grad[:, query_cols : query_cols + key_cols],
        attn_w_grad[:, query_cols + key_cols : query_cols + 2 * key_cols],
        query_gain_grad,
        key_gain_grad,
        out_w_grad,
        ln2_grad,
        gate_w_grad,
        up_w_grad,
        down_w_grad,
    )


def solution(mesh):
    in_specs = (
        P("fsdp", None),
        P("fsdp", None),
        P("fsdp"),
        P("fsdp", ("heads", "tensor")),
        P("fsdp", ("heads", "tensor")),
        P("fsdp", ("heads", "tensor")),
        P("fsdp"),
        P("fsdp"),
        P("fsdp", ("heads", "tensor")),
        P("fsdp"),
        P("fsdp", ("heads", "tensor")),
        P("fsdp", ("heads", "tensor")),
        P("fsdp", ("heads", "tensor")),
        P("fsdp", None),
    )
    out_specs = (
        P(("fsdp", "heads", "tensor"), None),
        P(("fsdp", "heads", "tensor"), None),
        P("fsdp"),
        P("fsdp", ("heads", "tensor")),
        P("fsdp", ("heads", "tensor")),
        P("fsdp", ("heads", "tensor")),
        P("fsdp"),
        P("fsdp"),
        P("fsdp", ("heads", "tensor")),
        P("fsdp"),
        P("fsdp", ("heads", "tensor")),
        P("fsdp", ("heads", "tensor")),
        P("fsdp", ("heads", "tensor")),
    )
    return jax.shard_map(
        per_device, mesh=mesh, in_specs=in_specs, out_specs=out_specs, check_vma=False
    )
```

```python
import functools

import jax
import jax.numpy as jnp
from jax import lax
from jax.experimental import pallas as pl
from jax.experimental.pallas import tpu as pltpu
from jax.sharding import PartitionSpec as P

HD = 128


EPSILON = 1e-06
THETA = 1000000.0
ROWS = 256
BAND = 512
PLANE = ("heads", "tensor")
SWAP = ((0, 1), (1, 0))
NEAR = ((0, 1), (1, 0), (2, 3), (3, 2))
FAR = ((0, 2), (2, 0), (1, 3), (3, 1))


def rms_parts(values):
    return lax.rsqrt(jnp.mean(values * values, axis=-1, keepdims=True) + EPSILON)


def norm_back(values, scale, upstream):
    return scale * upstream - values * scale**3 * jnp.mean(
        values * upstream, axis=-1, keepdims=True
    )


def contract(left, right, left_dim, right_dim):
    return lax.dot_general(
        left, right, (((left_dim,), (right_dim,)), ((), ())), preferred_element_type=jnp.float32
    )


def doc_positions(segment_row):
    places = jnp.arange(segment_row.shape[0], dtype=jnp.int32)
    previous = jnp.concatenate([segment_row[:1], segment_row[:-1]])
    starts = lax.cummax(jnp.where(segment_row != previous, places, 0), axis=0)
    return places - starts


def rope_tables(positions):
    frequency = THETA ** (-(jnp.arange(HD // 2, dtype=jnp.float32) * 2.0 / HD))
    angles = positions.astype(jnp.float32)[:, None] * frequency[None, :]
    cosine, sine = jnp.cos(angles), jnp.sin(angles)
    return (
        jnp.concatenate([cosine, cosine], axis=1),
        jnp.concatenate([-sine, sine], axis=1),
    )


def low(values):
    return values.astype(jnp.bfloat16)


def wide(values):
    return values.astype(jnp.float32)


def flip(axis, stride):
    return [(k, k ^ stride) for k in range(lax.axis_size(axis))]


def after(value, *others):
    return lax.optimization_barrier((value, *others))[0]


def apart(work, *args):
    zeros = [jnp.zeros(out.shape, out.dtype) for out in jax.eval_shape(work, *args)]
    return lax.cond(
        lax.axis_index("fsdp") < lax.axis_size("fsdp"), work, lambda *_: tuple(zeros), *args
    )


class Job:
    def __init__(self, steps):
        self.steps, self.moves, self.keep, self.held, self.value = steps, (), (), (), None
        self.resume(None)

    def resume(self, got):
        self.held, self.arrived = self.keep, got
        try:
            given = self.steps.send(got)
            self.moves, self.keep = given if isinstance(given, tuple) else (given, ())
        except StopIteration as end:
            self.moves, self.keep, self.value = (), (), end.value


def beside(*jobs, kernels=(), ready=()):
    jobs = [job for job in jobs if job.moves]
    ready = [job for job in ready if job.moves]
    given = [[move[0] for move in job.moves] for job in jobs], [args for _, args in kernels]
    arrays, args = lax.optimization_barrier(given)
    got = [
        [lax.ppermute(array, *move[1:]) for array, move in zip(held, job.moves)]
        for held, job in zip(arrays, jobs)
    ]
    results = [kernel[0](*own) for own, kernel in zip(args, kernels)]
    later = [[move[0] for move in job.moves] for job in ready]
    got, results, later = lax.optimization_barrier((got, results, later))
    for job, arrays in zip(ready, later):
        job.moves = [(array, *move[1:]) for array, move in zip(arrays, job.moves)]
    for job, arrived in zip(jobs, got):
        job.resume(arrived)
    return results


def finish(*jobs):
    while any(job.moves for job in jobs):
        beside(*jobs)


def bits(axis):
    size = lax.axis_size(axis)
    return [1 << k for k in range(size.bit_length() - 1)]


def swap(array, axis, stride):
    return lax.ppermute(array, axis, flip(axis, stride))


def bit(axis, stride):
    return (lax.axis_index(axis) // stride) % 2


def line_gather(block, strides):
    block = block[None]
    for stride in strides:
        block = both(block, swap(block, "fsdp", stride), bit("fsdp", stride), 0)
        block = block.reshape(-1, *block.shape[2:])
    return block


def pick(array, index, axis):
    return lax.dynamic_index_in_dim(array, index, axis, keepdims=False)


def both(mine, got, index, axis):
    lower = jnp.where(index == 0, mine, got)
    upper = jnp.where(index == 0, got, mine)
    return jnp.stack([lower, upper], axis=axis)


def position():
    heads = lax.axis_index("heads")
    return jnp.stack([lax.axis_index("tensor"), heads % 2, heads // 2]).astype(jnp.int32)


def vmem_call(kernel, name, megabytes, out_shape, *args):
    return pl.pallas_call(
        kernel,
        in_specs=[pl.BlockSpec(memory_space=pltpu.SMEM)]
        + [pl.BlockSpec(memory_space=pltpu.VMEM)] * len(args),
        out_specs=[pl.BlockSpec(memory_space=pltpu.VMEM)] * len(out_shape),
        out_shape=[jax.ShapeDtypeStruct(shape, jnp.bfloat16) for shape in out_shape],
        compiler_params=call_params(megabytes),
        cost_estimate=cheap(),
        name=name,
    )(position(), *args)


def fold_chip_kernel(position_ref, keep_ref, got_ref, give_first, keep_first, give_second, keep_second):
    x, y = position_ref[1], position_ref[2]
    middle = keep_ref.shape[-1] // 2
    first, second = slice(0, middle), slice(middle, 2 * middle)

    def summed(row, column, cols):
        return low(wide(keep_ref[row, column, :, cols]) + wide(got_ref[row, column, :, cols]))

    for k in range(2):
        give_first[k] = summed(k, 1 - x, first)
        keep_first[k] = summed(k, x, first)
        give_second[k] = summed(1 - y, k, second)
        keep_second[k] = summed(y, k, second)


def fold_chip(keep, got):
    rows, width = keep.shape
    shape = (2, 2, rows // 4, width)
    return vmem_call(
        fold_chip_kernel, "fold_chip", 24, [(2, rows // 4, width // 2)] * 4, keep.reshape(shape), got.reshape(shape)
    )


def fold_line_kernel(
    position_ref, keep_first_ref, got_first_ref, keep_second_ref, got_second_ref, give_first, keep_first, give_second, keep_second
):
    x, y = position_ref[1], position_ref[2]
    for at, keep_ref, got_ref, give, keep in (
        (y, keep_first_ref, got_first_ref, give_first, keep_first),
        (x, keep_second_ref, got_second_ref, give_second, keep_second),
    ):
        give[...] = low(wide(keep_ref[1 - at]) + wide(got_ref[1 - at]))
        keep[...] = low(wide(keep_ref[at]) + wide(got_ref[at]))


def fold_line(keep_first, got_first, keep_second, got_second):
    shape = keep_first.shape[1:]
    return vmem_call(
        fold_line_kernel, "fold_line", 16, [shape] * 4, keep_first, got_first, keep_second, got_second
    )


def fold_end_kernel(position_ref, keep_first_ref, got_first_ref, keep_second_ref, got_second_ref, out_ref):
    middle = keep_first_ref.shape[-1]
    out_ref[:, :middle] = low(wide(keep_first_ref[...]) + wide(got_first_ref[...]))
    out_ref[:, middle:] = low(wide(keep_second_ref[...]) + wide(got_second_ref[...]))


def fold_end(keep_first, got_first, keep_second, got_second):
    rows, width = keep_first.shape
    (out,) = vmem_call(
        fold_end_kernel, "fold_end", 16, [(rows, 2 * width)], keep_first, got_first, keep_second, got_second
    )
    return out


def plane_scatter(keep, give, rounded=False):
    (got,) = yield [(give, "tensor", SWAP)]
    folded = fold_chip(keep, got)
    return (yield from chip_scatter(*folded, rounded))


def chip_scatter(give_first, keep_first, give_second, keep_second, rounded=False):
    held = (give_first, keep_first, give_second, keep_second)
    got = yield [(give_first, "heads", NEAR), (give_second, "heads", FAR)], held
    return (yield from line_scatter(*fold_line(keep_first, got[0], keep_second, got[1]), rounded))


def line_scatter(give_first, keep_first, give_second, keep_second, rounded=False):
    held = (give_first, keep_first, give_second, keep_second)
    got = yield [(give_first, "heads", FAR), (give_second, "heads", NEAR)], held
    if rounded:
        return fold_end(keep_first, got[0], keep_second, got[1])
    first = wide(keep_first) + wide(got[0])
    second = wide(keep_second) + wide(got[1])
    return jnp.concatenate([first, second], axis=-1)


def open_line_kernel(position_ref, first_ref, got_first_ref, second_ref, got_second_ref, first, second):
    x, y = position_ref[1], position_ref[2]
    first[y] = first_ref[...]
    first[1 - y] = got_first_ref[...]
    second[x] = second_ref[...]
    second[1 - x] = got_second_ref[...]


def open_chip_kernel(position_ref, first_ref, got_first_ref, second_ref, got_second_ref, out_ref):
    x, y = position_ref[1], position_ref[2]
    lead, middle = first_ref.shape[1], first_ref.shape[-1]
    for k in range(lead):
        for j in range(2):
            out_ref[k, j, x, :, :middle] = first_ref[j, k]
            out_ref[k, j, 1 - x, :, :middle] = got_first_ref[j, k]
            out_ref[k, y, j, :, middle:] = second_ref[j, k]
            out_ref[k, 1 - y, j, :, middle:] = got_second_ref[j, k]


def plane_gather(share):
    lead, rows, width = share.shape
    first, second = share[..., : width // 2], share[..., width // 2 :]
    got = yield [(first, "heads", FAR), (second, "heads", NEAR)], (first, second)
    first, second = vmem_call(
        open_line_kernel, "open_line", 16, [(2, lead, rows, width // 2)] * 2, first, got[0], second, got[1]
    )
    got = yield [(first, "heads", NEAR), (second, "heads", FAR)], (first, second)
    return (yield from core_gather(first, second, *got))


def core_gather(first, second, got_first, got_second):
    _, lead, rows, middle = first.shape
    (mine,) = vmem_call(
        open_chip_kernel, "open_chip", 24, [(lead, 2, 2, rows, 2 * middle)], first, got_first, second, got_second
    )
    mine = mine.reshape(lead, 4 * rows, 2 * middle)
    (other,) = yield [(mine, "tensor", SWAP)]
    return mine, other


def pair_swap(array, pieces=1):
    rows = array.shape[0] // pieces
    got = []
    for k in range(pieces):
        got += yield [(array[k * rows : (k + 1) * rows], "fsdp", flip("fsdp", 1))]
    return jnp.concatenate(got, axis=0) if pieces > 1 else got[0]


def pair_gather(share, pieces):
    got = yield from pair_swap(share, pieces)
    return (yield from plane_gather(got[None]))


def sum_all(values):
    for axis in ("tensor", "heads", "fsdp"):
        strides = bits(axis)
        if axis == "fsdp" and len(strides) > 1:
            strides = [strides[0] + strides[1]] + strides[1:]
        for stride in strides:
            (got,) = yield [(values, axis, flip(axis, stride))]
            values = values + got
    return values


def alike():
    return [list(range(k, lax.axis_size("fsdp"), 2)) for k in range(2)]


def rotate(values, cosine, sine):
    return values * cosine + pltpu.roll(values, HD // 2, 1) * sine


def call_params(megabytes):
    return pltpu.CompilerParams(vmem_limit_bytes=megabytes << 20)


def cheap():
    return pl.CostEstimate(flops=1000, bytes_accessed=1000, transcendentals=0)


def key_blocks(at, count):
    return max(0, at - BAND // ROWS), at + 1


def masked_probs(query, keys, seg_rows, seg_keys, first_row, first_key):
    scores = contract(query, keys, 1, 1) * HD**-0.5
    rows = first_row + lax.broadcasted_iota(jnp.int32, scores.shape, 0)
    cols = first_key + lax.broadcasted_iota(jnp.int32, scores.shape, 1)
    scores = jnp.where((rows >= cols) & (seg_rows == seg_keys), scores, -1e30)
    expo = jnp.exp(scores - jnp.max(scores, axis=-1, keepdims=True))
    return expo / jnp.sum(expo, axis=-1, keepdims=True)


def by_core(core, block):
    middle = block.shape[0] // 2
    lower, upper = block[:middle], block[middle:]
    first = core == 0
    return jnp.where(first, lower, upper), jnp.where(first, upper, lower)


def joined(core, mine, other):
    first = core == 0
    return jnp.concatenate([jnp.where(first, mine, other), jnp.where(first, other, mine)], axis=0)


def attend_kernel(
    group,
    normed_ref,
    proj_ref,
    cosine_ref,
    sine_ref,
    query_gain_ref,
    key_gain_ref,
    seg_rows_ref,
    seg_keys_ref,
    raw_ref,
    query_ref,
    key_ref,
    value_ref,
    mixed_ref,
    keys,
    values,
):
    length, kv_cols = keys.shape
    kv_local = kv_cols // HD
    query_cols = kv_cols * group
    count = length // ROWS
    step = pl.program_id(0)
    raw = jnp.dot(normed_ref[...], proj_ref[...], preferred_element_type=jnp.float32)
    raw_ref[...] = raw[:, : query_cols + kv_cols]
    cosine, sine = cosine_ref[...], sine_ref[...]
    here = pl.ds(pl.multiple_of(step * ROWS, ROWS), ROWS)

    def turned(head, gain_ref):
        one = raw[:, head * HD : (head + 1) * HD]
        return low(rotate(one * rms_parts(one) * gain_ref[...], cosine, sine))

    for kv in range(kv_local):
        at = slice(kv * HD, (kv + 1) * HD)
        new_keys = turned(query_cols // HD + kv, key_gain_ref)
        new_values = low(raw[:, query_cols + kv_cols + kv * HD : query_cols + kv_cols + (kv + 1) * HD])
        key_ref[:, at] = new_keys
        value_ref[:, at] = new_values
        keys[here, at] = new_keys
        values[here, at] = new_values
    for head in range(query_cols // HD):
        query_ref[:, head * HD : (head + 1) * HD] = turned(head, query_gain_ref)

    for at in range(count):

        @pl.when(step == at)
        def _():
            lower, upper = key_blocks(at, count)
            span = slice(lower * ROWS, upper * ROWS)
            for head in range(query_cols // HD):
                cols = slice(head * HD, (head + 1) * HD)
                kv = slice((head // group) * HD, (head // group + 1) * HD)
                probs = masked_probs(
                    query_ref[:, cols],
                    keys[span, kv],
                    seg_rows_ref[...],
                    seg_keys_ref[:, span],
                    at * ROWS,
                    lower * ROWS,
                )
                mixed_ref[:, cols] = low(
                    jnp.dot(low(probs), values[span, kv], preferred_element_type=jnp.float32)
                )


def attend(group, normed, proj, cosine, sine, query_gain, key_gain, seg_rows, segment_row):
    length, model = normed.shape
    kv_cols = proj.shape[1] // (2 * group + 2)
    query_cols = kv_cols * group

    def rows(width):
        return pl.BlockSpec((ROWS, width), lambda i: (i, 0))

    def whole(array):
        return pl.BlockSpec(array.shape, lambda i: (0, 0))

    seg_keys = segment_row[None, :]
    args = (normed, proj, cosine, sine, query_gain[None], key_gain[None], seg_rows, seg_keys)
    outs = [
        (query_cols + kv_cols, jnp.float32),
        (query_cols, jnp.bfloat16),
        (kv_cols, jnp.bfloat16),
        (kv_cols, jnp.bfloat16),
        (query_cols, jnp.bfloat16),
    ]
    return pl.pallas_call(
        functools.partial(attend_kernel, group),
        grid=(length // ROWS,),
        in_specs=[
            rows(model),
            pl.BlockSpec((model, query_cols + 2 * kv_cols), lambda i: (0, 0)),
            rows(HD),
            rows(HD),
            whole(args[4]),
            whole(args[5]),
            rows(1),
            whole(seg_keys),
        ],
        out_specs=[rows(width) for width, _ in outs],
        out_shape=[jax.ShapeDtypeStruct((length, width), kind) for width, kind in outs],
        scratch_shapes=[
            pltpu.VMEM((length, kv_cols), jnp.bfloat16),
            pltpu.VMEM((length, kv_cols), jnp.bfloat16),
        ],
        compiler_params=call_params(40),
        cost_estimate=cheap(),
        name="attend",
    )(*args)


def attend_out_kernel(position_ref, mixed_ref, proj_ref, keep_ref, give_ref):
    keep_ref[...], give_ref[...] = by_core(
        position_ref[0], low(contract(mixed_ref[...], proj_ref[...], 1, 1))
    )


def attend_out(mixed, proj):
    length, cols = mixed.shape
    model = proj.shape[0]
    return pl.pallas_call(
        attend_out_kernel,
        grid=(length // ROWS,),
        in_specs=[
            pl.BlockSpec(memory_space=pltpu.SMEM),
            pl.BlockSpec((ROWS, cols), lambda i: (i, 0)),
            pl.BlockSpec((model, cols), lambda i: (0, proj.shape[1] // cols - 1)),
        ],
        out_specs=[pl.BlockSpec((ROWS // 2, model), lambda i: (i, 0))] * 2,
        out_shape=[jax.ShapeDtypeStruct((length // 2, model), jnp.bfloat16)] * 2,
        compiler_params=call_params(24),
        cost_estimate=cheap(),
        name="attend_out",
    )(position(), mixed, proj)


def attend_back_kernel(
    group,
    grad_mine_ref,
    grad_other_ref,
    out_proj_ref,
    cosine_ref,
    sine_ref,
    query_gain_ref,
    key_gain_ref,
    seg_rows_ref,
    seg_keys_ref,
    raw_ref,
    query_ref,
    key_ref,
    value_ref,
    mixed_ref,
    position_ref,
    low_ref,
    mixed_split_ref,
    head_gain_ref,
    mixed_grad,
    query_sum,
    key_sum,
    value_sum,
):
    length, kv_cols = key_sum.shape
    query_cols = kv_cols * group
    count = length // ROWS
    share = ROWS // 2
    core = position_ref[0]
    for k, ref in enumerate((grad_mine_ref, grad_other_ref)):
        part = low(jnp.dot(ref[...], out_proj_ref[...], preferred_element_type=jnp.float32))
        for at in range(count):
            start = pl.multiple_of(at * ROWS + (core + k - 2 * k * core) * share, share)
            mixed_grad[pl.ds(start, share), :] = part[at * share : (at + 1) * share]
            mixed_split_ref[k, at * share : (at + 1) * share, :] = mixed_ref[pl.ds(start, share), :]
    key_sum[...] = jnp.zeros_like(key_sum)
    value_sum[...] = jnp.zeros_like(value_sum)
    for at in range(count):
        here = slice(at * ROWS, (at + 1) * ROWS)
        lower, upper = key_blocks(at, count)
        span = slice(lower * ROWS, upper * ROWS)
        for head in range(query_cols // HD):
            cols = slice(head * HD, (head + 1) * HD)
            kv = slice((head // group) * HD, (head // group + 1) * HD)
            query = query_ref[here, cols]
            grad = mixed_grad[here, cols]
            probs = masked_probs(
                query,
                key_ref[span, kv],
                seg_rows_ref[here, :],
                seg_keys_ref[:, span],
                at * ROWS,
                lower * ROWS,
            )
            prob_grad = contract(grad, value_ref[span, kv], 1, 1)
            row_inner = jnp.sum(probs * prob_grad, axis=-1, keepdims=True)
            score_grad = low(HD**-0.5 * probs * (prob_grad - row_inner))
            query_sum[here, cols] = jnp.dot(
                score_grad, key_ref[span, kv], preferred_element_type=jnp.float32
            )
            key_sum[span, kv] += contract(score_grad, query, 0, 0)
            value_sum[span, kv] += contract(low(probs), grad, 0, 0)

    head_gain_ref[...] = jnp.zeros_like(head_gain_ref)
    for at in range(count):
        here = slice(at * ROWS, (at + 1) * ROWS)
        cosine, sine = cosine_ref[here, :], -sine_ref[here, :]
        for head in range((query_cols + kv_cols) // HD):
            cols = slice(head * HD, (head + 1) * HD)
            own = slice(head * HD - query_cols, (head + 1) * HD - query_cols)
            is_query = head * HD < query_cols
            turned = rotate(query_sum[here, cols] if is_query else key_sum[here, own], cosine, sine)
            raw = raw_ref[here, cols]
            scale = rms_parts(raw)
            row = 0 if is_query else 1
            head_gain_ref[row : row + 1, :] += jnp.sum(turned * raw * scale, axis=0, keepdims=True)
            gain = query_gain_ref[...] if is_query else key_gain_ref[...]
            low_ref[here, cols] = low(norm_back(raw, scale, turned * gain))
        low_ref[here, query_cols + kv_cols :] = low(value_sum[here, :])


def attend_back(
    group, grad_mine, grad_other, proj, cosine, sine, query_gain, key_gain, seg_rows, segment_row, raw, query, key, value, mixed
):
    length, query_cols, kv_cols = query.shape[0], query.shape[1], key.shape[1]
    args = (
        grad_mine, grad_other, proj, cosine, sine, query_gain[None], key_gain[None],
        seg_rows, segment_row[None, :], raw, query, key, value, mixed, position(),
    )
    out_shape = [
        jax.ShapeDtypeStruct((length, query_cols + 2 * kv_cols), jnp.bfloat16),
        jax.ShapeDtypeStruct((2, length // 2, query_cols), jnp.bfloat16),
        jax.ShapeDtypeStruct((2, HD), jnp.float32),
    ]

    def whole(array):
        return pl.BlockSpec(array.shape, lambda i: (0,) * len(array.shape), pipeline_mode=pl.Buffered(1))

    return pl.pallas_call(
        functools.partial(attend_back_kernel, group),
        grid=(1,),
        in_specs=[whole(grad_mine), whole(grad_other)]
        + [pl.BlockSpec((proj.shape[0], query_cols), lambda i: (0, proj.shape[1] // query_cols - 1))]
        + [whole(array) for array in args[3:-1]]
        + [pl.BlockSpec(memory_space=pltpu.SMEM)],
        out_specs=[whole(out) for out in out_shape],
        out_shape=out_shape,
        scratch_shapes=[
            pltpu.VMEM((length, query_cols), jnp.bfloat16),
            pltpu.VMEM((length, query_cols), jnp.float32),
            pltpu.VMEM((length, kv_cols), jnp.float32),
            pltpu.VMEM((length, kv_cols), jnp.float32),
        ],
        compiler_params=call_params(40),
        cost_estimate=cheap(),
        name="attend_back",
    )(*args)


def attend_weights_kernel(
    position_ref, low_ref, mixed_ref, scale_ref, grad_mine_ref, grad_other_ref, proj_ref, tokens_ref, normed_ref,
    weight_ref, keep_ref, give_ref, gain_ref,
):
    split = low_ref.shape[1]
    share = ROWS // 2
    gain = jnp.zeros_like(gain_ref)
    for at in range(low_ref.shape[0] // ROWS):
        here = slice(at * ROWS, (at + 1) * ROWS)
        rows = slice(at * share, (at + 1) * share)
        part = contract(low_ref[here, :], proj_ref[...], 1, 1)
        keep_ref[rows, :], give_ref[rows, :] = by_core(position_ref[0], low(part))
        gain += jnp.sum(part * wide(tokens_ref[here, :]) * scale_ref[here, :], axis=0, keepdims=True)
    gain_ref[...] = gain
    weight_ref[:, :split] = low(contract(normed_ref[...], low_ref[...], 0, 0))
    weight_ref[:, split:] = low(
        contract(grad_mine_ref[...], mixed_ref[0], 0, 0) + contract(grad_other_ref[...], mixed_ref[1], 0, 0)
    )


def attend_weights(low_grad, mixed, scale, grad_mine, grad_other, proj, tokens, normed):
    length, model = tokens.shape
    split = low_grad.shape[1]
    width = split + mixed.shape[-1]
    cols = min(512, model)

    def whole(array):
        return pl.BlockSpec(array.shape, lambda i: (0,) * array.ndim, pipeline_mode=pl.Buffered(1))

    def columns(rows):
        return pl.BlockSpec((rows, cols), lambda i: (0, i))

    return pl.pallas_call(
        attend_weights_kernel,
        grid=(model // cols,),
        in_specs=[
            pl.BlockSpec(memory_space=pltpu.SMEM),
            whole(low_grad),
            whole(mixed),
            whole(scale),
            columns(length // 2),
            columns(length // 2),
            pl.BlockSpec((cols, split), lambda i: (i, 0)),
            columns(length),
            columns(length),
        ],
        out_specs=[
            pl.BlockSpec((cols, width), lambda i: (i, 0)),
            columns(length // 2),
            columns(length // 2),
            columns(1),
        ],
        out_shape=[
            jax.ShapeDtypeStruct((model, width), jnp.bfloat16),
            jax.ShapeDtypeStruct((length // 2, model), jnp.bfloat16),
            jax.ShapeDtypeStruct((length // 2, model), jnp.bfloat16),
            jax.ShapeDtypeStruct((1, model), jnp.float32),
        ],
        compiler_params=call_params(40),
        cost_estimate=cheap(),
        name="attend_weights",
    )(position(), low_grad, mixed, scale, grad_mine, grad_other, proj, tokens, normed)


def prepare_kernel(tokens_ref, gain_ref, seg_ref, normed_ref, scale_ref, seg_rows_ref):
    block_in = wide(tokens_ref[...])
    scale = rms_parts(block_in)
    scale_ref[...] = scale
    normed_ref[...] = low(block_in * scale * gain_ref[...])
    seg_rows_ref[...] = seg_ref[...]


def prepare(tokens, gain, seg_rows):
    length, model = tokens.shape

    def rows(width):
        return pl.BlockSpec((ROWS, width), lambda i: (i, 0))

    return pl.pallas_call(
        prepare_kernel,
        grid=(length // ROWS,),
        in_specs=[rows(model), pl.BlockSpec((1, model), lambda i: (0, 0)), rows(1)],
        out_specs=[rows(model), rows(1), rows(1)],
        out_shape=[
            jax.ShapeDtypeStruct((length, model), jnp.bfloat16),
            jax.ShapeDtypeStruct((length, 1), jnp.float32),
            jax.ShapeDtypeStruct((length, 1), jnp.int32),
        ],
        compiler_params=call_params(24),
        cost_estimate=pl.CostEstimate(flops=20_000_000_000, bytes_accessed=20_000_000, transcendentals=0),
        name="prepare",
    )(tokens, gain[None], seg_rows)


def feed_kernel(*refs):
    sources, (proj_hbm, *results, normed, cotangent, proj, arrive) = refs[:8], refs[8:]
    acts, grads = results[:2], results[2:]
    half = acts[0].shape[-1]
    rows = sources[0].shape[0]
    tile = min(256, rows)

    def fetch(source, target, k):
        copy = pltpu.make_async_copy(source, target, arrive.at[k])
        copy.start()
        return copy

    loads = [fetch(proj_hbm, proj, 8)]
    for k in range(4):
        loads.append(fetch(sources[k], normed.at[k], 2 * k))
        loads.append(fetch(sources[4 + k], cotangent.at[k], 2 * k + 1))
    loads[0].wait()
    for k in range(4):
        loads[2 * k + 1].wait()
        loads[2 * k + 2].wait()
        act_ref, grad_ref = acts[k // 2], grads[k // 2]

        @pl.loop(0, rows // tile)
        def _(step):
            here = pl.ds(pl.multiple_of(step * tile, tile), tile)
            gate_up = jnp.dot(normed[k, here, :], proj[:, : 2 * half], preferred_element_type=jnp.float32)
            gate, up = gate_up[:, :half], gate_up[:, half:]
            act_grad = jnp.dot(cotangent[k, here, :], proj[:, 2 * half :], preferred_element_type=jnp.float32)
            sigmoid = jax.nn.sigmoid(gate)
            silu = gate * sigmoid
            act_ref[k % 2, here, :] = low(silu * up)
            grad_ref[k % 2, here, :half] = low(act_grad * up * sigmoid * (1.0 + gate * (1.0 - sigmoid)))
            grad_ref[k % 2, here, half:] = low(act_grad * silu)


def feed(normed, cotangent, proj):
    rows, model = normed[0].shape
    half = proj.shape[1] // 3
    widths = (half, half, 2 * half, 2 * half)
    return pl.pallas_call(
        feed_kernel,
        in_specs=[pl.BlockSpec(memory_space=pl.ANY)] * 9,
        out_specs=[pl.BlockSpec(memory_space=pltpu.VMEM)] * 4,
        out_shape=[jax.ShapeDtypeStruct((2, rows, w), jnp.bfloat16) for w in widths],
        scratch_shapes=[
            pltpu.VMEM((4, rows, model), jnp.bfloat16),
            pltpu.VMEM((4, rows, model), jnp.bfloat16),
            pltpu.VMEM(proj.shape, jnp.bfloat16),
            pltpu.SemaphoreType.DMA((9,)),
        ],
        compiler_params=call_params(48),
        cost_estimate=cheap(),
        name="feed",
    )(*normed, *cotangent, proj)


def feed_model_kernel(act_ref, grad_ref, proj_ref, keep_ref, give_ref, keep_out_ref, give_out_ref):
    half = act_ref.shape[-1]
    for k, (out_ref, out_out_ref) in enumerate(((keep_ref, keep_out_ref), (give_ref, give_out_ref))):
        out_ref[...] = low(contract(grad_ref[k], proj_ref[:, : 2 * half], 1, 1))
        out_out_ref[...] = low(contract(act_ref[k], proj_ref[:, 2 * half :], 1, 1))


def feed_model(act, grad, proj):
    _, rows, half = act.shape
    model = proj.shape[0]
    tile = min(256, rows)
    return pl.pallas_call(
        feed_model_kernel,
        grid=(rows // tile,),
        in_specs=[
            pl.BlockSpec((2, tile, half), lambda i: (0, i, 0)),
            pl.BlockSpec((2, tile, 2 * half), lambda i: (0, i, 0)),
            pl.BlockSpec(proj.shape, lambda i: (0, 0), pipeline_mode=pl.Buffered(1)),
        ],
        out_specs=[pl.BlockSpec((tile, model), lambda i: (i, 0))] * 4,
        out_shape=[jax.ShapeDtypeStruct((rows, model), jnp.bfloat16)] * 4,
        compiler_params=call_params(40),
        cost_estimate=cheap(),
        name="feed_model",
    )(act, grad, proj)


def feed_weights_kernel(*refs):
    normed, cotangent, grad, act, (wide_ref, out_ref) = refs[:4], refs[4:8], refs[8:10], refs[10:12], refs[12:]
    wide_ref[...] = low(
        sum(contract(normed[k][...], grad[k // 2][k % 2], 0, 0) for k in range(4))
    )
    out_ref[...] = low(
        sum(contract(cotangent[k][...], act[k // 2][k % 2], 0, 0) for k in range(4))
    )


def feed_weights(normed, cotangent, grad, act):
    rows, model = normed[0].shape
    widths = grad[0].shape[-1], act[0].shape[-1]
    cols = min(512, model)

    def whole(array):
        return pl.BlockSpec(array.shape, lambda i: (0, 0, 0), pipeline_mode=pl.Buffered(1))

    return pl.pallas_call(
        feed_weights_kernel,
        grid=(model // cols,),
        in_specs=[pl.BlockSpec((rows, cols), lambda i: (0, i))] * 8 + [whole(a) for a in (*grad, *act)],
        out_specs=[pl.BlockSpec((cols, width), lambda i: (i, 0)) for width in widths],
        out_shape=[jax.ShapeDtypeStruct((model, width), jnp.bfloat16) for width in widths],
        compiler_params=call_params(48),
        cost_estimate=cheap(),
        name="feed_weights",
    )(*normed, *cotangent, *grad, *act)


def feed_sums_kernel(side_ref, *refs):
    sources, outs = refs[:4], refs[4:]
    half = outs[0].shape[1]
    mine = pl.program_id(0) == side_ref[0]
    for (wide_ref, down_ref), keep in ((sources[:2], mine), (sources[2:], jnp.logical_not(mine))):

        @pl.when(keep)
        def _():
            for k in range(2):
                outs[k][...] = wide(wide_ref[:, k * half : (k + 1) * half])
            outs[2][...] = wide(down_ref[...])


def feed_sums(side, own, other):
    rows, half = other[1].shape
    return pl.pallas_call(
        feed_sums_kernel,
        grid_spec=pltpu.PrefetchScalarGridSpec(
            num_scalar_prefetch=1,
            grid=(2,),
            in_specs=[pl.BlockSpec((None, rows, w), lambda i, side: (side[0], 0, 0)) for w in (2 * half, half)]
            + [pl.BlockSpec((rows, w), lambda i, side: (0, 0)) for w in (2 * half, half)],
            out_specs=[pl.BlockSpec((rows, half), lambda i, side: (0, i))] * 3,
        ),
        out_shape=[jax.ShapeDtypeStruct((rows, 2 * half), jnp.float32)] * 3,
        compiler_params=call_params(32),
        cost_estimate=cheap(),
        name="feed_sums",
    )(side, *own, *other)


def per_device(
    tokens,
    segments,
    ln1_gain,
    w_query,
    w_key,
    w_value,
    query_gain,
    key_gain,
    w_out,
    ln2_gain,
    w_gate,
    w_up,
    w_down,
    cotangent,
):
    length, model = tokens.shape
    query_cols, key_cols = w_query.shape[1], w_key.shape[1]
    query_heads = query_cols // HD
    kv_local = key_cols // HD
    group = query_heads // kv_local
    size = lax.axis_size("fsdp")
    shard = model // size
    hidden = w_gate.shape[1]
    half = hidden // 2
    strides = bits("fsdp")
    group_size = lax.axis_size(PLANE)
    share_rows = length // group_size
    share_start = lax.axis_index(PLANE) * share_rows
    segment_row = segments[0]

    def share_of(array):
        return lax.dynamic_slice_in_dim(array, share_start, share_rows, 0)

    proj = lax.all_gather(
        jnp.concatenate([w_query, w_key, w_value, w_out], axis=1), "fsdp", axis=0, tiled=True
    )
    side = bit("fsdp", 1)

    def half_of(which):
        return jnp.concatenate(
            [lax.dynamic_slice_in_dim(w, which * half, half, 1) for w in (w_gate, w_up, w_down)], axis=1
        )

    got = swap(after(half_of(1 - side), proj), "fsdp", 1)
    feed_block = both(half_of(side), got, side, 0)

    gains = line_gather(jnp.concatenate([ln1_gain, ln2_gain, query_gain, key_gain]), strides)
    gain_attn = gains[:, :shard].reshape(model)
    gain_ffn = gains[:, shard : 2 * shard].reshape(model)
    head_part = HD // size
    query_norm = gains[:, 2 * shard : 2 * shard + head_part].reshape(HD)
    key_norm = gains[:, 2 * shard + head_part :].reshape(HD)

    cosine, sine = rope_tables(doc_positions(segment_row))
    normed, scale_one, seg_rows = prepare(tokens, wide(gain_attn), segment_row[:, None])
    query_gain_wide, key_gain_wide = wide(query_norm), wide(key_norm)
    by_chip = cotangent.reshape(4, 2, share_rows, model)
    core = lax.axis_index("tensor")
    own_cot = [pick(by_chip, k, 1).reshape(length // 2, model) for k in (core, 1 - core)]
    own_cot, normed = lax.optimization_barrier((own_cot, normed))
    raw, query_rot, key_rot, values, mixed_low = attend(
        group, normed, proj, cosine, sine, query_gain_wide, key_gain_wide, seg_rows, segment_row
    )
    out_keep, out_give = attend_out(mixed_low, proj)
    out_got = swap(out_give, "tensor", 1)
    out_got, feed_block = lax.optimization_barrier((out_got, feed_block))
    feed_proj = lax.all_gather(
        feed_block, "fsdp", axis=0, tiled=True, axis_index_groups=alike()
    ).reshape(model, -1)

    def middle(tokens, cotangent, out_keep, out_got):
        cot = Job(pair_gather(share_of(cotangent), 2))
        out_sum = Job(chip_scatter(*fold_chip(out_keep, out_got)))
        beside(out_sum, cot)
        beside(out_sum, cot)
        hidden_share = wide(share_of(tokens)) + out_sum.value
        scale_share = rms_parts(hidden_share)
        normed_share = low(hidden_share * scale_share * wide(gain_ffn))
        gather = Job(plane_gather(normed_share[None]))
        pair_share = Job(pair_swap(normed_share, 2))
        beside(pair_share, gather, cot)
        beside(pair_share, gather)
        pair_gather_x = Job(plane_gather(pair_share.value[None]))
        beside(pair_gather_x, cot, gather)
        beside(pair_gather_x, cot)
        finish(pair_gather_x, cot, gather)
        arrays = (*gather.value, *pair_gather_x.value, *cot.value)
        return hidden_share, scale_share, *(array[0] for array in arrays)

    hidden_share, scale_share, *parts = apart(middle, tokens, cotangent, out_keep, out_got)
    own_normed, pair_normed, pair_cot = parts[:2], parts[2:4], parts[4:]

    act, pair_act, grad, pair_grad = feed((*own_normed, *pair_normed), (*own_cot, *pair_cot), feed_proj)
    pair_parts = feed_model(pair_act, pair_grad, feed_proj)
    pair_sum = Job(plane_scatter(*pair_parts[:2]))
    (own_parts,) = beside(pair_sum, kernels=[(feed_model, (act, grad, feed_proj))])
    weight_args = ((*own_normed, *pair_normed), (*own_cot, *pair_cot), (grad, pair_grad), (act, pair_act))
    (feed_w_parts,) = beside(pair_sum, kernels=[(feed_weights, weight_args)])
    feed_w_sums = [
        lax.psum_scatter(part, "fsdp", scatter_dimension=0, tiled=True, axis_index_groups=alike()).reshape(2, shard, -1)
        for part in feed_w_parts
    ]
    pair_held = pair_sum.keep

    def back(hidden_share, scale_share, cotangent):
        pair_sum = Job(line_scatter(*pair_held, True))
        own_sum = Job(plane_scatter(*own_parts[:2]))
        out_sum = Job(plane_scatter(*own_parts[2:]))
        pair_out_sum = Job(plane_scatter(*pair_parts[2:], True))
        beside(pair_sum, own_sum, pair_out_sum, out_sum)
        pair_share = Job(pair_swap(pair_sum.value, 2))
        beside(pair_share, own_sum, ready=[pair_out_sum])
        beside(pair_share, own_sum, pair_out_sum, ready=[out_sum])
        grad_share = own_sum.value + wide(pair_share.value)
        hidden_grad_share = wide(share_of(cotangent)) + norm_back(
            hidden_share, scale_share, grad_share * wide(gain_ffn)
        )
        ffn_gain_part = jnp.sum(grad_share * hidden_share * scale_share, axis=0, keepdims=True)
        gather = Job(plane_gather(low(hidden_grad_share)[None]))
        beside(gather, ready=[pair_out_sum])
        beside(gather)
        return hidden_grad_share, ffn_gain_part, *gather.held, *gather.arrived, *pair_out_sum.keep, *out_sum.keep

    hidden_grad_share, ffn_gain_part, *held = apart(back, hidden_share, scale_share, cotangent)
    wide_give, held = lax.optimization_barrier((pick(feed_w_sums[0], 1 - side, 0), held))
    wide_got = swap(wide_give, "fsdp", 1)

    def attention(held, *kept):
        gather = Job(core_gather(*held[:4]))
        pair_out_sum = Job(line_scatter(*held[4:8], True))
        out_sum = Job(chip_scatter(*held[8:]))
        beside(gather, pair_out_sum)
        grad_mine, grad_other = (array[0] for array in gather.value)
        pair_out = Job(pair_swap(pair_out_sum.value))

        def attended(*kept):
            low_grad, mixed_split, head_gain_part = attend_back(group, grad_mine, grad_other, *kept)
            return *attend_weights(low_grad, mixed_split, scale_one, grad_mine, grad_other, proj, tokens, normed), head_gain_part

        (results,) = beside(pair_out, out_sum, kernels=[(attended, kept)])
        return *results, pair_out.value, *out_sum.held, *out_sum.arrived

    attn_w_part, keep, give, attn_gain_part, head_gain_part, pair_out, *held = apart(
        attention, held, proj, cosine, sine, query_gain_wide, key_gain_wide, seg_rows, segment_row,
        raw, query_rot, key_rot, values, mixed_low,
    )
    attn_w_part, give, wide_got, feed_w_sums[1] = lax.optimization_barrier(
        (attn_w_part, give, wide_got, feed_w_sums[1])
    )
    down_got = swap(pick(feed_w_sums[1], 1 - side, 0), "fsdp", 1)
    attn_w_sum = lax.psum_scatter(attn_w_part, "fsdp", scatter_dimension=0, tiled=True)

    def last(keep, give, hidden_share, pair_out, hidden_grad_share, tokens, scale_one, *rest):
        gain_parts, (_, keep_first, _, keep_second, got_first, got_second) = rest[:4], rest[4:]
        out_sum = Job(line_scatter(*fold_line(keep_first, got_first, keep_second, got_second)))
        normed_sum = Job(plane_scatter(keep, give))
        gains = Job(sum_all(jnp.concatenate(gain_parts, axis=1)))
        beside(normed_sum, out_sum, gains)
        beside(normed_sum, gains)
        beside(normed_sum, gains)
        finish(gains)
        block_out = low(hidden_share + wide(pair_out) + out_sum.value)
        token_share = wide(share_of(tokens))
        scale_one_share = share_of(scale_one)
        tokens_grad = low(
            hidden_grad_share + norm_back(token_share, scale_one_share, normed_sum.value * wide(gain_attn))
        )
        return block_out, tokens_grad, gains.value

    block_out, tokens_grad, gain_sums = apart(
        last, keep, give, hidden_share, pair_out, hidden_grad_share, tokens, scale_one,
        attn_gain_part, ffn_gain_part, head_gain_part[:1], head_gain_part[1:], *held,
    )
    gain_sums, down_got = lax.optimization_barrier((gain_sums, down_got))
    feed_w_grads = feed_sums(side[None], feed_w_sums, (wide_got, down_got))
    attn_w_grad, (gate_w_grad, up_w_grad, down_w_grad) = lax.optimization_barrier((attn_w_sum, feed_w_grads))
    attn_w_grad = wide(attn_w_grad)
    out_w_grad = attn_w_grad[:, query_cols + 2 * key_cols :]
    ends = [0, model, 2 * model, 2 * model + HD, 2 * model + 2 * HD]
    ln1_grad, ln2_grad, query_gain_grad, key_gain_grad = (
        lax.dynamic_slice_in_dim(gain_sums[0, start:end], lax.axis_index("fsdp") * ((end - start) // size), (end - start) // size, 0)
        for start, end in zip(ends, ends[1:])
    )
    return (
        block_out,
        tokens_grad,
        ln1_grad,
        attn_w_grad[:, :query_cols],
        attn_w_grad[:, query_cols : query_cols + key_cols],
        attn_w_grad[:, query_cols + key_cols : query_cols + 2 * key_cols],
        query_gain_grad,
        key_gain_grad,
        out_w_grad,
        ln2_grad,
        gate_w_grad,
        up_w_grad,
        down_w_grad,
    )


def solution(mesh):
    in_specs = (
        P("fsdp", None),
        P("fsdp", None),
        P("fsdp"),
        P("fsdp", ("heads", "tensor")),
        P("fsdp", ("heads", "tensor")),
        P("fsdp", ("heads", "tensor")),
        P("fsdp"),
        P("fsdp"),
        P("fsdp", ("heads", "tensor")),
        P("fsdp"),
        P("fsdp", ("heads", "tensor")),
        P("fsdp", ("heads", "tensor")),
        P("fsdp", ("heads", "tensor")),
        P("fsdp", None),
    )
    out_specs = (
        P(("fsdp", "heads", "tensor"), None),
        P(("fsdp", "heads", "tensor"), None),
        P("fsdp"),
        P("fsdp", ("heads", "tensor")),
        P("fsdp", ("heads", "tensor")),
        P("fsdp", ("heads", "tensor")),
        P("fsdp"),
        P("fsdp"),
        P("fsdp", ("heads", "tensor")),
        P("fsdp"),
        P("fsdp", ("heads", "tensor")),
        P("fsdp", ("heads", "tensor")),
        P("fsdp", ("heads", "tensor")),
    )
    return jax.shard_map(
        per_device, mesh=mesh, in_specs=in_specs, out_specs=out_specs, check_vma=False
    )
```

```python
import functools

import jax
import jax.numpy as jnp
from jax import lax
from jax.experimental import pallas as pl
from jax.experimental.pallas import tpu as pltpu
from jax.sharding import PartitionSpec as P

HD = 128


EPSILON = 1e-06
THETA = 1000000.0
ROWS = 256
BAND = 512
PLANE = ("heads", "tensor")
SWAP = ((0, 1), (1, 0))
NEAR = ((0, 1), (1, 0), (2, 3), (3, 2))
FAR = ((0, 2), (2, 0), (1, 3), (3, 1))


def rms_parts(values):
    return lax.rsqrt(jnp.mean(values * values, axis=-1, keepdims=True) + EPSILON)


def norm_back(values, scale, upstream):
    return scale * upstream - values * scale**3 * jnp.mean(
        values * upstream, axis=-1, keepdims=True
    )


def contract(left, right, left_dim, right_dim):
    return lax.dot_general(
        left, right, (((left_dim,), (right_dim,)), ((), ())), preferred_element_type=jnp.float32
    )


def doc_positions(segment_row):
    places = jnp.arange(segment_row.shape[0], dtype=jnp.int32)
    previous = jnp.concatenate([segment_row[:1], segment_row[:-1]])
    starts = lax.cummax(jnp.where(segment_row != previous, places, 0), axis=0)
    return places - starts


def rope_tables(positions):
    frequency = THETA ** (-(jnp.arange(HD // 2, dtype=jnp.float32) * 2.0 / HD))
    angles = positions.astype(jnp.float32)[:, None] * frequency[None, :]
    cosine, sine = jnp.cos(angles), jnp.sin(angles)
    return (
        jnp.concatenate([cosine, cosine], axis=1),
        jnp.concatenate([-sine, sine], axis=1),
    )


def low(values):
    return values.astype(jnp.bfloat16)


def wide(values):
    return values.astype(jnp.float32)


def flip(axis, stride):
    return [(k, k ^ stride) for k in range(lax.axis_size(axis))]


def after(value, *others):
    return lax.optimization_barrier((value, *others))[0]


def apart(work, *args):
    zeros = [jnp.zeros(out.shape, out.dtype) for out in jax.eval_shape(work, *args)]
    return lax.cond(
        lax.axis_index("fsdp") < lax.axis_size("fsdp"), work, lambda *_: tuple(zeros), *args
    )


class Job:
    def __init__(self, steps):
        self.steps, self.moves, self.keep, self.held, self.value = steps, (), (), (), None
        self.resume(None)

    def resume(self, got):
        self.held, self.arrived = self.keep, got
        try:
            given = self.steps.send(got)
            self.moves, self.keep = given if isinstance(given, tuple) else (given, ())
        except StopIteration as end:
            self.moves, self.keep, self.value = (), (), end.value


def beside(*jobs, kernels=(), ready=()):
    jobs = [job for job in jobs if job.moves]
    ready = [job for job in ready if job.moves]
    given = [[move[0] for move in job.moves] for job in jobs], [args for _, args in kernels]
    arrays, args = lax.optimization_barrier(given)
    got = [
        [lax.ppermute(array, *move[1:]) for array, move in zip(held, job.moves)]
        for held, job in zip(arrays, jobs)
    ]
    results = [kernel[0](*own) for own, kernel in zip(args, kernels)]
    later = [[move[0] for move in job.moves] for job in ready]
    got, results, later = lax.optimization_barrier((got, results, later))
    for job, arrays in zip(ready, later):
        job.moves = [(array, *move[1:]) for array, move in zip(arrays, job.moves)]
    for job, arrived in zip(jobs, got):
        job.resume(arrived)
    return results


def finish(*jobs):
    while any(job.moves for job in jobs):
        beside(*jobs)


def bits(axis):
    size = lax.axis_size(axis)
    return [1 << k for k in range(size.bit_length() - 1)]


def swap(array, axis, stride):
    return lax.ppermute(array, axis, flip(axis, stride))


def bit(axis, stride):
    return (lax.axis_index(axis) // stride) % 2


def line_gather(block, strides):
    block = block[None]
    for stride in strides:
        block = both(block, swap(block, "fsdp", stride), bit("fsdp", stride), 0)
        block = block.reshape(-1, *block.shape[2:])
    return block


def pick(array, index, axis):
    return lax.dynamic_index_in_dim(array, index, axis, keepdims=False)


def both(mine, got, index, axis):
    lower = jnp.where(index == 0, mine, got)
    upper = jnp.where(index == 0, got, mine)
    return jnp.stack([lower, upper], axis=axis)


def join_kernel(*refs):
    first = 0
    for part in refs[:-1]:
        refs[-1][:, first : first + part.shape[1]] = part[...]
        first += part.shape[1]


def joined_columns(*parts):
    shape = (parts[0].shape[0], sum(part.shape[1] for part in parts))
    return pl.pallas_call(
        join_kernel,
        in_specs=[pl.BlockSpec(memory_space=pltpu.VMEM)] * len(parts),
        out_specs=pl.BlockSpec(memory_space=pltpu.VMEM),
        out_shape=jax.ShapeDtypeStruct(shape, parts[0].dtype),
        compiler_params=call_params(16),
        cost_estimate=cheap(),
        name="join",
    )(*parts)


def widen_kernel(source_ref, *outs):
    first = 0
    for out in outs:
        out[...] = wide(source_ref[:, first : first + out.shape[1]])
        first += out.shape[1]


def widened(source, widths):
    rows = source.shape[0]
    return pl.pallas_call(
        widen_kernel,
        in_specs=[pl.BlockSpec(memory_space=pltpu.VMEM)],
        out_specs=[pl.BlockSpec(memory_space=pltpu.VMEM)] * len(widths),
        out_shape=[jax.ShapeDtypeStruct((rows, width), jnp.float32) for width in widths],
        compiler_params=call_params(16),
        cost_estimate=cheap(),
        name="widen",
    )(source)


def position():
    heads = lax.axis_index("heads")
    return jnp.stack([lax.axis_index("tensor"), heads % 2, heads // 2]).astype(jnp.int32)


def vmem_call(kernel, name, megabytes, out_shape, *args):
    return pl.pallas_call(
        kernel,
        in_specs=[pl.BlockSpec(memory_space=pltpu.SMEM)]
        + [pl.BlockSpec(memory_space=pltpu.VMEM)] * len(args),
        out_specs=[pl.BlockSpec(memory_space=pltpu.VMEM)] * len(out_shape),
        out_shape=[jax.ShapeDtypeStruct(shape, jnp.bfloat16) for shape in out_shape],
        compiler_params=call_params(megabytes),
        cost_estimate=cheap(),
        name=name,
    )(position(), *args)


def fold_chip_kernel(position_ref, keep_ref, got_ref, give_first, keep_first, give_second, keep_second):
    x, y = position_ref[1], position_ref[2]
    middle = keep_ref.shape[-1] // 2
    first, second = slice(0, middle), slice(middle, 2 * middle)

    def summed(row, column, cols):
        return low(wide(keep_ref[row, column, :, cols]) + wide(got_ref[row, column, :, cols]))

    for k in range(2):
        give_first[k] = summed(k, 1 - x, first)
        keep_first[k] = summed(k, x, first)
        give_second[k] = summed(1 - y, k, second)
        keep_second[k] = summed(y, k, second)


def fold_chip(keep, got):
    rows, width = keep.shape
    shape = (2, 2, rows // 4, width)
    return vmem_call(
        fold_chip_kernel, "fold_chip", 24, [(2, rows // 4, width // 2)] * 4, keep.reshape(shape), got.reshape(shape)
    )


def fold_line_kernel(
    position_ref, keep_first_ref, got_first_ref, keep_second_ref, got_second_ref, give_first, keep_first, give_second, keep_second
):
    x, y = position_ref[1], position_ref[2]
    for at, keep_ref, got_ref, give, keep in (
        (y, keep_first_ref, got_first_ref, give_first, keep_first),
        (x, keep_second_ref, got_second_ref, give_second, keep_second),
    ):
        give[...] = low(wide(keep_ref[1 - at]) + wide(got_ref[1 - at]))
        keep[...] = low(wide(keep_ref[at]) + wide(got_ref[at]))


def fold_line(keep_first, got_first, keep_second, got_second):
    shape = keep_first.shape[1:]
    return vmem_call(
        fold_line_kernel, "fold_line", 16, [shape] * 4, keep_first, got_first, keep_second, got_second
    )


def fold_end_kernel(position_ref, keep_first_ref, got_first_ref, keep_second_ref, got_second_ref, out_ref):
    middle = keep_first_ref.shape[-1]
    out_ref[:, :middle] = low(wide(keep_first_ref[...]) + wide(got_first_ref[...]))
    out_ref[:, middle:] = low(wide(keep_second_ref[...]) + wide(got_second_ref[...]))


def fold_end(keep_first, got_first, keep_second, got_second):
    rows, width = keep_first.shape
    (out,) = vmem_call(
        fold_end_kernel, "fold_end", 16, [(rows, 2 * width)], keep_first, got_first, keep_second, got_second
    )
    return out


def share_back_kernel(
    eps, first_ref, got_first_ref, second_ref, got_second_ref, pair_upper_ref, pair_lower_ref, hidden_ref, cotangent_ref, gain_ref, out_ref, low_ref, part_ref
):
    middle = first_ref.shape[-1]
    hidden = hidden_ref[...]
    scale = lax.rsqrt(jnp.mean(hidden * hidden, axis=-1, keepdims=True) + eps)
    grads = []
    for k, (mine, got) in enumerate(((first_ref, got_first_ref), (second_ref, got_second_ref))):
        cols = slice(k * middle, (k + 1) * middle)
        pair = jnp.concatenate([pair_upper_ref[:, cols], pair_lower_ref[:, cols]], axis=0)
        grads.append(wide(mine[...]) + wide(got[...]) + wide(pair))
    grad = jnp.concatenate(grads, axis=1)
    part_ref[...] = jnp.sum(grad * hidden * scale, axis=0, keepdims=True)
    out = wide(cotangent_ref[...]) + norm_back(hidden, scale, grad * gain_ref[...])
    out_ref[...] = out
    low_ref[...] = low(out)


def share_back(first, got_first, second, got_second, pair_upper, pair_lower, hidden, cotangent, gain):
    rows, model = hidden.shape
    args = (first, got_first, second, got_second, pair_upper, pair_lower, hidden, cotangent, gain)
    return pl.pallas_call(
        functools.partial(share_back_kernel, EPSILON),
        in_specs=[pl.BlockSpec(memory_space=pltpu.VMEM)] * len(args),
        out_specs=[pl.BlockSpec(memory_space=pltpu.VMEM)] * 3,
        out_shape=[
            jax.ShapeDtypeStruct((rows, model), jnp.float32),
            jax.ShapeDtypeStruct((rows, model), jnp.bfloat16),
            jax.ShapeDtypeStruct((1, model), jnp.float32),
        ],
        compiler_params=call_params(24),
        cost_estimate=cheap(),
        name="share_back",
    )(*args)


def plane_scatter(keep, give, rounded=False):
    (got,) = yield [(give, "tensor", SWAP)]
    folded = fold_chip(keep, got)
    return (yield from chip_scatter(*folded, rounded))


def chip_scatter(give_first, keep_first, give_second, keep_second, rounded=False):
    held = (give_first, keep_first, give_second, keep_second)
    got = yield [(give_first, "heads", NEAR), (give_second, "heads", FAR)], held
    return (yield from line_scatter(*fold_line(keep_first, got[0], keep_second, got[1]), rounded))


def line_scatter(give_first, keep_first, give_second, keep_second, rounded=False):
    held = (give_first, keep_first, give_second, keep_second)
    got = yield [(give_first, "heads", FAR), (give_second, "heads", NEAR)], held
    if rounded:
        return fold_end(keep_first, got[0], keep_second, got[1])
    first = wide(keep_first) + wide(got[0])
    second = wide(keep_second) + wide(got[1])
    return jnp.concatenate([first, second], axis=-1)


def open_line_kernel(position_ref, first_ref, got_first_ref, second_ref, got_second_ref, first, second):
    x, y = position_ref[1], position_ref[2]
    first[y] = first_ref[...]
    first[1 - y] = got_first_ref[...]
    second[x] = second_ref[...]
    second[1 - x] = got_second_ref[...]


def open_chip_kernel(position_ref, first_ref, got_first_ref, second_ref, got_second_ref, out_ref):
    x, y = position_ref[1], position_ref[2]
    lead, middle = first_ref.shape[1], first_ref.shape[-1]
    for k in range(lead):
        for j in range(2):
            out_ref[k, j, x, :, :middle] = first_ref[j, k]
            out_ref[k, j, 1 - x, :, :middle] = got_first_ref[j, k]
            out_ref[k, y, j, :, middle:] = second_ref[j, k]
            out_ref[k, 1 - y, j, :, middle:] = got_second_ref[j, k]


def plane_gather(share):
    lead, rows, width = share.shape
    first, second = share[..., : width // 2], share[..., width // 2 :]
    got = yield [(first, "heads", FAR), (second, "heads", NEAR)], (first, second)
    first, second = vmem_call(
        open_line_kernel, "open_line", 16, [(2, lead, rows, width // 2)] * 2, first, got[0], second, got[1]
    )
    got = yield [(first, "heads", NEAR), (second, "heads", FAR)], (first, second)
    return (yield from core_gather(first, second, *got))


def core_gather(first, second, got_first, got_second):
    _, lead, rows, middle = first.shape
    (mine,) = vmem_call(
        open_chip_kernel, "open_chip", 24, [(lead, 2, 2, rows, 2 * middle)], first, got_first, second, got_second
    )
    mine = mine.reshape(lead, 4 * rows, 2 * middle)
    (other,) = yield [(mine, "tensor", SWAP)]
    return mine, other


def pair_swap(array, pieces=1):
    rows = array.shape[0] // pieces
    got = []
    for k in range(pieces):
        got += yield [(array[k * rows : (k + 1) * rows], "fsdp", flip("fsdp", 1))]
    return jnp.concatenate(got, axis=0) if pieces > 1 else got[0]


def pair_gather(share, pieces):
    got = yield from pair_swap(share, pieces)
    return (yield from plane_gather(got[None]))


def sum_all(values):
    for axis in ("tensor", "heads", "fsdp"):
        strides = bits(axis)
        if axis == "fsdp" and len(strides) > 1:
            strides = [strides[0] + strides[1]] + strides[1:]
        for stride in strides:
            (got,) = yield [(values, axis, flip(axis, stride))]
            values = values + got
    return values


def alike():
    return [list(range(k, lax.axis_size("fsdp"), 2)) for k in range(2)]


def rotate(values, cosine, sine):
    return values * cosine + pltpu.roll(values, HD // 2, 1) * sine


def call_params(megabytes):
    return pltpu.CompilerParams(vmem_limit_bytes=megabytes << 20)


def cheap():
    return pl.CostEstimate(flops=1000, bytes_accessed=1000, transcendentals=0)


def key_blocks(at, count):
    return max(0, at - BAND // ROWS), at + 1


def masked_probs(query, keys, seg_rows, seg_keys, first_row, first_key):
    scores = contract(query, keys, 1, 1) * HD**-0.5
    rows = first_row + lax.broadcasted_iota(jnp.int32, scores.shape, 0)
    cols = first_key + lax.broadcasted_iota(jnp.int32, scores.shape, 1)
    scores = jnp.where((rows >= cols) & (seg_rows == seg_keys), scores, -1e30)
    expo = jnp.exp(scores - jnp.max(scores, axis=-1, keepdims=True))
    return expo / jnp.sum(expo, axis=-1, keepdims=True)


def by_core(core, block):
    middle = block.shape[0] // 2
    lower, upper = block[:middle], block[middle:]
    first = core == 0
    return jnp.where(first, lower, upper), jnp.where(first, upper, lower)


def joined(core, mine, other):
    first = core == 0
    return jnp.concatenate([jnp.where(first, mine, other), jnp.where(first, other, mine)], axis=0)


def attend_kernel(
    group,
    normed_ref,
    proj_ref,
    cosine_ref,
    sine_ref,
    query_gain_ref,
    key_gain_ref,
    seg_rows_ref,
    seg_keys_ref,
    raw_ref,
    query_ref,
    key_ref,
    value_ref,
    mixed_ref,
    keys,
    values,
):
    length, kv_cols = keys.shape
    kv_local = kv_cols // HD
    query_cols = kv_cols * group
    count = length // ROWS
    step = pl.program_id(0)
    raw = jnp.dot(normed_ref[...], proj_ref[...], preferred_element_type=jnp.float32)
    raw_ref[...] = raw[:, : query_cols + kv_cols]
    cosine, sine = cosine_ref[...], sine_ref[...]
    here = pl.ds(pl.multiple_of(step * ROWS, ROWS), ROWS)

    def turned(head, gain_ref):
        one = raw[:, head * HD : (head + 1) * HD]
        return low(rotate(one * rms_parts(one) * gain_ref[...], cosine, sine))

    for kv in range(kv_local):
        at = slice(kv * HD, (kv + 1) * HD)
        new_keys = turned(query_cols // HD + kv, key_gain_ref)
        new_values = low(raw[:, query_cols + kv_cols + kv * HD : query_cols + kv_cols + (kv + 1) * HD])
        key_ref[:, at] = new_keys
        value_ref[:, at] = new_values
        keys[here, at] = new_keys
        values[here, at] = new_values
    for head in range(query_cols // HD):
        query_ref[:, head * HD : (head + 1) * HD] = turned(head, query_gain_ref)

    for at in range(count):

        @pl.when(step == at)
        def _():
            lower, upper = key_blocks(at, count)
            span = slice(lower * ROWS, upper * ROWS)
            for head in range(query_cols // HD):
                cols = slice(head * HD, (head + 1) * HD)
                kv = slice((head // group) * HD, (head // group + 1) * HD)
                probs = masked_probs(
                    query_ref[:, cols],
                    keys[span, kv],
                    seg_rows_ref[...],
                    seg_keys_ref[:, span],
                    at * ROWS,
                    lower * ROWS,
                )
                mixed_ref[:, cols] = low(
                    jnp.dot(low(probs), values[span, kv], preferred_element_type=jnp.float32)
                )


def attend(group, normed, proj, cosine, sine, query_gain, key_gain, seg_rows, segment_row):
    length, model = normed.shape
    kv_cols = proj.shape[1] // (2 * group + 2)
    query_cols = kv_cols * group

    def rows(width):
        return pl.BlockSpec((ROWS, width), lambda i: (i, 0))

    def whole(array):
        return pl.BlockSpec(array.shape, lambda i: (0, 0))

    seg_keys = segment_row[None, :]
    args = (normed, proj, cosine, sine, query_gain[None], key_gain[None], seg_rows, seg_keys)
    outs = [
        (query_cols + kv_cols, jnp.float32),
        (query_cols, jnp.bfloat16),
        (kv_cols, jnp.bfloat16),
        (kv_cols, jnp.bfloat16),
        (query_cols, jnp.bfloat16),
    ]
    return pl.pallas_call(
        functools.partial(attend_kernel, group),
        grid=(length // ROWS,),
        in_specs=[
            rows(model),
            pl.BlockSpec((model, query_cols + 2 * kv_cols), lambda i: (0, 0)),
            rows(HD),
            rows(HD),
            whole(args[4]),
            whole(args[5]),
            rows(1),
            whole(seg_keys),
        ],
        out_specs=[rows(width) for width, _ in outs],
        out_shape=[jax.ShapeDtypeStruct((length, width), kind) for width, kind in outs],
        scratch_shapes=[
            pltpu.VMEM((length, kv_cols), jnp.bfloat16),
            pltpu.VMEM((length, kv_cols), jnp.bfloat16),
        ],
        compiler_params=call_params(40),
        cost_estimate=cheap(),
        name="attend",
    )(*args)


def attend_out_kernel(position_ref, mixed_ref, proj_ref, keep_ref, give_ref):
    keep_ref[...], give_ref[...] = by_core(
        position_ref[0], low(contract(mixed_ref[...], proj_ref[...], 1, 1))
    )


def attend_out(mixed, proj):
    length, cols = mixed.shape
    model = proj.shape[0]
    return pl.pallas_call(
        attend_out_kernel,
        grid=(length // ROWS,),
        in_specs=[
            pl.BlockSpec(memory_space=pltpu.SMEM),
            pl.BlockSpec((ROWS, cols), lambda i: (i, 0)),
            pl.BlockSpec((model, cols), lambda i: (0, proj.shape[1] // cols - 1)),
        ],
        out_specs=[pl.BlockSpec((ROWS // 2, model), lambda i: (i, 0))] * 2,
        out_shape=[jax.ShapeDtypeStruct((length // 2, model), jnp.bfloat16)] * 2,
        compiler_params=call_params(24),
        cost_estimate=cheap(),
        name="attend_out",
    )(position(), mixed, proj)


def attend_back_kernel(
    group,
    grad_mine_ref,
    grad_other_ref,
    out_proj_ref,
    cosine_ref,
    sine_ref,
    query_gain_ref,
    key_gain_ref,
    seg_rows_ref,
    seg_keys_ref,
    raw_ref,
    query_ref,
    key_ref,
    value_ref,
    mixed_ref,
    position_ref,
    low_ref,
    mixed_split_ref,
    head_gain_ref,
    mixed_grad,
    query_sum,
    key_sum,
    value_sum,
):
    length, kv_cols = key_sum.shape
    query_cols = kv_cols * group
    count = length // ROWS
    share = ROWS // 2
    core = position_ref[0]
    for k, ref in enumerate((grad_mine_ref, grad_other_ref)):
        part = low(jnp.dot(ref[...], out_proj_ref[...], preferred_element_type=jnp.float32))
        for at in range(count):
            start = pl.multiple_of(at * ROWS + (core + k - 2 * k * core) * share, share)
            mixed_grad[pl.ds(start, share), :] = part[at * share : (at + 1) * share]
            mixed_split_ref[k, at * share : (at + 1) * share, :] = mixed_ref[pl.ds(start, share), :]
    key_sum[...] = jnp.zeros_like(key_sum)
    value_sum[...] = jnp.zeros_like(value_sum)
    for at in range(count):
        here = slice(at * ROWS, (at + 1) * ROWS)
        lower, upper = key_blocks(at, count)
        span = slice(lower * ROWS, upper * ROWS)
        for head in range(query_cols // HD):
            cols = slice(head * HD, (head + 1) * HD)
            kv = slice((head // group) * HD, (head // group + 1) * HD)
            query = query_ref[here, cols]
            grad = mixed_grad[here, cols]
            probs = masked_probs(
                query,
                key_ref[span, kv],
                seg_rows_ref[here, :],
                seg_keys_ref[:, span],
                at * ROWS,
                lower * ROWS,
            )
            prob_grad = contract(grad, value_ref[span, kv], 1, 1)
            row_inner = jnp.sum(probs * prob_grad, axis=-1, keepdims=True)
            score_grad = low(HD**-0.5 * probs * (prob_grad - row_inner))
            query_sum[here, cols] = jnp.dot(
                score_grad, key_ref[span, kv], preferred_element_type=jnp.float32
            )
            key_sum[span, kv] += contract(score_grad, query, 0, 0)
            value_sum[span, kv] += contract(low(probs), grad, 0, 0)

    head_gain_ref[...] = jnp.zeros_like(head_gain_ref)
    for at in range(count):
        here = slice(at * ROWS, (at + 1) * ROWS)
        cosine, sine = cosine_ref[here, :], -sine_ref[here, :]
        for head in range((query_cols + kv_cols) // HD):
            cols = slice(head * HD, (head + 1) * HD)
            own = slice(head * HD - query_cols, (head + 1) * HD - query_cols)
            is_query = head * HD < query_cols
            turned = rotate(query_sum[here, cols] if is_query else key_sum[here, own], cosine, sine)
            raw = raw_ref[here, cols]
            scale = rms_parts(raw)
            row = 0 if is_query else 1
            head_gain_ref[row : row + 1, :] += jnp.sum(turned * raw * scale, axis=0, keepdims=True)
            gain = query_gain_ref[...] if is_query else key_gain_ref[...]
            low_ref[here, cols] = low(norm_back(raw, scale, turned * gain))
        low_ref[here, query_cols + kv_cols :] = low(value_sum[here, :])


def attend_back(
    group, grad_mine, grad_other, proj, cosine, sine, query_gain, key_gain, seg_rows, segment_row, raw, query, key, value, mixed
):
    length, query_cols, kv_cols = query.shape[0], query.shape[1], key.shape[1]
    args = (
        grad_mine, grad_other, proj, cosine, sine, query_gain[None], key_gain[None],
        seg_rows, segment_row[None, :], raw, query, key, value, mixed, position(),
    )
    out_shape = [
        jax.ShapeDtypeStruct((length, query_cols + 2 * kv_cols), jnp.bfloat16),
        jax.ShapeDtypeStruct((2, length // 2, query_cols), jnp.bfloat16),
        jax.ShapeDtypeStruct((2, HD), jnp.float32),
    ]

    def whole(array):
        return pl.BlockSpec(array.shape, lambda i: (0,) * len(array.shape), pipeline_mode=pl.Buffered(1))

    return pl.pallas_call(
        functools.partial(attend_back_kernel, group),
        grid=(1,),
        in_specs=[whole(grad_mine), whole(grad_other)]
        + [pl.BlockSpec((proj.shape[0], query_cols), lambda i: (0, proj.shape[1] // query_cols - 1))]
        + [whole(array) for array in args[3:-1]]
        + [pl.BlockSpec(memory_space=pltpu.SMEM)],
        out_specs=[whole(out) for out in out_shape],
        out_shape=out_shape,
        scratch_shapes=[
            pltpu.VMEM((length, query_cols), jnp.bfloat16),
            pltpu.VMEM((length, query_cols), jnp.float32),
            pltpu.VMEM((length, kv_cols), jnp.float32),
            pltpu.VMEM((length, kv_cols), jnp.float32),
        ],
        compiler_params=call_params(40),
        cost_estimate=cheap(),
        name="attend_back",
    )(*args)


def attend_weights_kernel(
    position_ref, low_ref, mixed_ref, scale_ref, grad_mine_ref, grad_other_ref, proj_ref, tokens_ref, normed_ref,
    weight_ref, keep_ref, give_ref, gain_ref,
):
    split = low_ref.shape[1]
    share = ROWS // 2
    gain = jnp.zeros_like(gain_ref)
    for at in range(low_ref.shape[0] // ROWS):
        here = slice(at * ROWS, (at + 1) * ROWS)
        rows = slice(at * share, (at + 1) * share)
        part = contract(low_ref[here, :], proj_ref[...], 1, 1)
        keep_ref[rows, :], give_ref[rows, :] = by_core(position_ref[0], low(part))
        gain += jnp.sum(part * wide(tokens_ref[here, :]) * scale_ref[here, :], axis=0, keepdims=True)
    gain_ref[...] = gain
    weight_ref[:, :split] = low(contract(normed_ref[...], low_ref[...], 0, 0))
    weight_ref[:, split:] = low(
        contract(grad_mine_ref[...], mixed_ref[0], 0, 0) + contract(grad_other_ref[...], mixed_ref[1], 0, 0)
    )


def attend_weights(low_grad, mixed, scale, grad_mine, grad_other, proj, tokens, normed):
    length, model = tokens.shape
    split = low_grad.shape[1]
    width = split + mixed.shape[-1]
    cols = min(512, model)

    def whole(array):
        return pl.BlockSpec(array.shape, lambda i: (0,) * array.ndim, pipeline_mode=pl.Buffered(1))

    def columns(rows):
        return pl.BlockSpec((rows, cols), lambda i: (0, i))

    return pl.pallas_call(
        attend_weights_kernel,
        grid=(model // cols,),
        in_specs=[
            pl.BlockSpec(memory_space=pltpu.SMEM),
            whole(low_grad),
            whole(mixed),
            whole(scale),
            columns(length // 2),
            columns(length // 2),
            pl.BlockSpec((cols, split), lambda i: (i, 0)),
            columns(length),
            columns(length),
        ],
        out_specs=[
            pl.BlockSpec((cols, width), lambda i: (i, 0)),
            columns(length // 2),
            columns(length // 2),
            columns(1),
        ],
        out_shape=[
            jax.ShapeDtypeStruct((model, width), jnp.bfloat16),
            jax.ShapeDtypeStruct((length // 2, model), jnp.bfloat16),
            jax.ShapeDtypeStruct((length // 2, model), jnp.bfloat16),
            jax.ShapeDtypeStruct((1, model), jnp.float32),
        ],
        compiler_params=call_params(40),
        cost_estimate=cheap(),
        name="attend_weights",
    )(position(), low_grad, mixed, scale, grad_mine, grad_other, proj, tokens, normed)


def prepare_kernel(tokens_ref, gain_ref, seg_ref, normed_ref, scale_ref, seg_rows_ref):
    block_in = wide(tokens_ref[...])
    scale = rms_parts(block_in)
    scale_ref[...] = scale
    normed_ref[...] = low(block_in * scale * gain_ref[...])
    seg_rows_ref[...] = seg_ref[...]


def prepare(tokens, gain, seg_rows):
    length, model = tokens.shape

    def rows(width):
        return pl.BlockSpec((ROWS, width), lambda i: (i, 0))

    return pl.pallas_call(
        prepare_kernel,
        grid=(length // ROWS,),
        in_specs=[rows(model), pl.BlockSpec((1, model), lambda i: (0, 0)), rows(1)],
        out_specs=[rows(model), rows(1), rows(1)],
        out_shape=[
            jax.ShapeDtypeStruct((length, model), jnp.bfloat16),
            jax.ShapeDtypeStruct((length, 1), jnp.float32),
            jax.ShapeDtypeStruct((length, 1), jnp.int32),
        ],
        compiler_params=call_params(24),
        cost_estimate=pl.CostEstimate(flops=20_000_000_000, bytes_accessed=20_000_000, transcendentals=0),
        name="prepare",
    )(tokens, gain[None], seg_rows)


def feed_kernel(*refs):
    sources, (proj_hbm, *results, normed, cotangent, proj, arrive) = refs[:8], refs[8:]
    acts, grads = results[:2], results[2:]
    half = acts[0].shape[-1]
    rows = sources[0].shape[0]
    tile = min(256, rows)

    def fetch(source, target, k):
        copy = pltpu.make_async_copy(source, target, arrive.at[k])
        copy.start()
        return copy

    loads = [fetch(proj_hbm, proj, 8)]
    for k in range(4):
        loads.append(fetch(sources[k], normed.at[k], 2 * k))
        loads.append(fetch(sources[4 + k], cotangent.at[k], 2 * k + 1))
    loads[0].wait()
    for k in range(4):
        loads[2 * k + 1].wait()
        loads[2 * k + 2].wait()
        act_ref, grad_ref = acts[k // 2], grads[k // 2]

        @pl.loop(0, rows // tile)
        def _(step):
            here = pl.ds(pl.multiple_of(step * tile, tile), tile)
            gate_up = jnp.dot(normed[k, here, :], proj[:, : 2 * half], preferred_element_type=jnp.float32)
            gate, up = gate_up[:, :half], gate_up[:, half:]
            act_grad = jnp.dot(cotangent[k, here, :], proj[:, 2 * half :], preferred_element_type=jnp.float32)
            sigmoid = jax.nn.sigmoid(gate)
            silu = gate * sigmoid
            act_ref[k % 2, here, :] = low(silu * up)
            grad_ref[k % 2, here, :half] = low(act_grad * up * sigmoid * (1.0 + gate * (1.0 - sigmoid)))
            grad_ref[k % 2, here, half:] = low(act_grad * silu)


def feed(normed, cotangent, proj):
    rows, model = normed[0].shape
    half = proj.shape[1] // 3
    widths = (half, half, 2 * half, 2 * half)
    return pl.pallas_call(
        feed_kernel,
        in_specs=[pl.BlockSpec(memory_space=pl.ANY)] * 9,
        out_specs=[pl.BlockSpec(memory_space=pltpu.VMEM)] * 4,
        out_shape=[jax.ShapeDtypeStruct((2, rows, w), jnp.bfloat16) for w in widths],
        scratch_shapes=[
            pltpu.VMEM((4, rows, model), jnp.bfloat16),
            pltpu.VMEM((4, rows, model), jnp.bfloat16),
            pltpu.VMEM(proj.shape, jnp.bfloat16),
            pltpu.SemaphoreType.DMA((9,)),
        ],
        compiler_params=call_params(48),
        cost_estimate=cheap(),
        name="feed",
    )(*normed, *cotangent, proj)


def feed_model_kernel(act_ref, grad_ref, proj_ref, keep_ref, give_ref, keep_out_ref, give_out_ref):
    half = act_ref.shape[-1]
    for k, (out_ref, out_out_ref) in enumerate(((keep_ref, keep_out_ref), (give_ref, give_out_ref))):
        out_ref[...] = low(contract(grad_ref[k], proj_ref[:, : 2 * half], 1, 1))
        out_out_ref[...] = low(contract(act_ref[k], proj_ref[:, 2 * half :], 1, 1))


def feed_model(act, grad, proj):
    _, rows, half = act.shape
    model = proj.shape[0]
    tile = min(256, rows)
    return pl.pallas_call(
        feed_model_kernel,
        grid=(rows // tile,),
        in_specs=[
            pl.BlockSpec((2, tile, half), lambda i: (0, i, 0)),
            pl.BlockSpec((2, tile, 2 * half), lambda i: (0, i, 0)),
            pl.BlockSpec(proj.shape, lambda i: (0, 0), pipeline_mode=pl.Buffered(1)),
        ],
        out_specs=[pl.BlockSpec((tile, model), lambda i: (i, 0))] * 4,
        out_shape=[jax.ShapeDtypeStruct((rows, model), jnp.bfloat16)] * 4,
        compiler_params=call_params(40),
        cost_estimate=cheap(),
        name="feed_model",
    )(act, grad, proj)


def feed_weights_kernel(*refs):
    normed, cotangent, grad, act, (wide_ref, out_ref) = refs[:4], refs[4:8], refs[8:10], refs[10:12], refs[12:]
    wide_ref[...] = low(
        sum(contract(normed[k][...], grad[k // 2][k % 2], 0, 0) for k in range(4))
    )
    out_ref[...] = low(
        sum(contract(cotangent[k][...], act[k // 2][k % 2], 0, 0) for k in range(4))
    )


def feed_weights(normed, cotangent, grad, act):
    rows, model = normed[0].shape
    widths = grad[0].shape[-1], act[0].shape[-1]
    cols = min(512, model)

    def whole(array):
        return pl.BlockSpec(array.shape, lambda i: (0, 0, 0), pipeline_mode=pl.Buffered(1))

    return pl.pallas_call(
        feed_weights_kernel,
        grid=(model // cols,),
        in_specs=[pl.BlockSpec((rows, cols), lambda i: (0, i))] * 8 + [whole(a) for a in (*grad, *act)],
        out_specs=[pl.BlockSpec((cols, width), lambda i: (i, 0)) for width in widths],
        out_shape=[jax.ShapeDtypeStruct((model, width), jnp.bfloat16) for width in widths],
        compiler_params=call_params(48),
        cost_estimate=cheap(),
        name="feed_weights",
    )(*normed, *cotangent, *grad, *act)


def feed_sums_kernel(side_ref, *refs):
    sources, outs = refs[:4], refs[4:]
    half = outs[0].shape[1]
    mine = pl.program_id(0) == side_ref[0]
    for (wide_ref, down_ref), keep in ((sources[:2], mine), (sources[2:], jnp.logical_not(mine))):

        @pl.when(keep)
        def _():
            for k in range(2):
                outs[k][...] = wide(wide_ref[:, k * half : (k + 1) * half])
            outs[2][...] = wide(down_ref[...])


def feed_sums(side, own, other):
    rows, half = other[1].shape
    return pl.pallas_call(
        feed_sums_kernel,
        grid_spec=pltpu.PrefetchScalarGridSpec(
            num_scalar_prefetch=1,
            grid=(2,),
            in_specs=[pl.BlockSpec((None, rows, w), lambda i, side: (side[0], 0, 0)) for w in (2 * half, half)]
            + [pl.BlockSpec((rows, w), lambda i, side: (0, 0)) for w in (2 * half, half)],
            out_specs=[pl.BlockSpec((rows, half), lambda i, side: (0, i))] * 3,
        ),
        out_shape=[jax.ShapeDtypeStruct((rows, 2 * half), jnp.float32)] * 3,
        compiler_params=call_params(32),
        cost_estimate=cheap(),
        name="feed_sums",
    )(side, *own, *other)


def per_device(
    tokens,
    segments,
    ln1_gain,
    w_query,
    w_key,
    w_value,
    query_gain,
    key_gain,
    w_out,
    ln2_gain,
    w_gate,
    w_up,
    w_down,
    cotangent,
):
    length, model = tokens.shape
    query_cols, key_cols = w_query.shape[1], w_key.shape[1]
    query_heads = query_cols // HD
    kv_local = key_cols // HD
    group = query_heads // kv_local
    size = lax.axis_size("fsdp")
    shard = model // size
    hidden = w_gate.shape[1]
    half = hidden // 2
    strides = bits("fsdp")
    group_size = lax.axis_size(PLANE)
    share_rows = length // group_size
    share_start = lax.axis_index(PLANE) * share_rows
    segment_row = segments[0]

    def share_of(array):
        return lax.dynamic_slice_in_dim(array, share_start, share_rows, 0)

    block = joined_columns(w_query, w_key, w_value, w_out)
    proj = lax.all_gather(block, "fsdp", axis=0, tiled=True)
    side = bit("fsdp", 1)

    def half_of(which):
        return jnp.concatenate(
            [lax.dynamic_slice_in_dim(w, which * half, half, 1) for w in (w_gate, w_up, w_down)], axis=1
        )

    got = swap(after(half_of(1 - side), proj), "fsdp", 1)
    feed_block = both(half_of(side), got, side, 0)

    gains = line_gather(after(jnp.concatenate([ln1_gain, ln2_gain, query_gain, key_gain]), block), strides)
    gain_attn = gains[:, :shard].reshape(model)
    gain_ffn = gains[:, shard : 2 * shard].reshape(model)
    head_part = HD // size
    query_norm = gains[:, 2 * shard : 2 * shard + head_part].reshape(HD)
    key_norm = gains[:, 2 * shard + head_part :].reshape(HD)

    cosine, sine = rope_tables(doc_positions(segment_row))
    normed, scale_one, seg_rows = prepare(tokens, wide(gain_attn), segment_row[:, None])
    query_gain_wide, key_gain_wide = wide(query_norm), wide(key_norm)
    by_chip = cotangent.reshape(4, 2, share_rows, model)
    core = lax.axis_index("tensor")
    own_cot = [pick(by_chip, k, 1).reshape(length // 2, model) for k in (core, 1 - core)]
    own_cot, normed = lax.optimization_barrier((own_cot, normed))
    raw, query_rot, key_rot, values, mixed_low = attend(
        group, normed, proj, cosine, sine, query_gain_wide, key_gain_wide, seg_rows, segment_row
    )
    out_keep, out_give = attend_out(mixed_low, proj)
    out_got = swap(out_give, "tensor", 1)
    out_got, feed_block = lax.optimization_barrier((out_got, feed_block))
    feed_proj = lax.all_gather(
        feed_block, "fsdp", axis=0, tiled=True, axis_index_groups=alike()
    ).reshape(model, -1)

    def middle(tokens, cotangent, out_keep, out_got):
        cot = Job(pair_gather(share_of(cotangent), 2))
        out_sum = Job(chip_scatter(*fold_chip(out_keep, out_got)))
        beside(out_sum, cot)
        beside(out_sum, cot)
        hidden_share = wide(share_of(tokens)) + out_sum.value
        scale_share = rms_parts(hidden_share)
        normed_share = low(hidden_share * scale_share * wide(gain_ffn))
        gather = Job(plane_gather(normed_share[None]))
        pair_share = Job(pair_swap(normed_share, 2))
        beside(pair_share, gather, cot)
        beside(pair_share, gather)
        pair_gather_x = Job(plane_gather(pair_share.value[None]))
        beside(pair_gather_x, cot, gather)
        beside(pair_gather_x, cot)
        finish(pair_gather_x, cot, gather)
        arrays = (*gather.value, *pair_gather_x.value, *cot.value)
        return hidden_share, scale_share, *(array[0] for array in arrays)

    hidden_share, scale_share, *parts = apart(middle, tokens, cotangent, out_keep, out_got)
    own_normed, pair_normed, pair_cot = parts[:2], parts[2:4], parts[4:]

    act, pair_act, grad, pair_grad = feed((*own_normed, *pair_normed), (*own_cot, *pair_cot), feed_proj)
    pair_parts = feed_model(pair_act, pair_grad, feed_proj)
    pair_sum = Job(plane_scatter(*pair_parts[:2]))
    (own_parts,) = beside(pair_sum, kernels=[(feed_model, (act, grad, feed_proj))])
    weight_args = ((*own_normed, *pair_normed), (*own_cot, *pair_cot), (grad, pair_grad), (act, pair_act))
    (feed_w_parts,) = beside(pair_sum, kernels=[(feed_weights, weight_args)])
    feed_w_sums = [
        lax.psum_scatter(part, "fsdp", scatter_dimension=0, tiled=True, axis_index_groups=alike()).reshape(2, shard, -1)
        for part in feed_w_parts
    ]
    pair_held = pair_sum.keep

    def back(hidden_share, scale_share, cotangent):
        pair_sum = Job(line_scatter(*pair_held, True))
        own_sum = Job(plane_scatter(*own_parts[:2]))
        out_sum = Job(plane_scatter(*own_parts[2:]))
        pair_out_sum = Job(plane_scatter(*pair_parts[2:], True))
        beside(pair_sum, own_sum, pair_out_sum, out_sum)
        cut = share_rows // 2
        upper, lower = (Job(pair_swap(pair_sum.value[k : k + cut])) for k in (0, cut))
        cot_share = share_of(cotangent)
        beside(upper, own_sum, ready=[pair_out_sum])
        beside(lower, own_sum, pair_out_sum, ready=[out_sum])
        _, keep_first, _, keep_second = own_sum.held
        got_first, got_second = own_sum.arrived
        hidden_grad_share, low_share, ffn_gain_part = share_back(
            keep_first, got_first, keep_second, got_second, upper.value, lower.value, hidden_share, cot_share,
            wide(gain_ffn)[None],
        )
        gather = Job(plane_gather(low_share[None]))
        beside(gather, ready=[pair_out_sum])
        beside(gather)
        return hidden_grad_share, ffn_gain_part, *gather.held, *gather.arrived, *pair_out_sum.keep, *out_sum.keep

    hidden_grad_share, ffn_gain_part, *held = apart(back, hidden_share, scale_share, cotangent)
    wide_give, held = lax.optimization_barrier((pick(feed_w_sums[0], 1 - side, 0), held))
    wide_got = swap(wide_give, "fsdp", 1)

    def attention(held, *kept):
        gather = Job(core_gather(*held[:4]))
        pair_out_sum = Job(line_scatter(*held[4:8], True))
        out_sum = Job(chip_scatter(*held[8:]))
        beside(gather, pair_out_sum)
        grad_mine, grad_other = (array[0] for array in gather.value)
        pair_out = Job(pair_swap(pair_out_sum.value))

        def attended(*kept):
            low_grad, mixed_split, head_gain_part = attend_back(group, grad_mine, grad_other, *kept)
            return *attend_weights(low_grad, mixed_split, scale_one, grad_mine, grad_other, proj, tokens, normed), head_gain_part

        (results,) = beside(pair_out, out_sum, kernels=[(attended, kept)])
        return *results, pair_out.value, *out_sum.held, *out_sum.arrived

    attn_w_part, keep, give, attn_gain_part, head_gain_part, pair_out, *held = apart(
        attention, held, proj, cosine, sine, query_gain_wide, key_gain_wide, seg_rows, segment_row,
        raw, query_rot, key_rot, values, mixed_low,
    )
    attn_w_part, give, wide_got, feed_w_sums[1] = lax.optimization_barrier(
        (attn_w_part, give, wide_got, feed_w_sums[1])
    )
    down_got = swap(pick(feed_w_sums[1], 1 - side, 0), "fsdp", 1)
    attn_w_sum = lax.psum_scatter(attn_w_part, "fsdp", scatter_dimension=0, tiled=True)

    def last(keep, give, hidden_share, pair_out, hidden_grad_share, tokens, scale_one, *rest):
        gain_parts, (_, keep_first, _, keep_second, got_first, got_second) = rest[:4], rest[4:]
        out_sum = Job(line_scatter(*fold_line(keep_first, got_first, keep_second, got_second)))
        normed_sum = Job(plane_scatter(keep, give))
        gains = Job(sum_all(jnp.concatenate(gain_parts, axis=1)))
        beside(normed_sum, out_sum, gains)
        beside(normed_sum, gains)
        beside(normed_sum, gains)
        finish(gains)
        block_out = low(hidden_share + wide(pair_out) + out_sum.value)
        token_share = wide(share_of(tokens))
        scale_one_share = share_of(scale_one)
        tokens_grad = low(
            hidden_grad_share + norm_back(token_share, scale_one_share, normed_sum.value * wide(gain_attn))
        )
        return block_out, tokens_grad, gains.value

    block_out, tokens_grad, gain_sums = apart(
        last, keep, give, hidden_share, pair_out, hidden_grad_share, tokens, scale_one,
        attn_gain_part, ffn_gain_part, head_gain_part[:1], head_gain_part[1:], *held,
    )
    gain_sums, down_got = lax.optimization_barrier((gain_sums, down_got))
    feed_w_grads = feed_sums(side[None], feed_w_sums, (wide_got, down_got))
    attn_w_grad, (gate_w_grad, up_w_grad, down_w_grad) = lax.optimization_barrier((attn_w_sum, feed_w_grads))
    query_w_grad, key_w_grad, value_w_grad, out_w_grad = widened(
        attn_w_grad, (query_cols, key_cols, key_cols, query_cols)
    )
    ends = [0, model, 2 * model, 2 * model + HD, 2 * model + 2 * HD]
    ln1_grad, ln2_grad, query_gain_grad, key_gain_grad = (
        lax.dynamic_slice_in_dim(gain_sums[0, start:end], lax.axis_index("fsdp") * ((end - start) // size), (end - start) // size, 0)
        for start, end in zip(ends, ends[1:])
    )
    return (
        block_out,
        tokens_grad,
        ln1_grad,
        query_w_grad,
        key_w_grad,
        value_w_grad,
        query_gain_grad,
        key_gain_grad,
        out_w_grad,
        ln2_grad,
        gate_w_grad,
        up_w_grad,
        down_w_grad,
    )


def solution(mesh):
    in_specs = (
        P("fsdp", None),
        P("fsdp", None),
        P("fsdp"),
        P("fsdp", ("heads", "tensor")),
        P("fsdp", ("heads", "tensor")),
        P("fsdp", ("heads", "tensor")),
        P("fsdp"),
        P("fsdp"),
        P("fsdp", ("heads", "tensor")),
        P("fsdp"),
        P("fsdp", ("heads", "tensor")),
        P("fsdp", ("heads", "tensor")),
        P("fsdp", ("heads", "tensor")),
        P("fsdp", None),
    )
    out_specs = (
        P(("fsdp", "heads", "tensor"), None),
        P(("fsdp", "heads", "tensor"), None),
        P("fsdp"),
        P("fsdp", ("heads", "tensor")),
        P("fsdp", ("heads", "tensor")),
        P("fsdp", ("heads", "tensor")),
        P("fsdp"),
        P("fsdp"),
        P("fsdp", ("heads", "tensor")),
        P("fsdp"),
        P("fsdp", ("heads", "tensor")),
        P("fsdp", ("heads", "tensor")),
        P("fsdp", ("heads", "tensor")),
    )
    return jax.shard_map(
        per_device, mesh=mesh, in_specs=in_specs, out_specs=out_specs, check_vma=False
    )
```

```python
import functools

import jax
import jax.numpy as jnp
from jax import lax
from jax.experimental import pallas as pl
from jax.experimental.pallas import tpu as pltpu
from jax.sharding import PartitionSpec as P

HD = 128


EPSILON = 1e-06
THETA = 1000000.0
ROWS = 256
BAND = 512
PLANE = ("heads", "tensor")
SWAP = ((0, 1), (1, 0))
NEAR = ((0, 1), (1, 0), (2, 3), (3, 2))
FAR = ((0, 2), (2, 0), (1, 3), (3, 1))


def rms_parts(values):
    return lax.rsqrt(jnp.mean(values * values, axis=-1, keepdims=True) + EPSILON)


def norm_back(values, scale, upstream):
    return scale * upstream - values * scale**3 * jnp.mean(
        values * upstream, axis=-1, keepdims=True
    )


def contract(left, right, left_dim, right_dim):
    return lax.dot_general(
        left, right, (((left_dim,), (right_dim,)), ((), ())), preferred_element_type=jnp.float32
    )


def doc_positions(segment_row):
    places = jnp.arange(segment_row.shape[0], dtype=jnp.int32)
    previous = jnp.concatenate([segment_row[:1], segment_row[:-1]])
    starts = lax.cummax(jnp.where(segment_row != previous, places, 0), axis=0)
    return places - starts


def rope_tables(positions):
    frequency = THETA ** (-(jnp.arange(HD // 2, dtype=jnp.float32) * 2.0 / HD))
    angles = positions.astype(jnp.float32)[:, None] * frequency[None, :]
    cosine, sine = jnp.cos(angles), jnp.sin(angles)
    return (
        jnp.concatenate([cosine, cosine], axis=1),
        jnp.concatenate([-sine, sine], axis=1),
    )


def low(values):
    return values.astype(jnp.bfloat16)


def wide(values):
    return values.astype(jnp.float32)


def flip(axis, stride):
    return [(k, k ^ stride) for k in range(lax.axis_size(axis))]


def after(value, *others):
    return lax.optimization_barrier((value, *others))[0]


def apart(work, *args):
    zeros = [jnp.zeros(out.shape, out.dtype) for out in jax.eval_shape(work, *args)]
    return lax.cond(
        lax.axis_index("fsdp") < lax.axis_size("fsdp"), work, lambda *_: tuple(zeros), *args
    )


class Job:
    def __init__(self, steps):
        self.steps, self.moves, self.keep, self.held, self.value = steps, (), (), (), None
        self.resume(None)

    def resume(self, got):
        self.held, self.arrived = self.keep, got
        try:
            given = self.steps.send(got)
            self.moves, self.keep = given if isinstance(given, tuple) else (given, ())
        except StopIteration as end:
            self.moves, self.keep, self.value = (), (), end.value


def beside(*jobs, kernels=(), ready=()):
    jobs = [job for job in jobs if job.moves]
    ready = [job for job in ready if job.moves]
    given = [[move[0] for move in job.moves] for job in jobs], [args for _, args in kernels]
    arrays, args = lax.optimization_barrier(given)
    got = [
        [lax.ppermute(array, *move[1:]) for array, move in zip(held, job.moves)]
        for held, job in zip(arrays, jobs)
    ]
    results = [kernel[0](*own) for own, kernel in zip(args, kernels)]
    later = [[move[0] for move in job.moves] for job in ready]
    got, results, later = lax.optimization_barrier((got, results, later))
    for job, arrays in zip(ready, later):
        job.moves = [(array, *move[1:]) for array, move in zip(arrays, job.moves)]
    for job, arrived in zip(jobs, got):
        job.resume(arrived)
    return results


def finish(*jobs):
    while any(job.moves for job in jobs):
        beside(*jobs)


def bits(axis):
    size = lax.axis_size(axis)
    return [1 << k for k in range(size.bit_length() - 1)]


def swap(array, axis, stride):
    return lax.ppermute(array, axis, flip(axis, stride))


def bit(axis, stride):
    return (lax.axis_index(axis) // stride) % 2


def line_gather(block, strides):
    block = block[None]
    for stride in strides:
        block = both(block, swap(block, "fsdp", stride), bit("fsdp", stride), 0)
        block = block.reshape(-1, *block.shape[2:])
    return block


def pick(array, index, axis):
    return lax.dynamic_index_in_dim(array, index, axis, keepdims=False)


def both(mine, got, index, axis):
    lower = jnp.where(index == 0, mine, got)
    upper = jnp.where(index == 0, got, mine)
    return jnp.stack([lower, upper], axis=axis)


def join_kernel(*refs):
    first = 0
    for part in refs[:-1]:
        refs[-1][:, first : first + part.shape[1]] = part[...]
        first += part.shape[1]


def joined_columns(*parts):
    shape = (parts[0].shape[0], sum(part.shape[1] for part in parts))
    return pl.pallas_call(
        join_kernel,
        in_specs=[pl.BlockSpec(memory_space=pltpu.VMEM)] * len(parts),
        out_specs=pl.BlockSpec(memory_space=pltpu.VMEM),
        out_shape=jax.ShapeDtypeStruct(shape, parts[0].dtype),
        compiler_params=call_params(60),
        cost_estimate=cheap(),
        name="join",
    )(*parts)


def widen_kernel(source_ref, *outs):
    first = 0
    for out in outs:
        out[...] = wide(source_ref[:, first : first + out.shape[1]])
        first += out.shape[1]


def widened(source, widths):
    rows = source.shape[0]
    return pl.pallas_call(
        widen_kernel,
        in_specs=[pl.BlockSpec(memory_space=pltpu.VMEM)],
        out_specs=[pl.BlockSpec(memory_space=pltpu.VMEM)] * len(widths),
        out_shape=[jax.ShapeDtypeStruct((rows, width), jnp.float32) for width in widths],
        compiler_params=call_params(16),
        cost_estimate=cheap(),
        name="widen",
    )(source)


def position():
    heads = lax.axis_index("heads")
    return jnp.stack([lax.axis_index("tensor"), heads % 2, heads // 2]).astype(jnp.int32)


def vmem_call(kernel, name, megabytes, out_shape, *args):
    return pl.pallas_call(
        kernel,
        in_specs=[pl.BlockSpec(memory_space=pltpu.SMEM)]
        + [pl.BlockSpec(memory_space=pltpu.VMEM)] * len(args),
        out_specs=[pl.BlockSpec(memory_space=pltpu.VMEM)] * len(out_shape),
        out_shape=[jax.ShapeDtypeStruct(shape, jnp.bfloat16) for shape in out_shape],
        compiler_params=call_params(megabytes),
        cost_estimate=cheap(),
        name=name,
    )(position(), *args)


def fold_chip_kernel(position_ref, keep_ref, got_ref, give_first, keep_first, give_second, keep_second):
    x, y = position_ref[1], position_ref[2]
    middle = keep_ref.shape[-1] // 2
    first, second = slice(0, middle), slice(middle, 2 * middle)

    def summed(row, column, cols):
        return low(wide(keep_ref[row, column, :, cols]) + wide(got_ref[row, column, :, cols]))

    for k in range(2):
        give_first[k] = summed(k, 1 - x, first)
        keep_first[k] = summed(k, x, first)
        give_second[k] = summed(1 - y, k, second)
        keep_second[k] = summed(y, k, second)


def fold_chip(keep, got):
    rows, width = keep.shape
    shape = (2, 2, rows // 4, width)
    return vmem_call(
        fold_chip_kernel, "fold_chip", 24, [(2, rows // 4, width // 2)] * 4, keep.reshape(shape), got.reshape(shape)
    )


def fold_line_kernel(
    position_ref, keep_first_ref, got_first_ref, keep_second_ref, got_second_ref, give_first, keep_first, give_second, keep_second
):
    x, y = position_ref[1], position_ref[2]
    for at, keep_ref, got_ref, give, keep in (
        (y, keep_first_ref, got_first_ref, give_first, keep_first),
        (x, keep_second_ref, got_second_ref, give_second, keep_second),
    ):
        give[...] = low(wide(keep_ref[1 - at]) + wide(got_ref[1 - at]))
        keep[...] = low(wide(keep_ref[at]) + wide(got_ref[at]))


def fold_line(keep_first, got_first, keep_second, got_second):
    shape = keep_first.shape[1:]
    return vmem_call(
        fold_line_kernel, "fold_line", 16, [shape] * 4, keep_first, got_first, keep_second, got_second
    )


def fold_end_kernel(position_ref, keep_first_ref, got_first_ref, keep_second_ref, got_second_ref, out_ref):
    middle = keep_first_ref.shape[-1]
    out_ref[:, :middle] = low(wide(keep_first_ref[...]) + wide(got_first_ref[...]))
    out_ref[:, middle:] = low(wide(keep_second_ref[...]) + wide(got_second_ref[...]))


def fold_end(keep_first, got_first, keep_second, got_second):
    rows, width = keep_first.shape
    (out,) = vmem_call(
        fold_end_kernel, "fold_end", 16, [(rows, 2 * width)], keep_first, got_first, keep_second, got_second
    )
    return out


def share_back_kernel(
    eps, first_ref, got_first_ref, second_ref, got_second_ref, pair_upper_ref, pair_lower_ref, hidden_ref, cotangent_ref, gain_ref, out_ref, low_ref, part_ref
):
    middle = first_ref.shape[-1]
    hidden = hidden_ref[...]
    scale = lax.rsqrt(jnp.mean(hidden * hidden, axis=-1, keepdims=True) + eps)
    grads = []
    for k, (mine, got) in enumerate(((first_ref, got_first_ref), (second_ref, got_second_ref))):
        cols = slice(k * middle, (k + 1) * middle)
        pair = jnp.concatenate([pair_upper_ref[:, cols], pair_lower_ref[:, cols]], axis=0)
        grads.append(wide(mine[...]) + wide(got[...]) + wide(pair))
    grad = jnp.concatenate(grads, axis=1)
    part_ref[...] = jnp.sum(grad * hidden * scale, axis=0, keepdims=True)
    out = wide(cotangent_ref[...]) + norm_back(hidden, scale, grad * gain_ref[...])
    out_ref[...] = out
    low_ref[...] = low(out)


def share_back(first, got_first, second, got_second, pair_upper, pair_lower, hidden, cotangent, gain):
    rows, model = hidden.shape
    args = (first, got_first, second, got_second, pair_upper, pair_lower, hidden, cotangent, gain)
    return pl.pallas_call(
        functools.partial(share_back_kernel, EPSILON),
        in_specs=[pl.BlockSpec(memory_space=pltpu.VMEM)] * len(args),
        out_specs=[pl.BlockSpec(memory_space=pltpu.VMEM)] * 3,
        out_shape=[
            jax.ShapeDtypeStruct((rows, model), jnp.float32),
            jax.ShapeDtypeStruct((rows, model), jnp.bfloat16),
            jax.ShapeDtypeStruct((1, model), jnp.float32),
        ],
        compiler_params=call_params(24),
        cost_estimate=cheap(),
        name="share_back",
    )(*args)


def plane_scatter(keep, give, rounded=False):
    (got,) = yield [(give, "tensor", SWAP)]
    folded = fold_chip(keep, got)
    return (yield from chip_scatter(*folded, rounded))


def chip_scatter(give_first, keep_first, give_second, keep_second, rounded=False):
    held = (give_first, keep_first, give_second, keep_second)
    got = yield [(give_first, "heads", NEAR), (give_second, "heads", FAR)], held
    return (yield from line_scatter(*fold_line(keep_first, got[0], keep_second, got[1]), rounded))


def line_scatter(give_first, keep_first, give_second, keep_second, rounded=False):
    held = (give_first, keep_first, give_second, keep_second)
    got = yield [(give_first, "heads", FAR), (give_second, "heads", NEAR)], held
    if rounded:
        return fold_end(keep_first, got[0], keep_second, got[1])
    first = wide(keep_first) + wide(got[0])
    second = wide(keep_second) + wide(got[1])
    return jnp.concatenate([first, second], axis=-1)


def open_line_kernel(position_ref, first_ref, got_first_ref, second_ref, got_second_ref, first, second):
    x, y = position_ref[1], position_ref[2]
    first[y] = first_ref[...]
    first[1 - y] = got_first_ref[...]
    second[x] = second_ref[...]
    second[1 - x] = got_second_ref[...]


def open_chip_kernel(position_ref, first_ref, got_first_ref, second_ref, got_second_ref, out_ref):
    x, y = position_ref[1], position_ref[2]
    lead, middle = first_ref.shape[1], first_ref.shape[-1]
    for k in range(lead):
        for j in range(2):
            out_ref[k, j, x, :, :middle] = first_ref[j, k]
            out_ref[k, j, 1 - x, :, :middle] = got_first_ref[j, k]
            out_ref[k, y, j, :, middle:] = second_ref[j, k]
            out_ref[k, 1 - y, j, :, middle:] = got_second_ref[j, k]


def plane_gather(share):
    lead, rows, width = share.shape
    first, second = share[..., : width // 2], share[..., width // 2 :]
    got = yield [(first, "heads", FAR), (second, "heads", NEAR)], (first, second)
    first, second = vmem_call(
        open_line_kernel, "open_line", 16, [(2, lead, rows, width // 2)] * 2, first, got[0], second, got[1]
    )
    got = yield [(first, "heads", NEAR), (second, "heads", FAR)], (first, second)
    return (yield from core_gather(first, second, *got))


def core_gather(first, second, got_first, got_second):
    _, lead, rows, middle = first.shape
    (mine,) = vmem_call(
        open_chip_kernel, "open_chip", 24, [(lead, 2, 2, rows, 2 * middle)], first, got_first, second, got_second
    )
    mine = mine.reshape(lead, 4 * rows, 2 * middle)
    (other,) = yield [(mine, "tensor", SWAP)]
    return mine, other


def pair_swap(array, pieces=1):
    rows = array.shape[0] // pieces
    got = []
    for k in range(pieces):
        got += yield [(array[k * rows : (k + 1) * rows], "fsdp", flip("fsdp", 1))]
    return jnp.concatenate(got, axis=0) if pieces > 1 else got[0]


def pair_gather(share, pieces):
    got = yield from pair_swap(share, pieces)
    return (yield from plane_gather(got[None]))


def sum_all(values):
    for axis in ("tensor", "heads", "fsdp"):
        strides = bits(axis)
        if axis == "fsdp" and len(strides) > 1:
            strides = [strides[0] + strides[1]] + strides[1:]
        for stride in strides:
            (got,) = yield [(values, axis, flip(axis, stride))]
            values = values + got
    return values


def alike():
    return [list(range(k, lax.axis_size("fsdp"), 2)) for k in range(2)]


def rotate(values, cosine, sine):
    return values * cosine + pltpu.roll(values, HD // 2, 1) * sine


def call_params(megabytes):
    return pltpu.CompilerParams(vmem_limit_bytes=megabytes << 20)


def cheap():
    return pl.CostEstimate(flops=1000, bytes_accessed=1000, transcendentals=0)


def key_blocks(at, count):
    return max(0, at - BAND // ROWS), at + 1


def masked_probs(query, keys, seg_rows, seg_keys, first_row, first_key):
    scores = contract(query, keys, 1, 1) * HD**-0.5
    rows = first_row + lax.broadcasted_iota(jnp.int32, scores.shape, 0)
    cols = first_key + lax.broadcasted_iota(jnp.int32, scores.shape, 1)
    scores = jnp.where((rows >= cols) & (seg_rows == seg_keys), scores, -1e30)
    expo = jnp.exp(scores - jnp.max(scores, axis=-1, keepdims=True))
    return expo / jnp.sum(expo, axis=-1, keepdims=True)


def by_core(core, block):
    middle = block.shape[0] // 2
    lower, upper = block[:middle], block[middle:]
    first = core == 0
    return jnp.where(first, lower, upper), jnp.where(first, upper, lower)


def joined(core, mine, other):
    first = core == 0
    return jnp.concatenate([jnp.where(first, mine, other), jnp.where(first, other, mine)], axis=0)


def attend_kernel(
    group,
    normed_ref,
    proj_ref,
    cosine_ref,
    sine_ref,
    query_gain_ref,
    key_gain_ref,
    seg_rows_ref,
    seg_keys_ref,
    raw_ref,
    query_ref,
    key_ref,
    value_ref,
    mixed_ref,
    keys,
    values,
):
    length, kv_cols = keys.shape
    kv_local = kv_cols // HD
    query_cols = kv_cols * group
    count = length // ROWS
    step = pl.program_id(0)
    raw = jnp.dot(normed_ref[...], proj_ref[...], preferred_element_type=jnp.float32)
    raw_ref[...] = raw[:, : query_cols + kv_cols]
    cosine, sine = cosine_ref[...], sine_ref[...]
    here = pl.ds(pl.multiple_of(step * ROWS, ROWS), ROWS)

    def turned(head, gain_ref):
        one = raw[:, head * HD : (head + 1) * HD]
        return low(rotate(one * rms_parts(one) * gain_ref[...], cosine, sine))

    for kv in range(kv_local):
        at = slice(kv * HD, (kv + 1) * HD)
        new_keys = turned(query_cols // HD + kv, key_gain_ref)
        new_values = low(raw[:, query_cols + kv_cols + kv * HD : query_cols + kv_cols + (kv + 1) * HD])
        key_ref[:, at] = new_keys
        value_ref[:, at] = new_values
        keys[here, at] = new_keys
        values[here, at] = new_values
    for head in range(query_cols // HD):
        query_ref[:, head * HD : (head + 1) * HD] = turned(head, query_gain_ref)

    for at in range(count):

        @pl.when(step == at)
        def _():
            lower, upper = key_blocks(at, count)
            span = slice(lower * ROWS, upper * ROWS)
            for head in range(query_cols // HD):
                cols = slice(head * HD, (head + 1) * HD)
                kv = slice((head // group) * HD, (head // group + 1) * HD)
                probs = masked_probs(
                    query_ref[:, cols],
                    keys[span, kv],
                    seg_rows_ref[...],
                    seg_keys_ref[:, span],
                    at * ROWS,
                    lower * ROWS,
                )
                mixed_ref[:, cols] = low(
                    jnp.dot(low(probs), values[span, kv], preferred_element_type=jnp.float32)
                )


def attend(group, normed, proj, cosine, sine, query_gain, key_gain, seg_rows, segment_row):
    length, model = normed.shape
    kv_cols = proj.shape[1] // (2 * group + 2)
    query_cols = kv_cols * group

    def rows(width):
        return pl.BlockSpec((ROWS, width), lambda i: (i, 0))

    def whole(array):
        return pl.BlockSpec(array.shape, lambda i: (0, 0))

    seg_keys = segment_row[None, :]
    args = (normed, proj, cosine, sine, query_gain[None], key_gain[None], seg_rows, seg_keys)
    outs = [
        (query_cols + kv_cols, jnp.float32),
        (query_cols, jnp.bfloat16),
        (kv_cols, jnp.bfloat16),
        (kv_cols, jnp.bfloat16),
        (query_cols, jnp.bfloat16),
    ]
    return pl.pallas_call(
        functools.partial(attend_kernel, group),
        grid=(length // ROWS,),
        in_specs=[
            rows(model),
            pl.BlockSpec((model, query_cols + 2 * kv_cols), lambda i: (0, 0)),
            rows(HD),
            rows(HD),
            whole(args[4]),
            whole(args[5]),
            rows(1),
            whole(seg_keys),
        ],
        out_specs=[rows(width) for width, _ in outs],
        out_shape=[jax.ShapeDtypeStruct((length, width), kind) for width, kind in outs],
        scratch_shapes=[
            pltpu.VMEM((length, kv_cols), jnp.bfloat16),
            pltpu.VMEM((length, kv_cols), jnp.bfloat16),
        ],
        compiler_params=call_params(40),
        cost_estimate=cheap(),
        name="attend",
    )(*args)


def attend_out_kernel(position_ref, mixed_ref, proj_ref, keep_ref, give_ref):
    keep_ref[...], give_ref[...] = by_core(
        position_ref[0], low(contract(mixed_ref[...], proj_ref[...], 1, 1))
    )


def attend_out(mixed, proj):
    length, cols = mixed.shape
    model = proj.shape[0]
    return pl.pallas_call(
        attend_out_kernel,
        grid=(length // ROWS,),
        in_specs=[
            pl.BlockSpec(memory_space=pltpu.SMEM),
            pl.BlockSpec((ROWS, cols), lambda i: (i, 0)),
            pl.BlockSpec((model, cols), lambda i: (0, proj.shape[1] // cols - 1)),
        ],
        out_specs=[pl.BlockSpec((ROWS // 2, model), lambda i: (i, 0))] * 2,
        out_shape=[jax.ShapeDtypeStruct((length // 2, model), jnp.bfloat16)] * 2,
        compiler_params=call_params(24),
        cost_estimate=cheap(),
        name="attend_out",
    )(position(), mixed, proj)


def attend_back_kernel(
    group,
    grad_mine_ref,
    grad_other_ref,
    out_proj_ref,
    cosine_ref,
    sine_ref,
    query_gain_ref,
    key_gain_ref,
    seg_rows_ref,
    seg_keys_ref,
    raw_ref,
    query_ref,
    key_ref,
    value_ref,
    mixed_ref,
    position_ref,
    low_ref,
    mixed_split_ref,
    head_gain_ref,
    mixed_grad,
    query_sum,
    key_sum,
    value_sum,
):
    length, kv_cols = key_sum.shape
    query_cols = kv_cols * group
    count = length // ROWS
    share = ROWS // 2
    core = position_ref[0]
    for k, ref in enumerate((grad_mine_ref, grad_other_ref)):
        part = low(jnp.dot(ref[...], out_proj_ref[...], preferred_element_type=jnp.float32))
        for at in range(count):
            start = pl.multiple_of(at * ROWS + (core + k - 2 * k * core) * share, share)
            mixed_grad[pl.ds(start, share), :] = part[at * share : (at + 1) * share]
            mixed_split_ref[k, at * share : (at + 1) * share, :] = mixed_ref[pl.ds(start, share), :]
    key_sum[...] = jnp.zeros_like(key_sum)
    value_sum[...] = jnp.zeros_like(value_sum)
    for at in range(count):
        here = slice(at * ROWS, (at + 1) * ROWS)
        lower, upper = key_blocks(at, count)
        span = slice(lower * ROWS, upper * ROWS)
        for head in range(query_cols // HD):
            cols = slice(head * HD, (head + 1) * HD)
            kv = slice((head // group) * HD, (head // group + 1) * HD)
            query = query_ref[here, cols]
            grad = mixed_grad[here, cols]
            probs = masked_probs(
                query,
                key_ref[span, kv],
                seg_rows_ref[here, :],
                seg_keys_ref[:, span],
                at * ROWS,
                lower * ROWS,
            )
            prob_grad = contract(grad, value_ref[span, kv], 1, 1)
            row_inner = jnp.sum(probs * prob_grad, axis=-1, keepdims=True)
            score_grad = low(HD**-0.5 * probs * (prob_grad - row_inner))
            query_sum[here, cols] = jnp.dot(
                score_grad, key_ref[span, kv], preferred_element_type=jnp.float32
            )
            key_sum[span, kv] += contract(score_grad, query, 0, 0)
            value_sum[span, kv] += contract(low(probs), grad, 0, 0)

    head_gain_ref[...] = jnp.zeros_like(head_gain_ref)
    for at in range(count):
        here = slice(at * ROWS, (at + 1) * ROWS)
        cosine, sine = cosine_ref[here, :], -sine_ref[here, :]
        for head in range((query_cols + kv_cols) // HD):
            cols = slice(head * HD, (head + 1) * HD)
            own = slice(head * HD - query_cols, (head + 1) * HD - query_cols)
            is_query = head * HD < query_cols
            turned = rotate(query_sum[here, cols] if is_query else key_sum[here, own], cosine, sine)
            raw = raw_ref[here, cols]
            scale = rms_parts(raw)
            row = 0 if is_query else 1
            head_gain_ref[row : row + 1, :] += jnp.sum(turned * raw * scale, axis=0, keepdims=True)
            gain = query_gain_ref[...] if is_query else key_gain_ref[...]
            low_ref[here, cols] = low(norm_back(raw, scale, turned * gain))
        low_ref[here, query_cols + kv_cols :] = low(value_sum[here, :])


def attend_back(
    group, grad_mine, grad_other, proj, cosine, sine, query_gain, key_gain, seg_rows, segment_row, raw, query, key, value, mixed
):
    length, query_cols, kv_cols = query.shape[0], query.shape[1], key.shape[1]
    args = (
        grad_mine, grad_other, proj, cosine, sine, query_gain[None], key_gain[None],
        seg_rows, segment_row[None, :], raw, query, key, value, mixed, position(),
    )
    out_shape = [
        jax.ShapeDtypeStruct((length, query_cols + 2 * kv_cols), jnp.bfloat16),
        jax.ShapeDtypeStruct((2, length // 2, query_cols), jnp.bfloat16),
        jax.ShapeDtypeStruct((2, HD), jnp.float32),
    ]

    def whole(array):
        return pl.BlockSpec(array.shape, lambda i: (0,) * len(array.shape), pipeline_mode=pl.Buffered(1))

    return pl.pallas_call(
        functools.partial(attend_back_kernel, group),
        grid=(1,),
        in_specs=[whole(grad_mine), whole(grad_other)]
        + [pl.BlockSpec((proj.shape[0], query_cols), lambda i: (0, proj.shape[1] // query_cols - 1))]
        + [whole(array) for array in args[3:-1]]
        + [pl.BlockSpec(memory_space=pltpu.SMEM)],
        out_specs=[whole(out) for out in out_shape],
        out_shape=out_shape,
        scratch_shapes=[
            pltpu.VMEM((length, query_cols), jnp.bfloat16),
            pltpu.VMEM((length, query_cols), jnp.float32),
            pltpu.VMEM((length, kv_cols), jnp.float32),
            pltpu.VMEM((length, kv_cols), jnp.float32),
        ],
        compiler_params=call_params(40),
        cost_estimate=cheap(),
        name="attend_back",
    )(*args)


def attend_weights_kernel(
    position_ref, low_ref, mixed_ref, scale_ref, grad_mine_ref, grad_other_ref, proj_ref, tokens_ref, normed_ref,
    weight_ref, keep_ref, give_ref, gain_ref,
):
    split = low_ref.shape[1]
    share = ROWS // 2
    gain = jnp.zeros_like(gain_ref)
    for at in range(low_ref.shape[0] // ROWS):
        here = slice(at * ROWS, (at + 1) * ROWS)
        rows = slice(at * share, (at + 1) * share)
        part = contract(low_ref[here, :], proj_ref[...], 1, 1)
        keep_ref[rows, :], give_ref[rows, :] = by_core(position_ref[0], low(part))
        gain += jnp.sum(part * wide(tokens_ref[here, :]) * scale_ref[here, :], axis=0, keepdims=True)
    gain_ref[...] = gain
    weight_ref[:, :split] = low(contract(normed_ref[...], low_ref[...], 0, 0))
    weight_ref[:, split:] = low(
        contract(grad_mine_ref[...], mixed_ref[0], 0, 0) + contract(grad_other_ref[...], mixed_ref[1], 0, 0)
    )


def attend_weights(low_grad, mixed, scale, grad_mine, grad_other, proj, tokens, normed):
    length, model = tokens.shape
    split = low_grad.shape[1]
    width = split + mixed.shape[-1]
    cols = min(512, model)

    def whole(array):
        return pl.BlockSpec(array.shape, lambda i: (0,) * array.ndim, pipeline_mode=pl.Buffered(1))

    def columns(rows):
        return pl.BlockSpec((rows, cols), lambda i: (0, i))

    return pl.pallas_call(
        attend_weights_kernel,
        grid=(model // cols,),
        in_specs=[
            pl.BlockSpec(memory_space=pltpu.SMEM),
            whole(low_grad),
            whole(mixed),
            whole(scale),
            columns(length // 2),
            columns(length // 2),
            pl.BlockSpec((cols, split), lambda i: (i, 0)),
            columns(length),
            columns(length),
        ],
        out_specs=[
            pl.BlockSpec((cols, width), lambda i: (i, 0)),
            columns(length // 2),
            columns(length // 2),
            columns(1),
        ],
        out_shape=[
            jax.ShapeDtypeStruct((model, width), jnp.bfloat16),
            jax.ShapeDtypeStruct((length // 2, model), jnp.bfloat16),
            jax.ShapeDtypeStruct((length // 2, model), jnp.bfloat16),
            jax.ShapeDtypeStruct((1, model), jnp.float32),
        ],
        compiler_params=call_params(40),
        cost_estimate=cheap(),
        name="attend_weights",
    )(position(), low_grad, mixed, scale, grad_mine, grad_other, proj, tokens, normed)


def prepare_kernel(tokens_ref, gain_ref, seg_ref, normed_ref, scale_ref, seg_rows_ref):
    block_in = wide(tokens_ref[...])
    scale = rms_parts(block_in)
    scale_ref[...] = scale
    normed_ref[...] = low(block_in * scale * gain_ref[...])
    seg_rows_ref[...] = seg_ref[...]


def prepare(tokens, gain, seg_rows):
    length, model = tokens.shape

    def rows(width):
        return pl.BlockSpec((ROWS, width), lambda i: (i, 0))

    return pl.pallas_call(
        prepare_kernel,
        grid=(length // ROWS,),
        in_specs=[rows(model), pl.BlockSpec((1, model), lambda i: (0, 0)), rows(1)],
        out_specs=[rows(model), rows(1), rows(1)],
        out_shape=[
            jax.ShapeDtypeStruct((length, model), jnp.bfloat16),
            jax.ShapeDtypeStruct((length, 1), jnp.float32),
            jax.ShapeDtypeStruct((length, 1), jnp.int32),
        ],
        compiler_params=call_params(24),
        cost_estimate=pl.CostEstimate(flops=20_000_000_000, bytes_accessed=20_000_000, transcendentals=0),
        name="prepare",
    )(tokens, gain[None], seg_rows)


def feed_kernel(*refs):
    sources, (proj_hbm, *results, normed, cotangent, proj, arrive) = refs[:8], refs[8:]
    acts, grads = results[:2], results[2:]
    half = acts[0].shape[-1]
    rows = sources[0].shape[0]
    tile = min(256, rows)

    def fetch(source, target, k):
        copy = pltpu.make_async_copy(source, target, arrive.at[k])
        copy.start()
        return copy

    loads = [fetch(proj_hbm, proj, 8)]
    for k in range(4):
        loads.append(fetch(sources[k], normed.at[k], 2 * k))
        loads.append(fetch(sources[4 + k], cotangent.at[k], 2 * k + 1))
    loads[0].wait()
    for k in range(4):
        loads[2 * k + 1].wait()
        loads[2 * k + 2].wait()
        act_ref, grad_ref = acts[k // 2], grads[k // 2]

        @pl.loop(0, rows // tile)
        def _(step):
            here = pl.ds(pl.multiple_of(step * tile, tile), tile)
            gate_up = jnp.dot(normed[k, here, :], proj[:, : 2 * half], preferred_element_type=jnp.float32)
            gate, up = gate_up[:, :half], gate_up[:, half:]
            act_grad = jnp.dot(cotangent[k, here, :], proj[:, 2 * half :], preferred_element_type=jnp.float32)
            sigmoid = jax.nn.sigmoid(gate)
            silu = gate * sigmoid
            act_ref[k % 2, here, :] = low(silu * up)
            grad_ref[k % 2, here, :half] = low(act_grad * up * sigmoid * (1.0 + gate * (1.0 - sigmoid)))
            grad_ref[k % 2, here, half:] = low(act_grad * silu)


def feed(normed, cotangent, proj):
    rows, model = normed[0].shape
    half = proj.shape[1] // 3
    widths = (half, half, 2 * half, 2 * half)
    return pl.pallas_call(
        feed_kernel,
        in_specs=[pl.BlockSpec(memory_space=pl.ANY)] * 9,
        out_specs=[pl.BlockSpec(memory_space=pltpu.VMEM)] * 4,
        out_shape=[jax.ShapeDtypeStruct((2, rows, w), jnp.bfloat16) for w in widths],
        scratch_shapes=[
            pltpu.VMEM((4, rows, model), jnp.bfloat16),
            pltpu.VMEM((4, rows, model), jnp.bfloat16),
            pltpu.VMEM(proj.shape, jnp.bfloat16),
            pltpu.SemaphoreType.DMA((9,)),
        ],
        compiler_params=call_params(48),
        cost_estimate=cheap(),
        name="feed",
    )(*normed, *cotangent, proj)


def feed_model_kernel(act_ref, grad_ref, proj_ref, keep_ref, give_ref, keep_out_ref, give_out_ref):
    half = act_ref.shape[-1]
    for k, (out_ref, out_out_ref) in enumerate(((keep_ref, keep_out_ref), (give_ref, give_out_ref))):
        out_ref[...] = low(contract(grad_ref[k], proj_ref[:, : 2 * half], 1, 1))
        out_out_ref[...] = low(contract(act_ref[k], proj_ref[:, 2 * half :], 1, 1))


def feed_model(act, grad, proj):
    _, rows, half = act.shape
    model = proj.shape[0]
    tile = min(256, rows)
    return pl.pallas_call(
        feed_model_kernel,
        grid=(rows // tile,),
        in_specs=[
            pl.BlockSpec((2, tile, half), lambda i: (0, i, 0)),
            pl.BlockSpec((2, tile, 2 * half), lambda i: (0, i, 0)),
            pl.BlockSpec(proj.shape, lambda i: (0, 0), pipeline_mode=pl.Buffered(1)),
        ],
        out_specs=[pl.BlockSpec((tile, model), lambda i: (i, 0))] * 4,
        out_shape=[jax.ShapeDtypeStruct((rows, model), jnp.bfloat16)] * 4,
        compiler_params=call_params(40),
        cost_estimate=cheap(),
        name="feed_model",
    )(act, grad, proj)


def feed_weights_kernel(*refs):
    normed, cotangent, grad, act, (wide_ref, out_ref) = refs[:4], refs[4:8], refs[8:10], refs[10:12], refs[12:]
    wide_ref[...] = low(
        sum(contract(normed[k][...], grad[k // 2][k % 2], 0, 0) for k in range(4))
    )
    out_ref[...] = low(
        sum(contract(cotangent[k][...], act[k // 2][k % 2], 0, 0) for k in range(4))
    )


def feed_weights(normed, cotangent, grad, act):
    rows, model = normed[0].shape
    widths = grad[0].shape[-1], act[0].shape[-1]
    cols = min(512, model)

    def whole(array):
        return pl.BlockSpec(array.shape, lambda i: (0, 0, 0), pipeline_mode=pl.Buffered(1))

    return pl.pallas_call(
        feed_weights_kernel,
        grid=(model // cols,),
        in_specs=[pl.BlockSpec((rows, cols), lambda i: (0, i))] * 8 + [whole(a) for a in (*grad, *act)],
        out_specs=[pl.BlockSpec((cols, width), lambda i: (i, 0)) for width in widths],
        out_shape=[jax.ShapeDtypeStruct((model, width), jnp.bfloat16) for width in widths],
        compiler_params=call_params(48),
        cost_estimate=cheap(),
        name="feed_weights",
    )(*normed, *cotangent, *grad, *act)


def feed_sums_kernel(side_ref, *refs):
    sources, outs = refs[:4], refs[4:]
    half = outs[0].shape[1]
    mine = pl.program_id(0) == side_ref[0]
    for (wide_ref, down_ref), keep in ((sources[:2], mine), (sources[2:], jnp.logical_not(mine))):

        @pl.when(keep)
        def _():
            for k in range(2):
                outs[k][...] = wide(wide_ref[:, k * half : (k + 1) * half])
            outs[2][...] = wide(down_ref[...])


def feed_sums(side, own, other):
    rows, half = other[1].shape
    return pl.pallas_call(
        feed_sums_kernel,
        grid_spec=pltpu.PrefetchScalarGridSpec(
            num_scalar_prefetch=1,
            grid=(2,),
            in_specs=[pl.BlockSpec((None, rows, w), lambda i, side: (side[0], 0, 0)) for w in (2 * half, half)]
            + [pl.BlockSpec((rows, w), lambda i, side: (0, 0)) for w in (2 * half, half)],
            out_specs=[pl.BlockSpec((rows, half), lambda i, side: (0, i))] * 3,
        ),
        out_shape=[jax.ShapeDtypeStruct((rows, 2 * half), jnp.float32)] * 3,
        compiler_params=call_params(32),
        cost_estimate=cheap(),
        name="feed_sums",
    )(side, *own, *other)


def per_device(
    tokens,
    segments,
    ln1_gain,
    w_query,
    w_key,
    w_value,
    query_gain,
    key_gain,
    w_out,
    ln2_gain,
    w_gate,
    w_up,
    w_down,
    cotangent,
):
    length, model = tokens.shape
    query_cols, key_cols = w_query.shape[1], w_key.shape[1]
    query_heads = query_cols // HD
    kv_local = key_cols // HD
    group = query_heads // kv_local
    size = lax.axis_size("fsdp")
    shard = model // size
    hidden = w_gate.shape[1]
    half = hidden // 2
    strides = bits("fsdp")
    group_size = lax.axis_size(PLANE)
    share_rows = length // group_size
    share_start = lax.axis_index(PLANE) * share_rows
    segment_row = segments[0]

    def share_of(array):
        return lax.dynamic_slice_in_dim(array, share_start, share_rows, 0)

    block = joined_columns(w_query, w_key, w_value, w_out)
    proj = lax.all_gather(block, "fsdp", axis=0, tiled=True)
    side = bit("fsdp", 1)

    def half_of(which):
        return jnp.concatenate(
            [lax.dynamic_slice_in_dim(w, which * half, half, 1) for w in (w_gate, w_up, w_down)], axis=1
        )

    got = swap(after(half_of(1 - side), proj), "fsdp", 1)
    feed_block = both(half_of(side), got, side, 0)

    gains = line_gather(after(jnp.concatenate([ln1_gain, ln2_gain, query_gain, key_gain]), block), strides)
    gain_attn = gains[:, :shard].reshape(model)
    gain_ffn = gains[:, shard : 2 * shard].reshape(model)
    head_part = HD // size
    query_norm = gains[:, 2 * shard : 2 * shard + head_part].reshape(HD)
    key_norm = gains[:, 2 * shard + head_part :].reshape(HD)

    cosine, sine = rope_tables(doc_positions(segment_row))
    normed, scale_one, seg_rows = prepare(tokens, wide(gain_attn), segment_row[:, None])
    query_gain_wide, key_gain_wide = wide(query_norm), wide(key_norm)
    by_chip = cotangent.reshape(4, 2, share_rows, model)
    core = lax.axis_index("tensor")
    own_cot = [pick(by_chip, k, 1).reshape(length // 2, model) for k in (core, 1 - core)]
    own_cot, normed = lax.optimization_barrier((own_cot, normed))
    raw, query_rot, key_rot, values, mixed_low = attend(
        group, normed, proj, cosine, sine, query_gain_wide, key_gain_wide, seg_rows, segment_row
    )
    out_keep, out_give = attend_out(mixed_low, proj)
    out_got = swap(out_give, "tensor", 1)
    out_got, feed_block = lax.optimization_barrier((out_got, feed_block))
    feed_proj = lax.all_gather(
        feed_block, "fsdp", axis=0, tiled=True, axis_index_groups=alike()
    ).reshape(model, -1)

    def middle(tokens, cotangent, out_keep, out_got):
        cot = Job(pair_gather(share_of(cotangent), 2))
        out_sum = Job(chip_scatter(*fold_chip(out_keep, out_got)))
        beside(out_sum, cot)
        beside(out_sum, cot)
        hidden_share = wide(share_of(tokens)) + out_sum.value
        scale_share = rms_parts(hidden_share)
        normed_share = low(hidden_share * scale_share * wide(gain_ffn))
        gather = Job(plane_gather(normed_share[None]))
        pair_share = Job(pair_swap(normed_share, 2))
        beside(pair_share, gather, cot)
        beside(pair_share, gather)
        pair_gather_x = Job(plane_gather(pair_share.value[None]))
        beside(pair_gather_x, cot, gather)
        beside(pair_gather_x, cot)
        finish(pair_gather_x, cot, gather)
        arrays = (*gather.value, *pair_gather_x.value, *cot.value)
        return hidden_share, scale_share, *(array[0] for array in arrays)

    hidden_share, scale_share, *parts = apart(middle, tokens, cotangent, out_keep, out_got)
    own_normed, pair_normed, pair_cot = parts[:2], parts[2:4], parts[4:]

    act, pair_act, grad, pair_grad = feed((*own_normed, *pair_normed), (*own_cot, *pair_cot), feed_proj)
    pair_parts = feed_model(pair_act, pair_grad, feed_proj)
    pair_sum = Job(plane_scatter(*pair_parts[:2]))
    (own_parts,) = beside(pair_sum, kernels=[(feed_model, (act, grad, feed_proj))])
    weight_args = ((*own_normed, *pair_normed), (*own_cot, *pair_cot), (grad, pair_grad), (act, pair_act))
    (feed_w_parts,) = beside(pair_sum, kernels=[(feed_weights, weight_args)])
    feed_w_sums = [
        lax.psum_scatter(part, "fsdp", scatter_dimension=0, tiled=True, axis_index_groups=alike()).reshape(2, shard, -1)
        for part in feed_w_parts
    ]
    pair_held = pair_sum.keep

    def back(hidden_share, scale_share, cotangent):
        pair_sum = Job(line_scatter(*pair_held, True))
        own_sum = Job(plane_scatter(*own_parts[:2]))
        out_sum = Job(plane_scatter(*own_parts[2:]))
        pair_out_sum = Job(plane_scatter(*pair_parts[2:], True))
        beside(pair_sum, own_sum, pair_out_sum, out_sum)
        cut = share_rows // 2
        upper, lower = (Job(pair_swap(pair_sum.value[k : k + cut])) for k in (0, cut))
        cot_share = share_of(cotangent)
        beside(upper, own_sum, ready=[pair_out_sum])
        beside(lower, own_sum, pair_out_sum, ready=[out_sum])
        _, keep_first, _, keep_second = own_sum.held
        got_first, got_second = own_sum.arrived
        hidden_grad_share, low_share, ffn_gain_part = share_back(
            keep_first, got_first, keep_second, got_second, upper.value, lower.value, hidden_share, cot_share,
            wide(gain_ffn)[None],
        )
        gather = Job(plane_gather(low_share[None]))
        beside(gather, ready=[pair_out_sum])
        beside(gather)
        return hidden_grad_share, ffn_gain_part, *gather.held, *gather.arrived, *pair_out_sum.keep, *out_sum.keep

    hidden_grad_share, ffn_gain_part, *held = apart(back, hidden_share, scale_share, cotangent)
    wide_give, held = lax.optimization_barrier((pick(feed_w_sums[0], 1 - side, 0), held))
    wide_got = swap(wide_give, "fsdp", 1)

    def attention(held, *kept):
        gather = Job(core_gather(*held[:4]))
        pair_out_sum = Job(line_scatter(*held[4:8], True))
        out_sum = Job(chip_scatter(*held[8:]))
        beside(gather, pair_out_sum)
        grad_mine, grad_other = (array[0] for array in gather.value)
        pair_out = Job(pair_swap(pair_out_sum.value))

        def attended(*kept):
            low_grad, mixed_split, head_gain_part = attend_back(group, grad_mine, grad_other, *kept)
            return *attend_weights(low_grad, mixed_split, scale_one, grad_mine, grad_other, proj, tokens, normed), head_gain_part

        (results,) = beside(pair_out, out_sum, kernels=[(attended, kept)])
        return *results, pair_out.value, *out_sum.held, *out_sum.arrived

    attn_w_part, keep, give, attn_gain_part, head_gain_part, pair_out, *held = apart(
        attention, held, proj, cosine, sine, query_gain_wide, key_gain_wide, seg_rows, segment_row,
        raw, query_rot, key_rot, values, mixed_low,
    )
    attn_w_part, give, wide_got, feed_w_sums[1] = lax.optimization_barrier(
        (attn_w_part, give, wide_got, feed_w_sums[1])
    )
    down_got = swap(pick(feed_w_sums[1], 1 - side, 0), "fsdp", 1)
    attn_w_sum = lax.psum_scatter(attn_w_part, "fsdp", scatter_dimension=0, tiled=True)

    def last(keep, give, hidden_share, pair_out, hidden_grad_share, tokens, scale_one, *rest):
        gain_parts, (_, keep_first, _, keep_second, got_first, got_second) = rest[:4], rest[4:]
        out_sum = Job(line_scatter(*fold_line(keep_first, got_first, keep_second, got_second)))
        normed_sum = Job(plane_scatter(keep, give))
        gains = Job(sum_all(jnp.concatenate(gain_parts, axis=1)))
        beside(normed_sum, out_sum, gains)
        beside(normed_sum, gains)
        beside(normed_sum, gains)
        finish(gains)
        block_out = low(hidden_share + wide(pair_out) + out_sum.value)
        token_share = wide(share_of(tokens))
        scale_one_share = share_of(scale_one)
        tokens_grad = low(
            hidden_grad_share + norm_back(token_share, scale_one_share, normed_sum.value * wide(gain_attn))
        )
        return block_out, tokens_grad, gains.value

    block_out, tokens_grad, gain_sums = apart(
        last, keep, give, hidden_share, pair_out, hidden_grad_share, tokens, scale_one,
        attn_gain_part, ffn_gain_part, head_gain_part[:1], head_gain_part[1:], *held,
    )
    gain_sums, down_got = lax.optimization_barrier((gain_sums, down_got))
    feed_w_grads = feed_sums(side[None], feed_w_sums, (wide_got, down_got))
    attn_w_grad, (gate_w_grad, up_w_grad, down_w_grad) = lax.optimization_barrier((attn_w_sum, feed_w_grads))
    query_w_grad, key_w_grad, value_w_grad, out_w_grad = widened(
        attn_w_grad, (query_cols, key_cols, key_cols, query_cols)
    )
    ends = [0, model, 2 * model, 2 * model + HD, 2 * model + 2 * HD]
    ln1_grad, ln2_grad, query_gain_grad, key_gain_grad = (
        lax.dynamic_slice_in_dim(gain_sums[0, start:end], lax.axis_index("fsdp") * ((end - start) // size), (end - start) // size, 0)
        for start, end in zip(ends, ends[1:])
    )
    return (
        block_out,
        tokens_grad,
        ln1_grad,
        query_w_grad,
        key_w_grad,
        value_w_grad,
        query_gain_grad,
        key_gain_grad,
        out_w_grad,
        ln2_grad,
        gate_w_grad,
        up_w_grad,
        down_w_grad,
    )


def solution(mesh):
    in_specs = (
        P("fsdp", None),
        P("fsdp", None),
        P("fsdp"),
        P("fsdp", ("heads", "tensor")),
        P("fsdp", ("heads", "tensor")),
        P("fsdp", ("heads", "tensor")),
        P("fsdp"),
        P("fsdp"),
        P("fsdp", ("heads", "tensor")),
        P("fsdp"),
        P("fsdp", ("heads", "tensor")),
        P("fsdp", ("heads", "tensor")),
        P("fsdp", ("heads", "tensor")),
        P("fsdp", None),
    )
    out_specs = (
        P(("fsdp", "heads", "tensor"), None),
        P(("fsdp", "heads", "tensor"), None),
        P("fsdp"),
        P("fsdp", ("heads", "tensor")),
        P("fsdp", ("heads", "tensor")),
        P("fsdp", ("heads", "tensor")),
        P("fsdp"),
        P("fsdp"),
        P("fsdp", ("heads", "tensor")),
        P("fsdp"),
        P("fsdp", ("heads", "tensor")),
        P("fsdp", ("heads", "tensor")),
        P("fsdp", ("heads", "tensor")),
    )
    return jax.shard_map(
        per_device, mesh=mesh, in_specs=in_specs, out_specs=out_specs, check_vma=False
    )
```
